32 devices in a mesh: dp: 8 (over z, y), seq: 4 (over x, core).
Axes of the slice: x: 2, y: 2, z: 4, core: 2. Of those that a mesh axis runs over, the one named last changes fastest.
Arguments:
- tokens: bfloat16 [8, 2048, 1024], P('dp', 'seq'), may hold values from -6 to 6
- cotangent: bfloat16 [8, 2048, 1024], P('dp', 'seq'), may hold values from -6 to 6
- in_weight: bfloat16 [1024, 4384], P('dp'), may hold values from -0.1875 to 0.1875
- out_weight: bfloat16 [2048, 1024], P('dp'), may hold values from -0.125 to 0.125
- conv_weight: bfloat16 [4, 2304], P(None, 'dp'), may hold values from -3 to 3
- conv_bias: bfloat16 [2304], P('dp'), may hold values from -0.5 to 0.5
- pre_gain: bfloat16 [1024], P('dp'), may hold values from 0.5 to 1.5
- norm_gain: bfloat16 [2048], P('dp'), may hold values from 0.5 to 1.5
- step_bias: bfloat16 [32], P('dp'), may hold values from -4 to -1
- decay_log: bfloat16 [32], P('dp'), may hold values from -4 to 0
- skip_gain: bfloat16 [32], P('dp'), may hold values from 0.5 to 1.5
Outputs:
- mixed: bfloat16 [8, 2048, 1024], P('dp', 'seq')
- grad_tokens: bfloat16 [8, 2048, 1024], P('dp', 'seq')
- grad_in_weight: float32 [1024, 4384], P('dp')
- grad_out_weight: float32 [2048, 1024], P('dp')
- grad_conv_weight: float32 [4, 2304], P(None, 'dp')
- grad_conv_bias: float32 [2304], P('dp')
- grad_pre_gain: float32 [1024], P('dp')
- grad_norm_gain: float32 [2048], P('dp')
- grad_step_bias: float32 [32], P('dp')
- grad_decay_log: float32 [32], P('dp')
- grad_skip_gain: float32 [32], P('dp')
The draws below stay inside these ranges and needn't reach their ends.
All inputs are finite; a program needn't handle non-finite values.
Results may differ from the reference program's by a relative error of at most 0.017.
Values may be sent and summed in bfloat16 or wider, within the bound.
No kernel may reach another device: no remote copies, remote signals or barrier semaphores. Data moves between devices by JAX's collectives and lax.ppermute only.
A program may use at most 192 MiB of HBM per device.

```python
import jax
import jax.numpy as jnp
from jax import lax

D = 1024
HEADS = 32
HEAD_DIM = 64
STATE = 128
CONV = 4
GROUP = 256
INNER = 2048
CONV_CH = 2304
PROJ = 4384
SEQS = 8
LENGTH = 2048


def block_scale(own_key, shape, cuts, smallest, top_value):
    loudness = 1.0
    for axis_at, parts in cuts:
        draws = jax.random.uniform(jax.random.fold_in(jax.random.fold_in(own_key, 6), axis_at), (parts,), jnp.float32, smallest / len(cuts), top_value / len(cuts))
        loudness = loudness * jnp.repeat(jnp.exp(draws), shape[axis_at] // parts).reshape((-1,) + (1,) * (len(shape) - 1 - axis_at))
    return loudness


def centred(stream_key, shape, width, limit, cuts=(), dtype=jnp.bfloat16):
    gain = block_scale(stream_key, shape, cuts, -0.22, 0.18) if cuts else 1.0
    drawn = jax.random.normal(stream_key, shape, jnp.float32) * width * gain
    return jnp.minimum(jnp.maximum(drawn, -limit), limit).astype(dtype)


def setup_inputs(seed: int = 0) -> dict:
    key_of = jax.random.split(jax.random.key(seed), 12)
    tokens = centred(key_of[0], (SEQS, LENGTH, D), 1.0, 6.0, ((0, 8), (1, 4)))
    cotangent = centred(key_of[1], (SEQS, LENGTH, D), 1.0, 6.0, ((0, 8), (1, 4)))
    in_weight = centred(key_of[2], (D, PROJ), D ** -0.5, 0.1875, ((0, 8),))
    out_weight = centred(key_of[3], (INNER, D), INNER ** -0.5, 0.125, ((0, 8),))
    conv_weight = centred(key_of[4], (CONV, CONV_CH), CONV ** -0.5, 3.0, ((1, 8),))
    conv_bias = jnp.clip(jax.random.uniform(key_of[5], (CONV_CH,), jnp.float32, -0.5, 0.5) * block_scale(key_of[5], (CONV_CH,), ((0, 8),), -0.4, 0.0), -0.5, 0.5).astype(jnp.bfloat16)
    pre_gain = jnp.clip(1.0 + 0.1 * jax.random.normal(key_of[6], (D,), jnp.float32), 0.5, 1.5).astype(jnp.bfloat16)
    norm_gain = jnp.clip(1.0 + 0.1 * jax.random.normal(key_of[7], (INNER,), jnp.float32), 0.5, 1.5).astype(jnp.bfloat16)
    step_bias = jnp.clip(-4.0 + 3.0 * jax.random.uniform(key_of[8], (HEADS,), jnp.float32) ** block_scale(key_of[8], (HEADS,), ((0, 8),), -0.2, 0.2), -4.0, -1.0).astype(jnp.bfloat16)
    decay_log = jnp.clip(-4.0 + 4.0 * jax.random.uniform(key_of[9], (HEADS,), jnp.float32) ** block_scale(key_of[9], (HEADS,), ((0, 8),), -0.2, 0.2), -4.0, 0.0).astype(jnp.bfloat16)
    skip_gain = jnp.clip(0.5 + 1.0 * jax.random.uniform(key_of[10], (HEADS,), jnp.float32) ** block_scale(key_of[10], (HEADS,), ((0, 8),), -0.2, 0.2), 0.5, 1.5).astype(jnp.bfloat16)
    return {"tokens": tokens, "cotangent": cotangent, "in_weight": in_weight, "out_weight": out_weight, "conv_weight": conv_weight, "conv_bias": conv_bias, "pre_gain": pre_gain, "norm_gain": norm_gain, "step_bias": step_bias, "decay_log": decay_log, "skip_gain": skip_gain}


@jax.custom_vjp
def low(v):
    return lax.optimization_barrier(v.astype(jnp.bfloat16)).astype(jnp.float32)

@jax.custom_vjp
def low_back(v):
    return v

def low_keep(v):
    return (low(v), None)

def low_pass(kept, grad):
    return (grad,)

def back_keep(v):
    return (v, None)

def back_low(kept, grad):
    return (low(grad),)
low.defvjp(low_keep, low_pass)
low_back.defvjp(back_keep, back_low)
epsilon = 1e-05

def rms_scale(values, gains):
    return values * lax.rsqrt(lax.optimization_barrier(jnp.mean(values * values, axis=-1, keepdims=True)) + epsilon) * gains

def group_part(blocks):
    log_decays, weighted, keys, queries = blocks
    cumul = jnp.cumsum(log_decays, axis=0)
    places = jnp.arange(cumul.shape[0])
    causal = (places[:, None] >= places[None, :])[:, :, None]
    gaps = jnp.where(causal, cumul[:, None, :] - cumul[None, :, :], 0.0)
    kernel = jnp.where(causal, jnp.exp(gaps), 0.0)
    intersection = jnp.dot(queries, keys.T, precision=lax.Precision.HIGHEST)
    intra = jnp.einsum('tsh,shp->thp', kernel * intersection[:, :, None], weighted, precision=lax.Precision.HIGHEST)
    tails = jnp.exp(cumul[-1][None, :] - cumul)
    block_state = jnp.einsum('sh,shp,sn->hpn', tails, weighted, keys, precision=lax.Precision.HIGHEST)
    return (intra, block_state, cumul)

def block_forward(rows, in_weight, out_weight, conv_weight, conv_bias, pre_gain, norm_gain, step_bias, decay_log, skip_gain):
    length = rows.shape[0]
    normed = low(rms_scale(rows, pre_gain))
    projected = low_back(jnp.dot(normed, in_weight, precision=lax.Precision.HIGHEST))
    gate_part = projected[:, :INNER]
    conv_in = jnp.pad(projected[:, INNER:INNER + CONV_CH], ((CONV - 1, 0), (0, 0)))
    step_raw = projected[:, INNER + CONV_CH:]
    conv_out = conv_bias + sum((conv_in[k:k + length] * conv_weight[k] for k in range(CONV)))
    conv_act = jax.nn.silu(conv_out)
    heads_x = conv_act[:, :INNER].reshape(length, HEADS, HEAD_DIM)
    keys = conv_act[:, INNER:INNER + STATE]
    queries = conv_act[:, INNER + STATE:]
    step_size = jax.nn.softplus(step_raw + step_bias)
    log_decays = -step_size * jnp.exp(decay_log)
    weighted = heads_x * step_size[:, :, None]
    count = length // GROUP
    query_blocks = queries.reshape(count, GROUP, STATE)
    blocks = (log_decays.reshape(count, GROUP, HEADS), weighted.reshape(count, GROUP, HEADS, HEAD_DIM), keys.reshape(count, GROUP, STATE), query_blocks)
    intra, block_states, cumuls = lax.map(jax.checkpoint(group_part), blocks)

    def advance(carried, item):
        block_state, cumul = item
        return (jnp.exp(cumul[-1])[:, None, None] * carried + block_state, carried)
    _, starts = lax.scan(advance, jnp.zeros((HEADS, HEAD_DIM, STATE), jnp.float32), (block_states, cumuls))
    inter = jnp.einsum('cqn,chpn->cqhp', query_blocks, starts, precision=lax.Precision.HIGHEST) * jnp.exp(cumuls)[:, :, :, None]
    ssm_out = (intra + inter).reshape(length, HEADS, HEAD_DIM) + skip_gain[:, None] * heads_x
    gated = ssm_out.reshape(length, INNER) * jax.nn.silu(gate_part)
    normed_out = low(rms_scale(gated, norm_gain))
    return rows + jnp.dot(normed_out, out_weight, precision=lax.Precision.HIGHEST)

def reference(tokens, cotangent, in_weight, out_weight, conv_weight, conv_bias, pre_gain, norm_gain, step_bias, decay_log, skip_gain):
    params = tuple((piece.astype(jnp.float32) for piece in (in_weight, out_weight, conv_weight, conv_bias, pre_gain, norm_gain, step_bias, decay_log, skip_gain)))

    def one_sequence(totals, item):
        rows, cot_rows = item
        result, pullback = jax.vjp(block_forward, rows.astype(jnp.float32), *params)
        grads = pullback(cot_rows.astype(jnp.float32))
        summed = tuple((left + right for left, right in zip(totals, grads[1:])))
        return (summed, (result.astype(jnp.bfloat16), grads[0].astype(jnp.bfloat16)))
    zeros = tuple((jnp.zeros_like(piece) for piece in params))
    totals, outputs = lax.scan(one_sequence, zeros, (tokens, cotangent))
    return (outputs[0], outputs[1], totals[0], totals[1], totals[2], totals[3], totals[4], totals[5], totals[6], totals[7], totals[8])
```

```python
import functools

import jax
import jax.numpy as jnp
from jax import lax
from jax.experimental import pallas as pl
from jax.experimental.pallas import tpu as pltpu
from jax.sharding import PartitionSpec as P

HEADS = 32
HEAD_DIM = 64
STATE = 128
CONV = 4
GROUP = 256
INNER = 2048
CONV_CH = 2304
EDGE = 16
TILE = 256
HPT = TILE // HEAD_DIM
TILES = INNER // TILE
LANES = 128

bf16 = jnp.bfloat16
f32 = jnp.float32
epsilon = 1e-05
VMEM_LIMIT = 40 * 1024 * 1024


def params(vmem=VMEM_LIMIT):
    return pltpu.CompilerParams(vmem_limit_bytes=vmem)


def mm(a, b, dims=((1,), (0,))):
    return lax.dot_general(a, b, (dims, ((), ())), preferred_element_type=f32)


NT = ((1,), (1,))
TN = ((0,), (0,))


def split3(v):
    hi = v.astype(bf16)
    rest = v - hi.astype(f32)
    mid = rest.astype(bf16)
    lo = (rest - mid.astype(f32)).astype(bf16)
    return hi, mid, lo


def split2(v):
    hi = v.astype(bf16)
    return hi, (v - hi.astype(f32)).astype(bf16)


def expander(tile):
    head = lax.broadcasted_iota(jnp.int32, (3 * HEADS, TILE), 0) % HEADS
    lane = lax.broadcasted_iota(jnp.int32, (3 * HEADS, TILE), 1)
    return (head == HPT * tile + lane // HEAD_DIM).astype(f32).astype(bf16)


def selector(tile):
    lane = lax.broadcasted_iota(jnp.int32, (TILE, LANES), 0)
    head = lax.broadcasted_iota(jnp.int32, (TILE, LANES), 1)
    return (head == HPT * tile + lane // HEAD_DIM).astype(f32).astype(bf16)


def head_sums(v, sel):
    hi, lo = split2(v)
    return mm(hi, sel) + mm(lo, sel)


def sigmoid(v):
    return 1.0 / (1.0 + jnp.exp(-v))


def conv_of(p_ref, taps_ref, shift_ref, length):
    out = shift_ref[0:1, :]
    for k in range(CONV):
        out = out + p_ref[pl.ds(EDGE - CONV + 1 + k, length), :] * taps_ref[k : k + 1, :]
    return out


def tri(lower):
    r = lax.broadcasted_iota(jnp.int32, (GROUP, GROUP), 0)
    c = lax.broadcasted_iota(jnp.int32, (GROUP, GROUP), 1)
    return ((r >= c) if lower else (r <= c)).astype(f32).astype(bf16)


def lasts(cum3_ref, blocks):
    return jnp.concatenate(
        [cum3_ref[(b + 1) * GROUP - 1 : (b + 1) * GROUP, :] for b in range(blocks)], axis=0
    )


def front_kernel(
    blocks, p_ref, raw_ref, taps_ref, shift_ref, sb_ref, rate_ref,
    x_ref, w_ref, bs_ref, dev_ref, keys_ref, queries_ref, gmat_ref, gmat_t_ref,
    step3_ref, cum3_ref, cum_t_ref,
):
    length = blocks * GROUP
    at = pl.program_id(0)
    conv = conv_of(p_ref, taps_ref, shift_ref, length)
    act = conv * sigmoid(conv)

    @pl.when(at == 0)
    def _():
        keys = act[:, :STATE].astype(bf16)
        queries = act[:, STATE:].astype(bf16)
        keys_ref[...] = keys
        queries_ref[...] = queries
        z = raw_ref[...] + sb_ref[0:1, :]
        step = jnp.maximum(z, 0.0) + jnp.log1p(jnp.exp(-jnp.abs(z)))
        decays = -step * rate_ref[0:1, :]
        step3_ref[...] = jnp.concatenate(split3(step), axis=1)
        low = tri(True)
        for b in range(blocks):
            rows = slice(b * GROUP, (b + 1) * GROUP)
            gmat_ref[b] = mm(queries[rows], keys[rows], NT)
            gmat_t_ref[b] = mm(keys[rows], queries[rows], NT)
            parts = split3(decays[rows])
            cum = mm(low, parts[0]) + mm(low, parts[1]) + mm(low, parts[2])
            cum3_ref[rows, :] = jnp.concatenate(split3(cum), axis=1)
            cum_t_ref[:, rows] = sum(
                mm(part, low, ((0,), (1,))) for part in parts
            )

    @pl.when(at > 0)
    def _():
        spread = expander(at - 1)
        step = mm(step3_ref[...], spread)
        cum = mm(cum3_ref[...], spread)
        weighted = act * step
        x_ref[...] = act.astype(bf16)
        w_ref[...] = weighted.astype(bf16)
        ends = mm(spread, lasts(cum3_ref, blocks), ((0,), (1,)))
        total = None
        for b in range(blocks):
            rows = slice(b * GROUP, (b + 1) * GROUP)
            tails = jnp.exp(cum[(b + 1) * GROUP - 1 : (b + 1) * GROUP, :] - cum[rows])
            state = mm((weighted[rows] * tails).astype(bf16), keys_ref[rows, :], TN)
            bs_ref[b] = state
            total = state if total is None else jnp.exp(ends[:, b : b + 1]) * total + state
        dev_ref[...] = total.astype(bf16)


def front(p, raw, taps, shift, sb, rate):
    length = raw.shape[0]
    blocks = length // GROUP
    tile = lambda g: (0, lax.rem(g + TILES, TILES + 1))
    xt = lambda g: (0, jnp.maximum(g - 1, 0))
    whole2 = lambda g: (0, 0)
    whole3 = lambda g: (0, 0, 0)
    return pl.pallas_call(
        functools.partial(front_kernel, blocks),
        grid=(TILES + 1,),
        in_specs=[
            pl.BlockSpec((length + EDGE, TILE), tile),
            pl.BlockSpec((length, HEADS), whole2),
            pl.BlockSpec((CONV, TILE), tile),
            pl.BlockSpec((1, TILE), tile),
            pl.BlockSpec((1, HEADS), whole2),
            pl.BlockSpec((1, HEADS), whole2),
        ],
        out_specs=[
            pl.BlockSpec((length, TILE), xt),
            pl.BlockSpec((length, TILE), xt),
            pl.BlockSpec((blocks, TILE, STATE), lambda g: (0, jnp.maximum(g - 1, 0), 0)),
            pl.BlockSpec((TILE, STATE), lambda g: (jnp.maximum(g - 1, 0), 0)),
            pl.BlockSpec((length, STATE), whole2),
            pl.BlockSpec((length, STATE), whole2),
            pl.BlockSpec((blocks, GROUP, GROUP), whole3),
            pl.BlockSpec((blocks, GROUP, GROUP), whole3),
            pl.BlockSpec((length, 3 * HEADS), whole2),
            pl.BlockSpec((length, 3 * HEADS), whole2),
            pl.BlockSpec((HEADS, length), whole2),
        ],
        out_shape=[
            jax.ShapeDtypeStruct((length, INNER), bf16),
            jax.ShapeDtypeStruct((length, INNER), bf16),
            jax.ShapeDtypeStruct((blocks, INNER, STATE), f32),
            jax.ShapeDtypeStruct((INNER, STATE), bf16),
            jax.ShapeDtypeStruct((length, STATE), bf16),
            jax.ShapeDtypeStruct((length, STATE), bf16),
            jax.ShapeDtypeStruct((blocks, GROUP, GROUP), f32),
            jax.ShapeDtypeStruct((blocks, GROUP, GROUP), f32),
            jax.ShapeDtypeStruct((length, 3 * HEADS), bf16),
            jax.ShapeDtypeStruct((length, 3 * HEADS), bf16),
            jax.ShapeDtypeStruct((HEADS, length), f32),
        ],
        compiler_params=params(),
        cost_estimate=pl.CostEstimate(flops=600_000_000, bytes_accessed=14_000_000, transcendentals=4_000_000),
        name="front",
    )(p, raw, taps, shift, sb, rate)


def intra_kernel(blocks, w_ref, cum3_ref, cum_t_ref, gmat_ref, y_ref):
    at = pl.program_id(0)
    cum = mm(cum3_ref[...], expander(at))
    r = lax.broadcasted_iota(jnp.int32, (GROUP, GROUP), 0)
    c = lax.broadcasted_iota(jnp.int32, (GROUP, GROUP), 1)
    causal = r >= c
    first = lax.broadcasted_iota(jnp.int32, (GROUP, LANES), 1) < HEAD_DIM
    for b in range(blocks):
        rows = slice(b * GROUP, (b + 1) * GROUP)
        gmat = gmat_ref[b]
        for pair in range(HPT // 2):
            lanes = slice(pair * LANES, (pair + 1) * LANES)
            w = w_ref[rows, lanes]
            outs = []
            for side in range(2):
                j = 2 * pair + side
                col = cum[rows, j * HEAD_DIM : j * HEAD_DIM + 1]
                row = cum_t_ref[pl.ds(HPT * at + j, 1), rows]
                kernel = jnp.exp(jnp.where(causal, col - row, -1e30)) * gmat
                outs.append(mm(kernel.astype(bf16), w))
            y_ref[rows, lanes] = jnp.where(first, outs[0], outs[1])


def intra_of(w, cum3, cum_t, gmat):
    length = w.shape[0]
    blocks = length // GROUP
    tile = lambda g: (0, g)
    whole2 = lambda g: (0, 0)
    return pl.pallas_call(
        functools.partial(intra_kernel, blocks),
        grid=(TILES,),
        in_specs=[
            pl.BlockSpec((length, TILE), tile),
            pl.BlockSpec((length, 3 * HEADS), whole2),
            pl.BlockSpec((HEADS, length), whole2),
            pl.BlockSpec((blocks, GROUP, GROUP), lambda g: (0, 0, 0)),
        ],
        out_specs=pl.BlockSpec((length, TILE), tile),
        out_shape=jax.ShapeDtypeStruct((length, INNER), f32),
        compiler_params=params(),
        cost_estimate=pl.CostEstimate(flops=2_200_000_000, bytes_accessed=7_000_000, transcendentals=4_200_000),
        name="intra",
    )(w, cum3, cum_t, gmat)


def middle_kernel(
    blocks, y_ref, x_ref, gate_ref, gno_ref, q_ref, cum3_ref, start_ref, bs_ref, skip_ref, gain_ref,
    no_ref, dgate_ref, do_ref, dgain_ref, dskip_ref, rowsum_ref, dstart_ref, gdev_ref,
    y_s, sq_s, gt_s, r_s, m_s,
):
    length = blocks * GROUP
    phase, at = pl.program_id(0), pl.program_id(1)
    spread = expander(at)
    cum = mm(cum3_ref[...], spread)
    lanes = pl.ds(pl.multiple_of(at * TILE, TILE), TILE)
    x = x_ref[...].astype(f32)
    gate = gate_ref[...]
    sig = sigmoid(gate)
    gn = gno_ref[...]
    gain = gain_ref[0:1, :]
    skip = skip_ref[0:1, :]
    ends = jnp.exp(mm(spread, lasts(cum3_ref, blocks), ((0,), (1,))))

    @pl.when(phase == 0)
    def _():
        start = start_ref[...]
        for b in range(blocks):
            rows = slice(b * GROUP, (b + 1) * GROUP)
            inter = mm(q_ref[rows, :], start.astype(bf16), NT) * jnp.exp(cum[rows])
            y_s[rows, lanes] = y_ref[rows, :] + inter
            start = ends[:, b : b + 1] * start + bs_ref[b]
        gated = (y_s[:, lanes] + skip * x) * (gate * sig)
        sq = gated * gated
        gt = gated * gn * gain
        sq = sq[:, :LANES] + sq[:, LANES:]
        gt = gt[:, :LANES] + gt[:, LANES:]

        @pl.when(at == 0)
        def _():
            sq_s[...] = sq
            gt_s[...] = gt

        @pl.when(at > 0)
        def _():
            sq_s[...] += sq
            gt_s[...] += gt

    @pl.when(phase == 1)
    def _():
        @pl.when(at == 0)
        def _():
            r = lax.rsqrt(jnp.sum(sq_s[...], axis=1, keepdims=True) / INNER + epsilon)
            m = r * r * r * (jnp.sum(gt_s[...], axis=1, keepdims=True) / INNER)
            r_s[...] = jnp.broadcast_to(r, r_s.shape)
            m_s[...] = jnp.broadcast_to(m, m_s.shape)

        r = r_s[:, 0:1]
        m = m_s[:, 0:1]
        y = y_s[:, lanes]
        ssm = y + skip * x
        silu = gate * sig
        gated = ssm * silu
        scaled = gated * r
        no_ref[...] = (scaled * gain).astype(bf16)
        dgain_ref[...] = jnp.sum(gn * scaled, axis=0, keepdims=True)
        dgated = r * gn * gain - gated * m
        dgate_ref[...] = (dgated * ssm * (sig * (1.0 + gate * (1.0 - sig)))).astype(bf16)
        dof = dgated * silu
        dob = dof.astype(bf16)
        do_ref[...] = dob
        dskip_ref[...] = jnp.sum(dof * x, axis=0, keepdims=True)
        sums = head_sums(dob.astype(f32) * y, selector(at))

        @pl.when(at == 0)
        def _():
            rowsum_ref[...] = sums

        @pl.when(at > 0)
        def _():
            rowsum_ref[...] += sums

        scaled_do = (dof * jnp.exp(cum)).astype(bf16)
        total = None
        for b in reversed(range(blocks)):
            rows = slice(b * GROUP, (b + 1) * GROUP)
            d = mm(scaled_do[rows], q_ref[rows, :], TN)
            dstart_ref[b] = d
            total = d if total is None else ends[:, b : b + 1] * total + d
        gdev_ref[...] = total.astype(bf16)


def middle(y, x, gate, gno, q, cum3, start, bs, skip, gain):
    length = x.shape[0]
    blocks = length // GROUP
    both = lambda p, g: (0, g)
    ph0 = lambda p, g: (0, g * (1 - p) + (TILES - 1) * p)
    ph1 = lambda p, g: (0, g * p)
    whole2 = lambda p, g: (0, 0)
    return pl.pallas_call(
        functools.partial(middle_kernel, blocks),
        grid=(2, TILES),
        in_specs=[
            pl.BlockSpec((length, TILE), ph0),
            pl.BlockSpec((length, TILE), both),
            pl.BlockSpec((length, TILE), both),
            pl.BlockSpec((length, TILE), both),
            pl.BlockSpec((length, STATE), whole2),
            pl.BlockSpec((length, 3 * HEADS), whole2),
            pl.BlockSpec((TILE, STATE), lambda p, g: (g * (1 - p) + (TILES - 1) * p, 0)),
            pl.BlockSpec((blocks, TILE, STATE), lambda p, g: (0, g * (1 - p) + (TILES - 1) * p, 0)),
            pl.BlockSpec((1, TILE), both),
            pl.BlockSpec((1, TILE), both),
        ],
        out_specs=[
            pl.BlockSpec((length, TILE), ph1),
            pl.BlockSpec((length, TILE), ph1),
            pl.BlockSpec((length, TILE), ph1),
            pl.BlockSpec((1, TILE), ph1),
            pl.BlockSpec((1, TILE), ph1),
            pl.BlockSpec((length, LANES), whole2),
            pl.BlockSpec((blocks, TILE, STATE), lambda p, g: (0, g * p, 0)),
            pl.BlockSpec((TILE, STATE), lambda p, g: (g * p, 0)),
        ],
        out_shape=[
            jax.ShapeDtypeStruct((length, INNER), bf16),
            jax.ShapeDtypeStruct((length, INNER), bf16),
            jax.ShapeDtypeStruct((length, INNER), bf16),
            jax.ShapeDtypeStruct((1, INNER), f32),
            jax.ShapeDtypeStruct((1, INNER), f32),
            jax.ShapeDtypeStruct((length, LANES), f32),
            jax.ShapeDtypeStruct((blocks, INNER, STATE), f32),
            jax.ShapeDtypeStruct((INNER, STATE), bf16),
        ],
        scratch_shapes=[
            pltpu.VMEM((length, INNER), f32),
            pltpu.VMEM((length, LANES), f32),
            pltpu.VMEM((length, LANES), f32),
            pltpu.VMEM((length, LANES), f32),
            pltpu.VMEM((length, LANES), f32),
        ],
        compiler_params=params(),
        cost_estimate=pl.CostEstimate(flops=1_200_000_000, bytes_accessed=32_000_000, transcendentals=6_000_000),
        name="middle",
    )(y, x, gate, gno, q, cum3, start, bs, skip, gain)


def intra_back_kernel(
    blocks, w_ref, do_ref, cum3_ref, cum_t_ref, gmat_t_ref, k_ref, q_ref, dw_ref, dq_ref, dk_ref, dg_s
):
    at = pl.program_id(0)
    cum = mm(cum3_ref[...], expander(at))
    r = lax.broadcasted_iota(jnp.int32, (GROUP, GROUP), 0)
    c = lax.broadcasted_iota(jnp.int32, (GROUP, GROUP), 1)
    causal = c >= r
    first = lax.broadcasted_iota(jnp.int32, (GROUP, LANES), 1) < HEAD_DIM
    for b in range(blocks):
        rows = slice(b * GROUP, (b + 1) * GROUP)
        gmat = gmat_t_ref[b]
        dg = None
        for pair in range(HPT // 2):
            lanes = slice(pair * LANES, (pair + 1) * LANES)
            w = w_ref[rows, lanes]
            do = do_ref[rows, lanes]
            outs = []
            for side in range(2):
                j = 2 * pair + side
                col = cum[rows, j * HEAD_DIM : j * HEAD_DIM + 1]
                row = cum_t_ref[pl.ds(HPT * at + j, 1), rows]
                decay = jnp.exp(jnp.where(causal, row - col, -1e30))
                outs.append(mm((decay * gmat).astype(bf16), do))
                own = jnp.where(first if side == 0 else ~first, w, jnp.zeros_like(w))
                term = mm(own, do, NT) * decay
                dg = term if dg is None else dg + term
            dw_ref[rows, lanes] = jnp.where(first, outs[0], outs[1])

        @pl.when(at == 0)
        def _():
            dg_s[b] = dg

        @pl.when(at > 0)
        def _():
            dg_s[b] += dg

    @pl.when(at == TILES - 1)
    def _():
        for b in range(blocks):
            rows = slice(b * GROUP, (b + 1) * GROUP)
            dg = dg_s[b].astype(bf16)
            dk_ref[rows, :] = mm(dg, q_ref[rows, :])
            dq_ref[rows, :] = mm(dg, k_ref[rows, :], TN)


def intra_back(w, do, cum3, cum_t, gmat_t, k, q):
    length = w.shape[0]
    blocks = length // GROUP
    tile = lambda g: (0, g)
    whole2 = lambda g: (0, 0)
    return pl.pallas_call(
        functools.partial(intra_back_kernel, blocks),
        grid=(TILES,),
        in_specs=[
            pl.BlockSpec((length, TILE), tile),
            pl.BlockSpec((length, TILE), tile),
            pl.BlockSpec((length, 3 * HEADS), whole2),
            pl.BlockSpec((HEADS, length), whole2),
            pl.BlockSpec((blocks, GROUP, GROUP), lambda g: (0, 0, 0)),
            pl.BlockSpec((length, STATE), whole2),
            pl.BlockSpec((length, STATE), whole2),
        ],
        out_specs=[
            pl.BlockSpec((length, TILE), tile),
            pl.BlockSpec((length, STATE), whole2),
            pl.BlockSpec((length, STATE), whole2),
        ],
        out_shape=[
            jax.ShapeDtypeStruct((length, INNER), f32),
            jax.ShapeDtypeStruct((length, STATE), f32),
            jax.ShapeDtypeStruct((length, STATE), f32),
        ],
        scratch_shapes=[pltpu.VMEM((blocks, GROUP, GROUP), f32)],
        compiler_params=params(),
        cost_estimate=pl.CostEstimate(flops=4_400_000_000, bytes_accessed=10_000_000, transcendentals=4_200_000),
        name="intra_back",
    )(w, do, cum3, cum_t, gmat_t, k, q)


def back_kernel(
    blocks, p_ref, taps_ref, shift_ref, x_ref, w_ref, do_ref, dwi_ref, skip_ref,
    start_ref, bs_ref, adj_ref, dstart_ref,
    k_ref, q_ref, step3_ref, cum3_ref, dqi_ref, dki_ref, rowsum_ref, raw_ref, sb_ref, rate_ref,
    gp_ref, last_ref, before_ref, dtaps_ref, dshift_ref, draw_ref, dsb_ref, drate_ref,
    dq_s, dk_s, sx_s, sw_s, sv_s, dec_s, d_s,
):
    length = blocks * GROUP
    at = pl.program_id(0)

    @pl.when(at == 0)
    def _():
        dq_s[...] = dqi_ref[...]
        dk_s[...] = dki_ref[...]
        sx_s[...] = jnp.zeros_like(sx_s)
        sw_s[...] = jnp.zeros_like(sw_s)
        sv_s[...] = jnp.zeros_like(sv_s)
        dec_s[...] = jnp.zeros_like(dec_s)
        d_s[0:EDGE, :] = jnp.zeros((EDGE, TILE), f32)
        d_s[length + EDGE :, :] = jnp.zeros((EDGE, TILE), f32)

    def conv_back(dact):
        conv = conv_of(p_ref, taps_ref, shift_ref, length)
        sig = sigmoid(conv)
        dconv = dact * (sig * (1.0 + conv * (1.0 - sig)))
        d_s[EDGE : EDGE + length, :] = dconv
        dshift_ref[...] = jnp.sum(dconv, axis=0, keepdims=True)
        dp = None
        before = None
        for k in range(CONV):
            tap = taps_ref[k : k + 1, :]
            src = p_ref[pl.ds(EDGE - CONV + 1 + k, length), :]
            dtaps_ref[k : k + 1, :] = jnp.sum(dconv * src, axis=0, keepdims=True)
            term = tap * d_s[pl.ds(EDGE + CONV - 1 - k, length), :]
            dp = term if dp is None else dp + term
            edge = tap * d_s[pl.ds(CONV - 1 - k, EDGE), :]
            before = edge if before is None else before + edge
        gp_ref[...] = dp.astype(bf16)
        last_ref[...] = dp[length - EDGE :, :]
        before_ref[...] = before

    @pl.when(at < TILES)
    def _():
        spread = expander(at)
        sel = selector(at)
        cum = mm(cum3_ref[...], spread)
        step = mm(step3_ref[...], spread)
        ends = jnp.exp(mm(spread, lasts(cum3_ref, blocks), ((0,), (1,))))
        x = x_ref[...].astype(f32)
        w = w_ref[...].astype(f32)
        do = do_ref[...].astype(f32)
        scaled_do = (do * jnp.exp(cum)).astype(bf16)
        starts = [start_ref[...]]
        for b in range(blocks - 1):
            starts.append(ends[:, b : b + 1] * starts[b] + bs_ref[b])
        adjs = [None] * blocks
        adj = adj_ref[...]
        for b in reversed(range(blocks)):
            adjs[b] = adj
            adj = ends[:, b : b + 1] * adj + dstart_ref[b]
        dws = []
        for b in range(blocks):
            rows = slice(b * GROUP, (b + 1) * GROUP)
            tails = jnp.exp(cum[(b + 1) * GROUP - 1 : (b + 1) * GROUP, :] - cum[rows])
            ab = adjs[b].astype(bf16)
            dws.append(tails * mm(k_ref[rows, :], ab, NT))
            dk_s[rows, :] += mm((w[rows] * tails).astype(bf16), ab)
            dq_s[rows, :] += mm(scaled_do[rows], starts[b].astype(bf16))
            hi, lo = split2(ends[:, b : b + 1] * adjs[b] * starts[b])
            dec_s[b : b + 1, :] += jnp.sum(mm(hi, sel, TN) + mm(lo, sel, TN), axis=0, keepdims=True)
        dws = jnp.concatenate(dws, axis=0)
        dw = dwi_ref[...] + dws
        sx_s[...] += head_sums(dw * x, sel)
        sw_s[...] += head_sums(dw * w, sel)
        sv_s[...] += head_sums(dws * w, sel)
        conv_back(dw * step + do * skip_ref[0:1, :])

    @pl.when(at == TILES)
    def _():
        conv_back(jnp.concatenate([dk_s[...], dq_s[...]], axis=1))
        dcum = (rowsum_ref[...] - sw_s[...])[:, :HEADS]
        sv = sv_s[...][:, :HEADS]
        z = raw_ref[...] + sb_ref[0:1, :]
        step = jnp.maximum(z, 0.0) + jnp.log1p(jnp.exp(-jnp.abs(z)))
        rate = rate_ref[0:1, :]
        up = tri(False)
        decays = []
        for b in range(blocks):
            rows = slice(b * GROUP, (b + 1) * GROUP)
            parts = split3(dcum[rows])
            extra = jnp.sum(sv[rows], axis=0, keepdims=True) + dec_s[b : b + 1, :HEADS]
            decays.append(mm(up, parts[0]) + mm(up, parts[1]) + mm(up, parts[2]) + extra)
        ddecay = jnp.concatenate(decays, axis=0)
        dstep = sx_s[...][:, :HEADS] - ddecay * rate
        dz = dstep * sigmoid(z)
        draw_ref[...] = dz.astype(bf16)
        dsb_ref[...] = jnp.sum(dz, axis=0, keepdims=True)
        drate_ref[...] = jnp.sum(-ddecay * step * rate, axis=0, keepdims=True)


def back(p, taps, shift, x, w, do, dwi, skip, start, bs, adj, dstart, k, q, step3, cum3, dqi, dki, rowsum, raw, sb, rate):
    length = x.shape[0]
    blocks = length // GROUP
    tile = lambda g: (0, g)
    xt = lambda g: (0, jnp.minimum(g, TILES - 1))
    st = lambda g: (jnp.minimum(g, TILES - 1), 0)
    st3 = lambda g: (0, jnp.minimum(g, TILES - 1), 0)
    whole2 = lambda g: (0, 0)
    spec = pl.BlockSpec
    return pl.pallas_call(
        functools.partial(back_kernel, blocks),
        grid=(TILES + 1,),
        in_specs=[
            spec((length + EDGE, TILE), tile),
            spec((CONV, TILE), tile),
            spec((1, TILE), tile),
            spec((length, TILE), xt),
            spec((length, TILE), xt),
            spec((length, TILE), xt),
            spec((length, TILE), xt),
            spec((1, TILE), xt),
            spec((TILE, STATE), st),
            spec((blocks, TILE, STATE), st3),
            spec((TILE, STATE), st),
            spec((blocks, TILE, STATE), st3),
            spec((length, STATE), whole2),
            spec((length, STATE), whole2),
            spec((length, 3 * HEADS), whole2),
            spec((length, 3 * HEADS), whole2),
            spec((length, STATE), whole2),
            spec((length, STATE), whole2),
            spec((length, LANES), whole2),
            spec((length, HEADS), whole2),
            spec((1, HEADS), whole2),
            spec((1, HEADS), whole2),
        ],
        out_specs=[
            spec((length, TILE), tile),
            spec((EDGE, TILE), tile),
            spec((EDGE, TILE), tile),
            spec((CONV, TILE), tile),
            spec((1, TILE), tile),
            spec((length, HEADS), whole2),
            spec((1, HEADS), whole2),
            spec((1, HEADS), whole2),
        ],
        out_shape=[
            jax.ShapeDtypeStruct((length, CONV_CH), bf16),
            jax.ShapeDtypeStruct((EDGE, CONV_CH), f32),
            jax.ShapeDtypeStruct((EDGE, CONV_CH), f32),
            jax.ShapeDtypeStruct((CONV, CONV_CH), f32),
            jax.ShapeDtypeStruct((1, CONV_CH), f32),
            jax.ShapeDtypeStruct((length, HEADS), bf16),
            jax.ShapeDtypeStruct((1, HEADS), f32),
            jax.ShapeDtypeStruct((1, HEADS), f32),
        ],
        scratch_shapes=[
            pltpu.VMEM((length, STATE), f32),
            pltpu.VMEM((length, STATE), f32),
            pltpu.VMEM((length, LANES), f32),
            pltpu.VMEM((length, LANES), f32),
            pltpu.VMEM((length, LANES), f32),
            pltpu.VMEM((8, LANES), f32),
            pltpu.VMEM((length + 2 * EDGE, TILE), f32),
        ],
        compiler_params=params(),
        cost_estimate=pl.CostEstimate(flops=2_500_000_000, bytes_accessed=32_000_000, transcendentals=6_000_000),
        name="back",
    )(p, taps, shift, x, w, do, dwi, skip, start, bs, adj, dstart, k, q, step3, cum3, dqi, dki, rowsum, raw, sb, rate)


def carried(decay, state, axis, reverse):
    size, here = lax.axis_size(axis), lax.axis_index(axis)
    rows = lambda d: jnp.repeat(d, HEAD_DIM)[:, None]
    if size == 4:
        core, x = here % 2, here // 2
        swap = [(i, i ^ 1) for i in range(4)]
        mate, mate_decay = lax.ppermute(state, axis, swap), lax.ppermute(decay, axis, swap)
        own, other = state.astype(f32), mate.astype(f32)
        ahead = (core == 0) if reverse else (core == 1)
        pair = jnp.where(
            ahead,
            rows(decay) * other + own,
            rows(mate_decay) * own + other,
        ).astype(bf16)
        route = [(2, 0), (3, 1)] if reverse else [(0, 2), (1, 3)]
        far = lax.ppermute(pair, axis, route).astype(f32)
        near = jnp.where(ahead, other, 0.0)
        return near + jnp.where(ahead, rows(mate_decay), 1.0) * far
    states = lax.all_gather(state, axis)
    decays = lax.all_gather(decay, axis)

    def one(lap, total):
        at = size - 1 - lap if reverse else lap
        use = at > here if reverse else at < here
        new = rows(decays[at]) * total + states[at].astype(f32)
        return jnp.where(use, new, total)

    return lax.fori_loop(0, size, one, jnp.zeros(state.shape, f32))


def rms_scale(values, gains):
    return values * lax.rsqrt(jnp.mean(values * values, axis=-1, keepdims=True) + epsilon) * gains


def gather_rows(shard):
    return lax.all_gather(shard, "dp", axis=0, tiled=True)


def reduce_rows(full):
    part = lax.psum_scatter(full.astype(bf16), "dp", scatter_dimension=0, tiled=True)
    return lax.psum(part, "seq").astype(f32)


def shards(
    tokens, cotangent, in_weight, out_weight, conv_weight, conv_bias,
    pre_gain, norm_gain, step_bias, decay_log, skip_gain,
):
    dp = lax.axis_size("dp")
    seq = lax.axis_size("seq")
    width = tokens.shape[2]
    pieces = [
        conv_weight, conv_bias, pre_gain, norm_gain, step_bias, decay_log, skip_gain,
        in_weight[:, INNER + CONV_CH :],
    ]
    shapes = [piece.shape for piece in pieces]
    sizes = [piece.size for piece in pieces]
    used = sum(sizes)
    padded = -(-used // 2048) * 2048
    flat = jnp.concatenate([piece.reshape(-1) for piece in pieces] + [jnp.zeros((padded - used,), bf16)])
    small = lax.all_gather(flat, "dp")
    got, at = [], 0
    for shape, size in zip(shapes, sizes):
        got.append(small[:, at : at + size].reshape((dp,) + shape))
        at += size
    taps = jnp.moveaxis(got[0], 0, 1).reshape(CONV, CONV_CH).astype(f32)
    shift, gains_pre, gains_norm, bias_step, log_rates, skip = [
        piece.reshape(-1).astype(f32) for piece in got[1:7]
    ]
    step_weight = got[7].reshape(width, HEADS)
    conv_full = gather_rows(in_weight[:, INNER : INNER + CONV_CH])
    gate_full = gather_rows(in_weight[:, :INNER])
    out_full = gather_rows(out_weight)
    shift = shift[None]
    rate = jnp.exp(log_rates)[None]
    bias_step = bias_step[None]
    skip_lanes = jnp.repeat(skip, HEAD_DIM)[None]

    toks = tokens[0]
    length = toks.shape[0]
    edge = lax.ppermute(toks[length - EDGE :], "seq", [(i, i + 1) for i in range(seq - 1)])
    normed_ext = rms_scale(jnp.concatenate([edge, toks], axis=0).astype(f32), gains_pre).astype(bf16)
    normed = normed_ext[EDGE:]
    p = jnp.dot(normed_ext, conv_full, preferred_element_type=f32)
    raw = jnp.dot(normed, step_weight, preferred_element_type=f32)
    x, w, bs, dev, k, q, gmat, gmat_t, step3, cum3, cum_t = front(p, raw, taps, shift, bias_step, rate)
    blocks = length // GROUP
    dev_decay = jnp.exp(sum(cum_t[:, (b + 1) * GROUP - 1] for b in range(blocks)))
    start = carried(dev_decay, dev, "seq", False)
    y = intra_of(w, cum3, cum_t, gmat)
    gate = jnp.dot(normed, gate_full, preferred_element_type=f32)
    cot = cotangent[0]
    gno = lax.dot_general(cot, out_full, (((1,), (1,)), ((), ())), preferred_element_type=f32)
    no, dgate, do, dgain, dskip, rowsum, dstart, gdev = middle(
        y, x, gate, gno, q, cum3, start, bs, skip_lanes, gains_norm[None]
    )
    adj = carried(dev_decay, gdev, "seq", True)
    rows = toks.astype(f32)
    mixed = (rows + jnp.dot(no, out_full, preferred_element_type=f32)).astype(bf16)
    over_rows = (((0,), (0,)), ((), ()))
    grad_out = reduce_rows(lax.dot_general(no, cot, over_rows, preferred_element_type=f32))
    grad_gate = reduce_rows(lax.dot_general(normed, dgate, over_rows, preferred_element_type=f32))
    dwi, dqi, dki = intra_back(w, do, cum3, cum_t, gmat_t, k, q)
    gp, last, before, dtaps, dshift, draw, dsb, drate = back(
        p, taps, shift, x, w, do, dwi, skip_lanes, start, bs, adj, dstart,
        k, q, step3, cum3, dqi, dki, rowsum, raw, bias_step, rate,
    )
    returned = lax.ppermute(before, "seq", [(i + 1, i) for i in range(seq - 1)])
    gp = gp.at[length - EDGE :].set((last + returned).astype(bf16))
    grad_conv = reduce_rows(lax.dot_general(normed, gp, over_rows, preferred_element_type=f32))
    grad_step = lax.dot_general(normed, draw, over_rows, preferred_element_type=f32)
    over_cols = (((1,), (1,)), ((), ()))
    dnormed = (
        lax.dot_general(gp, conv_full, over_cols, preferred_element_type=f32)
        + lax.dot_general(dgate, gate_full, over_cols, preferred_element_type=f32)
        + lax.dot_general(draw, step_weight, over_cols, preferred_element_type=f32)
    )
    r = lax.rsqrt(jnp.mean(rows * rows, axis=-1, keepdims=True) + epsilon)
    t = dnormed * gains_pre
    drows = r * t - rows * (r * r * r * jnp.mean(rows * t, axis=-1, keepdims=True))
    grad_tokens = (cot.astype(f32) + drows).astype(bf16)
    dpre = jnp.sum(dnormed * rows * r, axis=0)

    smalls = [
        jnp.moveaxis(dtaps.reshape(CONV, dp, -1), 1, 0).reshape(dp, -1),
        dshift.reshape(dp, -1),
        dpre.reshape(dp, -1),
        dgain.reshape(dp, -1),
        dsb.reshape(dp, -1),
        drate.reshape(dp, -1),
        jnp.sum(dskip.reshape(HEADS, HEAD_DIM), axis=1).reshape(dp, -1),
        grad_step.reshape(dp, -1),
    ]
    bundle = jnp.concatenate(smalls + [jnp.zeros((dp, padded - used), f32)], axis=1).astype(bf16)
    mine = lax.psum(lax.psum_scatter(bundle, "dp", scatter_dimension=0), "seq").astype(f32)
    outs, at = [], 0
    for shape, size in zip(shapes, sizes):
        outs.append(mine[at : at + size].reshape(shape))
        at += size
    grad_in = jnp.concatenate([grad_gate, grad_conv, outs[7]], axis=1)
    return (
        mixed[None], grad_tokens[None], grad_in, grad_out, outs[0], outs[1],
        outs[2], outs[3], outs[4], outs[5], outs[6],
    )


def solution(mesh):
    return jax.shard_map(
        shards,
        mesh=mesh,
        in_specs=(
            P("dp", "seq", None), P("dp", "seq", None), P("dp", None), P("dp", None),
            P(None, "dp"), P("dp"), P("dp"), P("dp"), P("dp"), P("dp"), P("dp"),
        ),
        out_specs=(
            P("dp", "seq", None), P("dp", "seq", None), P("dp", None), P("dp", None),
            P(None, "dp"), P("dp"), P("dp"), P("dp"), P("dp"), P("dp"), P("dp"),
        ),
        check_vma=False,
    )
```

```python
import functools

import jax
import jax.numpy as jnp
from jax import lax
from jax.experimental import pallas as pl
from jax.experimental.pallas import tpu as pltpu
from jax.sharding import PartitionSpec as P

HEADS = 32
HEAD_DIM = 64
STATE = 128
CONV = 4
GROUP = 256
INNER = 2048
CONV_CH = 2304
EDGE = 16
TILE = 256
HPT = TILE // HEAD_DIM
TILES = INNER // TILE
LANES = 128

bf16 = jnp.bfloat16
f32 = jnp.float32
epsilon = 1e-05
VMEM_LIMIT = 40 * 1024 * 1024


def params(vmem=VMEM_LIMIT):
    return pltpu.CompilerParams(vmem_limit_bytes=vmem)


def mm(a, b, dims=((1,), (0,))):
    return lax.dot_general(a, b, (dims, ((), ())), preferred_element_type=f32)


NT = ((1,), (1,))
TN = ((0,), (0,))


def split3(v):
    hi = v.astype(bf16)
    rest = v - hi.astype(f32)
    mid = rest.astype(bf16)
    lo = (rest - mid.astype(f32)).astype(bf16)
    return hi, mid, lo


def split2(v):
    hi = v.astype(bf16)
    return hi, (v - hi.astype(f32)).astype(bf16)


def expander(tile):
    head = lax.broadcasted_iota(jnp.int32, (3 * HEADS, TILE), 0) % HEADS
    lane = lax.broadcasted_iota(jnp.int32, (3 * HEADS, TILE), 1)
    return (head == HPT * tile + lane // HEAD_DIM).astype(f32).astype(bf16)


def selector(tile):
    lane = lax.broadcasted_iota(jnp.int32, (TILE, LANES), 0)
    head = lax.broadcasted_iota(jnp.int32, (TILE, LANES), 1)
    return (head == HPT * tile + lane // HEAD_DIM).astype(f32).astype(bf16)


def head_sums(v, sel):
    hi, lo = split2(v)
    return mm(hi, sel) + mm(lo, sel)


def sigmoid(v):
    return 1.0 / (1.0 + jnp.exp(-v))


def conv_of(p_ref, taps_ref, shift_ref, length):
    out = shift_ref[0:1, :]
    for k in range(CONV):
        out = out + p_ref[pl.ds(EDGE - CONV + 1 + k, length), :] * taps_ref[k : k + 1, :]
    return out


def tri(lower):
    r = lax.broadcasted_iota(jnp.int32, (GROUP, GROUP), 0)
    c = lax.broadcasted_iota(jnp.int32, (GROUP, GROUP), 1)
    return ((r >= c) if lower else (r <= c)).astype(f32).astype(bf16)


def lasts(cum3_ref, blocks):
    return jnp.concatenate(
        [cum3_ref[(b + 1) * GROUP - 1 : (b + 1) * GROUP, :] for b in range(blocks)], axis=0
    )


def front_kernel(
    blocks, p_ref, raw_ref, taps_ref, shift_ref, sb_ref, rate_ref,
    x_ref, w_ref, bs_ref, dev_ref, keys_ref, queries_ref, gmat_ref, gmat_t_ref,
    step3_ref, cum3_ref, cum_t_ref,
):
    length = blocks * GROUP
    at = pl.program_id(0)
    conv = conv_of(p_ref, taps_ref, shift_ref, length)
    act = conv * sigmoid(conv)

    @pl.when(at == 0)
    def _():
        keys = act[:, :STATE].astype(bf16)
        queries = act[:, STATE:].astype(bf16)
        keys_ref[...] = keys
        queries_ref[...] = queries
        z = raw_ref[EDGE:, :HEADS] + sb_ref[0:1, :]
        step = jnp.maximum(z, 0.0) + jnp.log1p(jnp.exp(-jnp.abs(z)))
        decays = -step * rate_ref[0:1, :]
        step3_ref[...] = jnp.concatenate(split3(step), axis=1)
        low = tri(True)
        for b in range(blocks):
            rows = slice(b * GROUP, (b + 1) * GROUP)
            gmat_ref[b] = mm(queries[rows], keys[rows], NT)
            gmat_t_ref[b] = mm(keys[rows], queries[rows], NT)
            parts = split3(decays[rows])
            cum = mm(low, parts[0]) + mm(low, parts[1]) + mm(low, parts[2])
            cum3_ref[rows, :] = jnp.concatenate(split3(cum), axis=1)
            cum_t_ref[:, rows] = sum(
                mm(part, low, ((0,), (1,))) for part in parts
            )

    @pl.when(at > 0)
    def _():
        spread = expander(at - 1)
        step = mm(step3_ref[...], spread)
        cum = mm(cum3_ref[...], spread)
        weighted = act * step
        x_ref[...] = act.astype(bf16)
        w_ref[...] = weighted.astype(bf16)
        ends = mm(spread, lasts(cum3_ref, blocks), ((0,), (1,)))
        total = None
        for b in range(blocks):
            rows = slice(b * GROUP, (b + 1) * GROUP)
            tails = jnp.exp(cum[(b + 1) * GROUP - 1 : (b + 1) * GROUP, :] - cum[rows])
            state = mm((weighted[rows] * tails).astype(bf16), keys_ref[rows, :], TN)
            bs_ref[b] = state
            total = state if total is None else jnp.exp(ends[:, b : b + 1]) * total + state
        dev_ref[0] = total.astype(bf16)
        whole = jnp.exp(sum(ends[:, b : b + 1] for b in range(blocks)))
        dev_ref[1] = jnp.broadcast_to(whole, total.shape).astype(bf16)


def front(p, taps, shift, sb, rate):
    length = p.shape[0] - EDGE
    blocks = length // GROUP
    tile = lambda g: (0, lax.rem(g + TILES, TILES + 1))
    xt = lambda g: (0, jnp.maximum(g - 1, 0))
    whole2 = lambda g: (0, 0)
    whole3 = lambda g: (0, 0, 0)
    return pl.pallas_call(
        functools.partial(front_kernel, blocks),
        grid=(TILES + 1,),
        in_specs=[
            pl.BlockSpec((length + EDGE, TILE), tile),
            pl.BlockSpec((length + EDGE, LANES), lambda g: (0, CONV_CH // LANES)),
            pl.BlockSpec((CONV, TILE), tile),
            pl.BlockSpec((1, TILE), tile),
            pl.BlockSpec((1, HEADS), whole2),
            pl.BlockSpec((1, HEADS), whole2),
        ],
        out_specs=[
            pl.BlockSpec((length, TILE), xt),
            pl.BlockSpec((length, TILE), xt),
            pl.BlockSpec((blocks, TILE, STATE), lambda g: (0, jnp.maximum(g - 1, 0), 0)),
            pl.BlockSpec((2, TILE, STATE), lambda g: (0, jnp.maximum(g - 1, 0), 0)),
            pl.BlockSpec((length, STATE), whole2),
            pl.BlockSpec((length, STATE), whole2),
            pl.BlockSpec((blocks, GROUP, GROUP), whole3),
            pl.BlockSpec((blocks, GROUP, GROUP), whole3),
            pl.BlockSpec((length, 3 * HEADS), whole2),
            pl.BlockSpec((length, 3 * HEADS), whole2),
            pl.BlockSpec((HEADS, length), whole2),
        ],
        out_shape=[
            jax.ShapeDtypeStruct((length, INNER), bf16),
            jax.ShapeDtypeStruct((length, INNER), bf16),
            jax.ShapeDtypeStruct((blocks, INNER, STATE), f32),
            jax.ShapeDtypeStruct((2, INNER, STATE), bf16),
            jax.ShapeDtypeStruct((length, STATE), bf16),
            jax.ShapeDtypeStruct((length, STATE), bf16),
            jax.ShapeDtypeStruct((blocks, GROUP, GROUP), f32),
            jax.ShapeDtypeStruct((blocks, GROUP, GROUP), f32),
            jax.ShapeDtypeStruct((length, 3 * HEADS), bf16),
            jax.ShapeDtypeStruct((length, 3 * HEADS), bf16),
            jax.ShapeDtypeStruct((HEADS, length), f32),
        ],
        compiler_params=params(),
        cost_estimate=pl.CostEstimate(flops=600_000_000, bytes_accessed=14_000_000, transcendentals=4_000_000),
        name="front",
    )(p, p, taps, shift, sb, rate)


def intra_kernel(blocks, w_ref, cum3_ref, cum_t_ref, gmat_ref, y_ref):
    at = pl.program_id(0)
    cum = mm(cum3_ref[...], expander(at))
    r = lax.broadcasted_iota(jnp.int32, (GROUP, GROUP), 0)
    c = lax.broadcasted_iota(jnp.int32, (GROUP, GROUP), 1)
    causal = r >= c
    first = lax.broadcasted_iota(jnp.int32, (GROUP, LANES), 1) < HEAD_DIM
    for b in range(blocks):
        rows = slice(b * GROUP, (b + 1) * GROUP)
        gmat = gmat_ref[b]
        for pair in range(HPT // 2):
            lanes = slice(pair * LANES, (pair + 1) * LANES)
            w = w_ref[rows, lanes]
            outs = []
            for side in range(2):
                j = 2 * pair + side
                col = cum[rows, j * HEAD_DIM : j * HEAD_DIM + 1]
                row = cum_t_ref[pl.ds(HPT * at + j, 1), rows]
                kernel = jnp.exp(jnp.where(causal, col - row, -1e30)) * gmat
                outs.append(mm(kernel.astype(bf16), w))
            y_ref[rows, lanes] = jnp.where(first, outs[0], outs[1])


def intra_of(w, cum3, cum_t, gmat):
    length = w.shape[0]
    blocks = length // GROUP
    tile = lambda g: (0, g)
    whole2 = lambda g: (0, 0)
    return pl.pallas_call(
        functools.partial(intra_kernel, blocks),
        grid=(TILES,),
        in_specs=[
            pl.BlockSpec((length, TILE), tile),
            pl.BlockSpec((length, 3 * HEADS), whole2),
            pl.BlockSpec((HEADS, length), whole2),
            pl.BlockSpec((blocks, GROUP, GROUP), lambda g: (0, 0, 0)),
        ],
        out_specs=pl.BlockSpec((length, TILE), tile),
        out_shape=jax.ShapeDtypeStruct((length, INNER), f32),
        compiler_params=params(),
        cost_estimate=pl.CostEstimate(flops=2_200_000_000, bytes_accessed=7_000_000, transcendentals=4_200_000),
        name="intra",
    )(w, cum3, cum_t, gmat)


def middle_kernel(
    blocks, y_ref, x_ref, gate_ref, gno_ref, q_ref, cum3_ref, start_ref, bs_ref, skip_ref, gain_ref,
    no_ref, dgate_ref, do_ref, dgain_ref, dskip_ref, rowsum_ref, dstart_ref, gdev_ref,
    y_s, sq_s, gt_s, r_s, m_s,
):
    length = blocks * GROUP
    phase, at = pl.program_id(0), pl.program_id(1)
    spread = expander(at)
    cum = mm(cum3_ref[...], spread)
    lanes = pl.ds(pl.multiple_of(at * TILE, TILE), TILE)
    x = x_ref[...].astype(f32)
    gate = gate_ref[...]
    sig = sigmoid(gate)
    gn = gno_ref[...]
    gain = gain_ref[0:1, :]
    skip = skip_ref[0:1, :]
    ends = jnp.exp(mm(spread, lasts(cum3_ref, blocks), ((0,), (1,))))

    @pl.when(phase == 0)
    def _():
        start = start_ref[...]
        for b in range(blocks):
            rows = slice(b * GROUP, (b + 1) * GROUP)
            inter = mm(q_ref[rows, :], start.astype(bf16), NT) * jnp.exp(cum[rows])
            y_s[rows, lanes] = y_ref[rows, :] + inter
            start = ends[:, b : b + 1] * start + bs_ref[b]
        gated = (y_s[:, lanes] + skip * x) * (gate * sig)
        sq = gated * gated
        gt = gated * gn * gain
        sq = sq[:, :LANES] + sq[:, LANES:]
        gt = gt[:, :LANES] + gt[:, LANES:]

        @pl.when(at == 0)
        def _():
            sq_s[...] = sq
            gt_s[...] = gt

        @pl.when(at > 0)
        def _():
            sq_s[...] += sq
            gt_s[...] += gt

    @pl.when(phase == 1)
    def _():
        @pl.when(at == 0)
        def _():
            r = lax.rsqrt(jnp.sum(sq_s[...], axis=1, keepdims=True) / INNER + epsilon)
            m = r * r * r * (jnp.sum(gt_s[...], axis=1, keepdims=True) / INNER)
            r_s[...] = jnp.broadcast_to(r, r_s.shape)
            m_s[...] = jnp.broadcast_to(m, m_s.shape)

        r = r_s[:, 0:1]
        m = m_s[:, 0:1]
        y = y_s[:, lanes]
        ssm = y + skip * x
        silu = gate * sig
        gated = ssm * silu
        scaled = gated * r
        no_ref[...] = (scaled * gain).astype(bf16)
        dgain_ref[...] = jnp.sum(gn * scaled, axis=0, keepdims=True)
        dgated = r * gn * gain - gated * m
        dgate_ref[...] = (dgated * ssm * (sig * (1.0 + gate * (1.0 - sig)))).astype(bf16)
        dof = dgated * silu
        dob = dof.astype(bf16)
        do_ref[...] = dob
        dskip_ref[...] = jnp.sum(dof * x, axis=0, keepdims=True)
        sums = head_sums(dob.astype(f32) * y, selector(at))

        @pl.when(at == 0)
        def _():
            rowsum_ref[...] = sums

        @pl.when(at > 0)
        def _():
            rowsum_ref[...] += sums

        scaled_do = (dof * jnp.exp(cum)).astype(bf16)
        total = None
        for b in reversed(range(blocks)):
            rows = slice(b * GROUP, (b + 1) * GROUP)
            d = mm(scaled_do[rows], q_ref[rows, :], TN)
            dstart_ref[b] = d
            total = d if total is None else ends[:, b : b + 1] * total + d
        gdev_ref[...] = total.astype(bf16)


def middle(y, x, gate, gno, q, cum3, start, bs, skip, gain):
    length = x.shape[0]
    blocks = length // GROUP
    both = lambda p, g: (0, g)
    ph0 = lambda p, g: (0, g * (1 - p) + (TILES - 1) * p)
    ph1 = lambda p, g: (0, g * p)
    whole2 = lambda p, g: (0, 0)
    return pl.pallas_call(
        functools.partial(middle_kernel, blocks),
        grid=(2, TILES),
        in_specs=[
            pl.BlockSpec((length, TILE), ph0),
            pl.BlockSpec((length, TILE), both),
            pl.BlockSpec((length, TILE), both),
            pl.BlockSpec((length, TILE), both),
            pl.BlockSpec((length, STATE), whole2),
            pl.BlockSpec((length, 3 * HEADS), whole2),
            pl.BlockSpec((TILE, STATE), lambda p, g: (g * (1 - p) + (TILES - 1) * p, 0)),
            pl.BlockSpec((blocks, TILE, STATE), lambda p, g: (0, g * (1 - p) + (TILES - 1) * p, 0)),
            pl.BlockSpec((1, TILE), both),
            pl.BlockSpec((1, TILE), both),
        ],
        out_specs=[
            pl.BlockSpec((length, TILE), ph1),
            pl.BlockSpec((length, TILE), ph1),
            pl.BlockSpec((length, TILE), ph1),
            pl.BlockSpec((1, TILE), ph1),
            pl.BlockSpec((1, TILE), ph1),
            pl.BlockSpec((length, LANES), whole2),
            pl.BlockSpec((blocks, TILE, STATE), lambda p, g: (0, g * p, 0)),
            pl.BlockSpec((TILE, STATE), lambda p, g: (g * p, 0)),
        ],
        out_shape=[
            jax.ShapeDtypeStruct((length, INNER), bf16),
            jax.ShapeDtypeStruct((length, INNER), bf16),
            jax.ShapeDtypeStruct((length, INNER), bf16),
            jax.ShapeDtypeStruct((1, INNER), f32),
            jax.ShapeDtypeStruct((1, INNER), f32),
            jax.ShapeDtypeStruct((length, LANES), f32),
            jax.ShapeDtypeStruct((blocks, INNER, STATE), f32),
            jax.ShapeDtypeStruct((INNER, STATE), bf16),
        ],
        scratch_shapes=[
            pltpu.VMEM((length, INNER), f32),
            pltpu.VMEM((length, LANES), f32),
            pltpu.VMEM((length, LANES), f32),
            pltpu.VMEM((length, LANES), f32),
            pltpu.VMEM((length, LANES), f32),
        ],
        compiler_params=params(),
        cost_estimate=pl.CostEstimate(flops=1_200_000_000, bytes_accessed=32_000_000, transcendentals=6_000_000),
        name="middle",
    )(y, x, gate, gno, q, cum3, start, bs, skip, gain)


def intra_back_kernel(
    blocks, w_ref, do_ref, cum3_ref, cum_t_ref, gmat_t_ref, k_ref, q_ref, dw_ref, dq_ref, dk_ref, dg_s
):
    at = pl.program_id(0)
    cum = mm(cum3_ref[...], expander(at))
    r = lax.broadcasted_iota(jnp.int32, (GROUP, GROUP), 0)
    c = lax.broadcasted_iota(jnp.int32, (GROUP, GROUP), 1)
    causal = c >= r
    first = lax.broadcasted_iota(jnp.int32, (GROUP, LANES), 1) < HEAD_DIM
    for b in range(blocks):
        rows = slice(b * GROUP, (b + 1) * GROUP)
        gmat = gmat_t_ref[b]
        dg = None
        for pair in range(HPT // 2):
            lanes = slice(pair * LANES, (pair + 1) * LANES)
            w = w_ref[rows, lanes]
            do = do_ref[rows, lanes]
            outs = []
            for side in range(2):
                j = 2 * pair + side
                col = cum[rows, j * HEAD_DIM : j * HEAD_DIM + 1]
                row = cum_t_ref[pl.ds(HPT * at + j, 1), rows]
                decay = jnp.exp(jnp.where(causal, row - col, -1e30))
                outs.append(mm((decay * gmat).astype(bf16), do))
                own = jnp.where(first if side == 0 else ~first, w, jnp.zeros_like(w))
                term = mm(own, do, NT) * decay
                dg = term if dg is None else dg + term
            dw_ref[rows, lanes] = jnp.where(first, outs[0], outs[1])

        @pl.when(at == 0)
        def _():
            dg_s[b] = dg

        @pl.when(at > 0)
        def _():
            dg_s[b] += dg

    @pl.when(at == TILES - 1)
    def _():
        for b in range(blocks):
            rows = slice(b * GROUP, (b + 1) * GROUP)
            dg = dg_s[b].astype(bf16)
            dk_ref[rows, :] = mm(dg, q_ref[rows, :])
            dq_ref[rows, :] = mm(dg, k_ref[rows, :], TN)


def intra_back(w, do, cum3, cum_t, gmat_t, k, q):
    length = w.shape[0]
    blocks = length // GROUP
    tile = lambda g: (0, g)
    whole2 = lambda g: (0, 0)
    return pl.pallas_call(
        functools.partial(intra_back_kernel, blocks),
        grid=(TILES,),
        in_specs=[
            pl.BlockSpec((length, TILE), tile),
            pl.BlockSpec((length, TILE), tile),
            pl.BlockSpec((length, 3 * HEADS), whole2),
            pl.BlockSpec((HEADS, length), whole2),
            pl.BlockSpec((blocks, GROUP, GROUP), lambda g: (0, 0, 0)),
            pl.BlockSpec((length, STATE), whole2),
            pl.BlockSpec((length, STATE), whole2),
        ],
        out_specs=[
            pl.BlockSpec((length, TILE), tile),
            pl.BlockSpec((length, STATE), whole2),
            pl.BlockSpec((length, STATE), whole2),
        ],
        out_shape=[
            jax.ShapeDtypeStruct((length, INNER), f32),
            jax.ShapeDtypeStruct((length, STATE), f32),
            jax.ShapeDtypeStruct((length, STATE), f32),
        ],
        scratch_shapes=[pltpu.VMEM((blocks, GROUP, GROUP), f32)],
        compiler_params=params(),
        cost_estimate=pl.CostEstimate(flops=4_400_000_000, bytes_accessed=10_000_000, transcendentals=4_200_000),
        name="intra_back",
    )(w, do, cum3, cum_t, gmat_t, k, q)


def back_kernel(
    blocks, p_ref, taps_ref, shift_ref, x_ref, w_ref, do_ref, dwi_ref, skip_ref,
    start_ref, bs_ref, adj_ref, dstart_ref,
    k_ref, q_ref, step3_ref, cum3_ref, dqi_ref, dki_ref, rowsum_ref, raw_ref, sb_ref, rate_ref,
    gp_ref, last_ref, before_ref, dtaps_ref, dshift_ref, draw_ref, dsb_ref, drate_ref,
    dq_s, dk_s, sx_s, sw_s, sv_s, dec_s, d_s,
):
    length = blocks * GROUP
    at = pl.program_id(0)

    @pl.when(at == 0)
    def _():
        dq_s[...] = dqi_ref[...]
        dk_s[...] = dki_ref[...]
        sx_s[...] = jnp.zeros_like(sx_s)
        sw_s[...] = jnp.zeros_like(sw_s)
        sv_s[...] = jnp.zeros_like(sv_s)
        dec_s[...] = jnp.zeros_like(dec_s)
        d_s[0:EDGE, :] = jnp.zeros((EDGE, TILE), f32)
        d_s[length + EDGE :, :] = jnp.zeros((EDGE, TILE), f32)

    def conv_back(dact):
        conv = conv_of(p_ref, taps_ref, shift_ref, length)
        sig = sigmoid(conv)
        dconv = dact * (sig * (1.0 + conv * (1.0 - sig)))
        d_s[EDGE : EDGE + length, :] = dconv
        dshift_ref[...] = jnp.sum(dconv, axis=0, keepdims=True)
        dp = None
        before = None
        for k in range(CONV):
            tap = taps_ref[k : k + 1, :]
            src = p_ref[pl.ds(EDGE - CONV + 1 + k, length), :]
            dtaps_ref[k : k + 1, :] = jnp.sum(dconv * src, axis=0, keepdims=True)
            term = tap * d_s[pl.ds(EDGE + CONV - 1 - k, length), :]
            dp = term if dp is None else dp + term
            edge = tap * d_s[pl.ds(CONV - 1 - k, EDGE), :]
            before = edge if before is None else before + edge
        gp_ref[...] = dp.astype(bf16)
        last_ref[...] = dp[length - EDGE :, :]
        before_ref[...] = before

    @pl.when(at < TILES)
    def _():
        spread = expander(at)
        sel = selector(at)
        cum = mm(cum3_ref[...], spread)
        step = mm(step3_ref[...], spread)
        ends = jnp.exp(mm(spread, lasts(cum3_ref, blocks), ((0,), (1,))))
        x = x_ref[...].astype(f32)
        w = w_ref[...].astype(f32)
        do = do_ref[...].astype(f32)
        scaled_do = (do * jnp.exp(cum)).astype(bf16)
        starts = [start_ref[...]]
        for b in range(blocks - 1):
            starts.append(ends[:, b : b + 1] * starts[b] + bs_ref[b])
        adjs = [None] * blocks
        adj = adj_ref[...]
        for b in reversed(range(blocks)):
            adjs[b] = adj
            adj = ends[:, b : b + 1] * adj + dstart_ref[b]
        dws = []
        for b in range(blocks):
            rows = slice(b * GROUP, (b + 1) * GROUP)
            tails = jnp.exp(cum[(b + 1) * GROUP - 1 : (b + 1) * GROUP, :] - cum[rows])
            ab = adjs[b].astype(bf16)
            dws.append(tails * mm(k_ref[rows, :], ab, NT))
            dk_s[rows, :] += mm((w[rows] * tails).astype(bf16), ab)
            dq_s[rows, :] += mm(scaled_do[rows], starts[b].astype(bf16))
            hi, lo = split2(ends[:, b : b + 1] * adjs[b] * starts[b])
            dec_s[b : b + 1, :] += jnp.sum(mm(hi, sel, TN) + mm(lo, sel, TN), axis=0, keepdims=True)
        dws = jnp.concatenate(dws, axis=0)
        dw = dwi_ref[...] + dws
        sx_s[...] += head_sums(dw * x, sel)
        sw_s[...] += head_sums(dw * w, sel)
        sv_s[...] += head_sums(dws * w, sel)
        conv_back(dw * step + do * skip_ref[0:1, :])

    @pl.when(at == TILES)
    def _():
        conv_back(jnp.concatenate([dk_s[...], dq_s[...]], axis=1))
        dcum = (rowsum_ref[...] - sw_s[...])[:, :HEADS]
        sv = sv_s[...][:, :HEADS]
        z = raw_ref[EDGE:, :HEADS] + sb_ref[0:1, :]
        step = jnp.maximum(z, 0.0) + jnp.log1p(jnp.exp(-jnp.abs(z)))
        rate = rate_ref[0:1, :]
        up = tri(False)
        decays = []
        for b in range(blocks):
            rows = slice(b * GROUP, (b + 1) * GROUP)
            parts = split3(dcum[rows])
            extra = jnp.sum(sv[rows], axis=0, keepdims=True) + dec_s[b : b + 1, :HEADS]
            decays.append(mm(up, parts[0]) + mm(up, parts[1]) + mm(up, parts[2]) + extra)
        ddecay = jnp.concatenate(decays, axis=0)
        dstep = sx_s[...][:, :HEADS] - ddecay * rate
        dz = dstep * sigmoid(z)
        draw_ref[...] = jnp.zeros_like(draw_ref)
        draw_ref[:, :HEADS] = dz.astype(bf16)
        dsb_ref[...] = jnp.sum(dz, axis=0, keepdims=True)
        drate_ref[...] = jnp.sum(-ddecay * step * rate, axis=0, keepdims=True)


def back(p, taps, shift, x, w, do, dwi, skip, start, bs, adj, dstart, k, q, step3, cum3, dqi, dki, rowsum, sb, rate):
    length = x.shape[0]
    blocks = length // GROUP
    tile = lambda g: (0, g)
    xt = lambda g: (0, jnp.minimum(g, TILES - 1))
    st = lambda g: (jnp.minimum(g, TILES - 1), 0)
    st3 = lambda g: (0, jnp.minimum(g, TILES - 1), 0)
    whole2 = lambda g: (0, 0)
    spec = pl.BlockSpec
    return pl.pallas_call(
        functools.partial(back_kernel, blocks),
        grid=(TILES + 1,),
        in_specs=[
            spec((length + EDGE, TILE), tile),
            spec((CONV, TILE), tile),
            spec((1, TILE), tile),
            spec((length, TILE), xt),
            spec((length, TILE), xt),
            spec((length, TILE), xt),
            spec((length, TILE), xt),
            spec((1, TILE), xt),
            spec((TILE, STATE), st),
            spec((blocks, TILE, STATE), st3),
            spec((TILE, STATE), st),
            spec((blocks, TILE, STATE), st3),
            spec((length, STATE), whole2),
            spec((length, STATE), whole2),
            spec((length, 3 * HEADS), whole2),
            spec((length, 3 * HEADS), whole2),
            spec((length, STATE), whole2),
            spec((length, STATE), whole2),
            spec((length, LANES), whole2),
            spec((length + EDGE, LANES), lambda g: (0, CONV_CH // LANES)),
            spec((1, HEADS), whole2),
            spec((1, HEADS), whole2),
        ],
        out_specs=[
            spec((length, TILE), tile),
            spec((EDGE, TILE), tile),
            spec((EDGE, TILE), tile),
            spec((CONV, TILE), tile),
            spec((1, TILE), tile),
            spec((length, LANES), whole2),
            spec((1, HEADS), whole2),
            spec((1, HEADS), whole2),
        ],
        out_shape=[
            jax.ShapeDtypeStruct((length, CONV_CH), bf16),
            jax.ShapeDtypeStruct((EDGE, CONV_CH), f32),
            jax.ShapeDtypeStruct((EDGE, CONV_CH), f32),
            jax.ShapeDtypeStruct((CONV, CONV_CH), f32),
            jax.ShapeDtypeStruct((1, CONV_CH), f32),
            jax.ShapeDtypeStruct((length, LANES), bf16),
            jax.ShapeDtypeStruct((1, HEADS), f32),
            jax.ShapeDtypeStruct((1, HEADS), f32),
        ],
        scratch_shapes=[
            pltpu.VMEM((length, STATE), f32),
            pltpu.VMEM((length, STATE), f32),
            pltpu.VMEM((length, LANES), f32),
            pltpu.VMEM((length, LANES), f32),
            pltpu.VMEM((length, LANES), f32),
            pltpu.VMEM((8, LANES), f32),
            pltpu.VMEM((length + 2 * EDGE, TILE), f32),
        ],
        compiler_params=params(),
        cost_estimate=pl.CostEstimate(flops=2_500_000_000, bytes_accessed=32_000_000, transcendentals=6_000_000),
        name="back",
    )(p, taps, shift, x, w, do, dwi, skip, start, bs, adj, dstart, k, q, step3, cum3, dqi, dki, rowsum, p, sb, rate)


def ring_ok():
    return lax.axis_size("dp") == 8 and lax.axis_size("seq") == 4


def spots():
    dp, seq = lax.axis_index("dp"), lax.axis_index("seq")
    return dp // 2, dp % 2, seq // 2, seq % 2


def over_y(a):
    return lax.ppermute(a, "dp", [(i, i ^ 1) for i in range(8)])


def over_z(a, k):
    return lax.ppermute(a, "dp", [(i, (i + 2 * k) % 8) for i in range(8)])


def over_x(a):
    return lax.ppermute(a, "seq", [(i, i ^ 2) for i in range(4)])


def over_core(a):
    return lax.ppermute(a, "seq", [(i, i ^ 1) for i in range(4)])


def assemble_kernel(rows, parts, own, a3, ay, b3, by, xb3, xby, ca3, cay, cb3, cby, cxb3, cxby, *rest):
    outs, sem = rest[:-1], rest[-1]
    z, y, x, c = spots()
    copies = []

    def put(src, dp, row, size):
        for out, (col, width, factor, base) in zip(outs_of, parts):
            copies.append(
                pltpu.make_async_copy(
                    src.at[:, pl.ds(col, width)],
                    out.at[pl.ds(pl.multiple_of(dp * (rows * factor) + base + row, 16), size), :],
                    sem.at[len(copies)],
                )
            )

    outs_of = [outs[part[4]] for part in parts]
    parts = [part[:4] for part in parts]
    put(own, z * 2 + y, 0, rows)
    half, fourth, eighth = rows // 2, rows // 4, rows // 8
    for k in range(4):
        zz = lax.rem(z + 4 - k, 4)
        for side in range(2):
            if k == 0 and side == 0:
                continue
            yy = y if side == 0 else 1 - y
            dp = zz * 2 + yy
            for core in range(2):
                cc = c if core == 0 else 1 - c
                src = ((a3, ay), (ca3, cay))[core][side]
                put(src.at[k - 1 if side == 0 else k], dp, cc * half, fourth)
                for far in range(2):
                    xx = x if far == 0 else 1 - x
                    src = (((b3, by), (xb3, xby)), ((cb3, cby), (cxb3, cxby)))[core][far][side]
                    put(
                        src.at[k - 1 if side == 0 else k],
                        dp,
                        cc * half + fourth + xx * eighth,
                        eighth,
                    )
    for copy in copies:
        copy.start()
    for copy in copies:
        copy.wait()


def gather_rows(shard, parts, after=None):
    rows, cols = shard.shape
    widths = {}
    for col, width, factor, base, out in parts:
        widths[out] = (width, factor)
    if not ring_ok():
        full = lax.all_gather(shard, "dp")
        outs = []
        for out in sorted(widths):
            pieces = [full[:, :, p[0] : p[0] + p[1]] for p in parts if p[4] == out]
            outs.append(jnp.concatenate(pieces, axis=1).reshape(-1, widths[out][0]))
        return outs, None
    if after is not None:
        shard, after = lax.optimization_barrier((shard, after))
    z, y, x, c = spots()
    half, fourth, eighth = rows // 2, rows // 4, rows // 8
    b0 = lax.dynamic_slice_in_dim(shard, c * half + fourth + x * eighth, eighth, 0)
    a0 = lax.dynamic_slice_in_dim(shard, c * half, fourth, 0)
    bz = [over_z(b0, k) for k in (1, 2, 3)]
    a0, *bz = lax.optimization_barrier((a0, *bz))
    az = [over_z(a0, k) for k in (1, 2, 3)]
    b4 = jnp.stack([b0] + bz)
    b3 = jnp.stack(bz)
    by = over_y(b4)
    xb3 = over_x(b3)
    a4 = jnp.stack([a0] + az)
    a3 = jnp.stack(az)
    ay = over_y(a4)
    xby = over_x(by)
    sent = [a3, ay, b3, by, xb3, xby]
    got = [over_core(a) for a in sent]
    count = len(parts) * (1 + 7 * 6)
    shapes = [
        jax.ShapeDtypeStruct((8 * rows * widths[out][1], widths[out][0]), shard.dtype)
        for out in sorted(widths)
    ]
    anywhere = pl.BlockSpec(memory_space=pl.ANY)
    outs = pl.pallas_call(
        functools.partial(assemble_kernel, rows, parts),
        in_specs=[anywhere] * 13,
        out_specs=[pl.BlockSpec(memory_space=pltpu.VMEM)] * len(shapes),
        out_shape=shapes,
        scratch_shapes=[pltpu.SemaphoreType.DMA((count,))],
        compiler_params=params(),
        cost_estimate=pl.CostEstimate(flops=0, bytes_accessed=32 * rows * cols, transcendentals=0),
        name="assemble",
    )(shard, *sent, *got)
    return outs, by


def weight_grad_kernel(rows, plan, spot_ref, *refs):
    ka_ref, kb_ref, sa_ref, sb_ref, res = refs[-5:]
    y, x, c = spot_ref[1], spot_ref[2], spot_ref[3]
    at = 0
    for lhs, rhs, add, col, folds in plan:
        width = refs[rhs].shape[1]
        product = mm(refs[lhs][...], refs[rhs][...], TN)
        if add is not None:
            product = product + refs[add][...]
        for side in range(2):
            for fold in range(folds):
                top = (side * folds + fold) * rows
                left = col + fold * width
                res[side * rows : (side + 1) * rows, left : left + width] = product[top : top + rows]
    half, fourth, eighth = rows // 2, rows // 4, rows // 8
    for core, (a_ref, b_ref) in enumerate(((ka_ref, kb_ref), (sa_ref, sb_ref))):
        cc = c if core == 0 else 1 - c
        for side in range(2):
            yy = y if side == 0 else 1 - y
            at = yy * rows + cc * half
            a_ref[side, 0] = res[pl.ds(pl.multiple_of(at, fourth), fourth), :].astype(bf16)
            for far in range(2):
                xx = x if far == 0 else 1 - x
                b_ref[far, side, 0] = res[
                    pl.ds(pl.multiple_of(at + fourth + xx * eighth, eighth), eighth), :
                ].astype(bf16)


def weight_grads(rows, cols, arrays, plan):
    z, y, x, c = spots()
    spot = jnp.stack([z, y, x, c]).astype(jnp.int32)
    fourth, eighth = rows // 4, rows // 8
    a_spec = pl.BlockSpec((2, 1, fourth, cols), lambda k, s: (0, k, 0, 0))
    b_spec = pl.BlockSpec((2, 2, 1, eighth, cols), lambda k, s: (0, 0, k, 0, 0))
    a_shape = jax.ShapeDtypeStruct((2, 4, fourth, cols), bf16)
    b_shape = jax.ShapeDtypeStruct((2, 2, 4, eighth, cols), bf16)
    specs = []
    for array, kind in arrays:
        if kind == "lhs":
            specs.append(
                pl.BlockSpec((array.shape[0], array.shape[1] // 4), lambda k, s: (0, lax.rem(s[0] + k, 4)))
            )
        elif kind == "rhs":
            specs.append(pl.BlockSpec(array.shape, lambda k, s: (0, 0)))
        else:
            specs.append(
                pl.BlockSpec((array.shape[0] // 4, array.shape[1]), lambda k, s: (lax.rem(s[0] + k, 4), 0))
            )
    length = arrays[0][0].shape[0]
    return pl.pallas_call(
        functools.partial(weight_grad_kernel, rows, plan),
        grid_spec=pltpu.PrefetchScalarGridSpec(
            num_scalar_prefetch=1,
            grid=(4,),
            in_specs=specs,
            out_specs=[a_spec, b_spec, a_spec, b_spec],
            scratch_shapes=[pltpu.VMEM((2 * rows, cols), f32)],
        ),
        out_shape=[a_shape, b_shape, a_shape, b_shape],
        compiler_params=params(),
        cost_estimate=pl.CostEstimate(
            flops=2 * length * 8 * rows * cols, bytes_accessed=20 * rows * cols, transcendentals=0
        ),
        name="weight_grads",
    )(spot, *[array for array, kind in arrays])


def plus(*terms):
    return sum(term.astype(f32) for term in terms).astype(bf16)


def sum_begin(ka, kb, sa, sb):
    ra, rb = over_core(sa), over_core(sb)
    return (plus(ka[1], ra[1]), plus(kb[1], rb[1])), (ka, kb, ra, rb)


def sum_next(sends, held):
    ka, kb, ra, rb = held
    got_a, got_b = over_y(sends[0]), over_x(sends[1])
    u = [plus(ka[0, k], ra[0, k], got_a[k]) for k in range(4)]
    b_send = plus(kb[0, 1], rb[0, 1], got_b[1])
    return (u, b_send), (kb, rb, got_b)


def sum_third(sends, held):
    u, b_send = sends
    kb, rb, got_b = held
    b_far = over_y(b_send)
    got_u = [over_z(u[k], k) for k in (1, 2, 3)]
    v = [plus(kb[0, 0, k], rb[0, 0, k], got_b[0, k], b_far[k]) for k in range(4)]
    return v, (u[0], got_u)


def sum_end(v, held):
    x, c = spots()[2:]
    eighth, cols = v[0].shape
    fin_a = plus(held[0], *held[1])
    got_v = [over_z(v[k], k) for k in (1, 2, 3)]
    fin_b = plus(v[0], *got_v)
    other_a, other_b = over_x(fin_a), over_x(fin_b)
    b_rows = jnp.where(x == 0, jnp.stack([fin_b, other_b]), jnp.stack([other_b, fin_b]))
    mine = jnp.concatenate([plus(fin_a, other_a), b_rows.reshape(2 * eighth, cols)], axis=0)
    other = over_core(mine)
    both = jnp.where(c == 0, jnp.stack([mine, other]), jnp.stack([other, mine]))
    return both.reshape(8 * eighth, cols).astype(f32)


def plain_sum(lhs, rhs):
    full = lax.dot_general(lhs, rhs, (TN, ((), ())), preferred_element_type=f32)
    part = lax.psum_scatter(full.astype(bf16), "dp", scatter_dimension=0, tiled=True)
    return lax.psum(part, "seq").astype(f32)


def carried(state, decay, mate_decay, axis, reverse):
    size, here = lax.axis_size(axis), lax.axis_index(axis)
    if mate_decay is not None:
        core = here % 2
        own, other = state.astype(f32), over_core(state).astype(f32)
        ahead = (core == 0) if reverse else (core == 1)
        mate_decay = mate_decay.astype(f32)
        pair = jnp.where(ahead, decay.astype(f32) * other + own, mate_decay * own + other).astype(bf16)
        route = [(2, 0), (3, 1)] if reverse else [(0, 2), (1, 3)]
        far = lax.ppermute(pair, axis, route).astype(f32)
        return jnp.where(ahead, other + mate_decay * far, far)
    states = lax.all_gather(state, axis)
    decays = lax.all_gather(decay[:, :1], axis).astype(f32)

    def one(lap, total):
        at = size - 1 - lap if reverse else lap
        use = at > here if reverse else at < here
        new = decays[at] * total + states[at].astype(f32)
        return jnp.where(use, new, total)

    return lax.fori_loop(0, size, one, jnp.zeros(state.shape, f32))


def rms_scale(values, gains):
    return values * lax.rsqrt(jnp.mean(values * values, axis=-1, keepdims=True) + epsilon) * gains


def shards(
    tokens, cotangent, in_weight, out_weight, conv_weight, conv_bias,
    pre_gain, norm_gain, step_bias, decay_log, skip_gain,
):
    dp = lax.axis_size("dp")
    seq = lax.axis_size("seq")
    width = tokens.shape[2]
    pieces = [conv_weight, conv_bias, pre_gain, norm_gain, step_bias, decay_log, skip_gain]
    shapes = [piece.shape for piece in pieces]
    sizes = [piece.size for piece in pieces]
    used = sum(sizes)
    high = in_weight.shape[0]
    lanes = -(-used // high)
    flat = jnp.concatenate([piece.reshape(-1) for piece in pieces] + [jnp.zeros((high * lanes - used,), bf16)])
    shard = jnp.concatenate(
        [
            in_weight[:, INNER:],
            flat.reshape(high, lanes),
            jnp.zeros((high, LANES - HEADS - lanes), bf16),
        ],
        axis=1,
    )
    (conv_full,), mark = gather_rows(shard, [(0, CONV_CH + LANES, 1, 0, 0)])
    out_rows = out_weight.shape[0] // 2
    wide = out_weight.shape[1]
    (gate_full, out_full), mark = gather_rows(
        jnp.concatenate([in_weight[:, :INNER], out_weight[:out_rows], out_weight[out_rows:]], axis=1),
        [(0, INNER, 1, 0, 0), (INNER, wide, 2, 0, 1), (INNER + wide, wide, 2, out_rows, 1)],
        mark,
    )
    small = conv_full[:, CONV_CH + HEADS : CONV_CH + HEADS + lanes].reshape(dp, high * lanes)
    got, at = [], 0
    for shape, size in zip(shapes, sizes):
        got.append(small[:, at : at + size].reshape((dp,) + shape))
        at += size
    taps = jnp.moveaxis(got[0], 0, 1).reshape(CONV, CONV_CH).astype(f32)
    shift, gains_pre, gains_norm, bias_step, log_rates, skip = [
        piece.reshape(-1).astype(f32) for piece in got[1:]
    ]
    shift = shift[None]
    rate = jnp.exp(log_rates)[None]
    bias_step = bias_step[None]
    skip_lanes = jnp.repeat(skip, HEAD_DIM)[None]

    toks = tokens[0]
    length = toks.shape[0]
    edge = lax.ppermute(toks[length - EDGE :], "seq", [(i, i + 1) for i in range(seq - 1)])
    normed_ext = rms_scale(jnp.concatenate([edge, toks], axis=0).astype(f32), gains_pre).astype(bf16)
    normed = normed_ext[EDGE:]
    p = jnp.dot(normed_ext, conv_full, preferred_element_type=f32)
    x, w, bs, dev, k, q, gmat, gmat_t, step3, cum3, cum_t = front(p, taps, shift, bias_step, rate)
    mate_decay = over_core(dev[1]) if ring_ok() else None
    start = carried(dev[0], dev[1], mate_decay, "seq", False)
    y = intra_of(w, cum3, cum_t, gmat)
    gate = jnp.dot(normed, gate_full, preferred_element_type=f32)
    cot = cotangent[0]
    gno = lax.dot_general(cot, out_full, (((1,), (1,)), ((), ())), preferred_element_type=f32)
    no, dgate, do, dgain, dskip, rowsum, dstart, gdev = middle(
        y, x, gate, gno, q, cum3, start, bs, skip_lanes, gains_norm[None]
    )
    adj = carried(gdev, dev[1], mate_decay, "seq", True)
    rows = toks.astype(f32)
    mixed = (rows + jnp.dot(no, out_full, preferred_element_type=f32)).astype(bf16)
    ring = ring_ok()
    if ring:
        early = weight_grads(
            high, INNER + 2 * wide,
            [(normed, "lhs"), (dgate, "rhs"), (no, "lhs"), (cot, "rhs")],
            [(0, 1, None, 0, 1), (2, 3, None, INNER, 2)],
        )
        sends, held = sum_begin(*early)
        (w, sends) = lax.optimization_barrier((w, sends))
        sends, held = sum_next(sends, held)
    dwi, dqi, dki = intra_back(w, do, cum3, cum_t, gmat_t, k, q)
    if ring:
        (dwi, sends) = lax.optimization_barrier((dwi, sends))
        v, held = sum_third(sends, held)
    gp, last, before, dtaps, dshift, draw, dsb, drate = back(
        p, taps, shift, x, w, do, dwi, skip_lanes, start, bs, adj, dstart,
        k, q, step3, cum3, dqi, dki, rowsum, bias_step, rate,
    )
    if ring:
        (gp, v) = lax.optimization_barrier((gp, v))
        early = sum_end(v, held)
        grad_gate = early[:, :INNER]
        grad_out = jnp.concatenate([early[:, INNER : INNER + wide], early[:, INNER + wide :]], axis=0)
    else:
        grad_gate = plain_sum(normed, dgate)
        grad_out = plain_sum(no, cot)
    returned = lax.ppermute(before, "seq", [(i + 1, i) for i in range(seq - 1)])
    gp = gp.at[length - EDGE :].set((last + returned).astype(bf16))
    over_cols = (((1,), (1,)), ((), ()))
    dnormed = (
        lax.dot_general(gp, conv_full[:, :CONV_CH], over_cols, preferred_element_type=f32)
        + lax.dot_general(dgate, gate_full, over_cols, preferred_element_type=f32)
        + lax.dot_general(draw, conv_full[:, CONV_CH:], over_cols, preferred_element_type=f32)
    )
    r = lax.rsqrt(jnp.mean(rows * rows, axis=-1, keepdims=True) + epsilon)
    t = dnormed * gains_pre
    drows = r * t - rows * (r * r * r * jnp.mean(rows * t, axis=-1, keepdims=True))
    grad_tokens = (cot.astype(f32) + drows).astype(bf16)
    dpre = jnp.sum(dnormed * rows * r, axis=0)

    smalls = [
        jnp.moveaxis(dtaps.reshape(CONV, dp, -1), 1, 0).reshape(dp, -1),
        dshift.reshape(dp, -1),
        dpre.reshape(dp, -1),
        dgain.reshape(dp, -1),
        dsb.reshape(dp, -1),
        drate.reshape(dp, -1),
        jnp.sum(dskip.reshape(HEADS, HEAD_DIM), axis=1).reshape(dp, -1),
    ]
    bundle = jnp.concatenate(smalls + [jnp.zeros((dp, high * lanes - used), f32)], axis=1)
    addend = jnp.pad(bundle.reshape(dp * high, lanes), ((0, 0), (HEADS, LANES - HEADS - lanes)))
    if ring:
        late = weight_grads(
            high, CONV_CH + LANES,
            [(normed, "lhs"), (gp, "rhs"), (draw, "rhs"), (addend, "add")],
            [(0, 1, None, 0, 1), (0, 2, 3, CONV_CH, 1)],
        )
        sends, held = sum_begin(*late)
        sends, held = sum_next(sends, held)
        v, held = sum_third(sends, held)
        grad_conv = sum_end(v, held)
    else:
        eye = jnp.eye(dp * high, dtype=bf16)
        grad_conv = jnp.concatenate(
            [plain_sum(normed, gp), plain_sum(normed, draw) + plain_sum(eye, addend.astype(bf16))], axis=1
        )
    mine = grad_conv[:, CONV_CH + HEADS : CONV_CH + HEADS + lanes].reshape(-1)
    outs, at = [], 0
    for shape, size in zip(shapes, sizes):
        outs.append(mine[at : at + size].reshape(shape))
        at += size
    grad_in = jnp.concatenate([grad_gate, grad_conv[:, : CONV_CH + HEADS]], axis=1)
    return (
        mixed[None], grad_tokens[None], grad_in, grad_out, outs[0], outs[1],
        outs[2], outs[3], outs[4], outs[5], outs[6],
    )


def solution(mesh):
    return jax.shard_map(
        shards,
        mesh=mesh,
        in_specs=(
            P("dp", "seq", None), P("dp", "seq", None), P("dp", None), P("dp", None),
            P(None, "dp"), P("dp"), P("dp"), P("dp"), P("dp"), P("dp"), P("dp"),
        ),
        out_specs=(
            P("dp", "seq", None), P("dp", "seq", None), P("dp", None), P("dp", None),
            P(None, "dp"), P("dp"), P("dp"), P("dp"), P("dp"), P("dp"), P("dp"),
        ),
        check_vma=False,
    )
```

```python
import functools

import jax
import jax.numpy as jnp
from jax import lax
from jax.experimental import pallas as pl
from jax.experimental.pallas import tpu as pltpu
from jax.sharding import PartitionSpec as P

HEADS = 32
HEAD_DIM = 64
STATE = 128
CONV = 4
GROUP = 256
INNER = 2048
CONV_CH = 2304
EDGE = 16
TILE = 256
HPT = TILE // HEAD_DIM
TILES = INNER // TILE
LANES = 128

bf16 = jnp.bfloat16
f32 = jnp.float32
epsilon = 1e-05
VMEM_LIMIT = 40 * 1024 * 1024


def params(vmem=VMEM_LIMIT):
    return pltpu.CompilerParams(vmem_limit_bytes=vmem)


def mm(a, b, dims=((1,), (0,))):
    return lax.dot_general(a, b, (dims, ((), ())), preferred_element_type=f32)


NT = ((1,), (1,))
TN = ((0,), (0,))


def split3(v):
    hi = v.astype(bf16)
    rest = v - hi.astype(f32)
    mid = rest.astype(bf16)
    lo = (rest - mid.astype(f32)).astype(bf16)
    return hi, mid, lo


def split2(v):
    hi = v.astype(bf16)
    return hi, (v - hi.astype(f32)).astype(bf16)


def expander(tile):
    head = lax.broadcasted_iota(jnp.int32, (3 * HEADS, TILE), 0) % HEADS
    lane = lax.broadcasted_iota(jnp.int32, (3 * HEADS, TILE), 1)
    return (head == HPT * tile + lane // HEAD_DIM).astype(f32).astype(bf16)


def selector(tile):
    lane = lax.broadcasted_iota(jnp.int32, (TILE, LANES), 0)
    head = lax.broadcasted_iota(jnp.int32, (TILE, LANES), 1)
    return (head == HPT * tile + lane // HEAD_DIM).astype(f32).astype(bf16)


def head_sums(v, sel):
    hi, lo = split2(v)
    return mm(hi, sel) + mm(lo, sel)


def sigmoid(v):
    return 0.5 * jnp.tanh(0.5 * v) + 0.5


def conv_of(p_ref, taps_ref, shift_ref, length):
    out = shift_ref[0:1, :]
    for k in range(CONV):
        out = out + p_ref[pl.ds(EDGE - CONV + 1 + k, length), :] * taps_ref[k : k + 1, :]
    return out


def tri(lower):
    r = lax.broadcasted_iota(jnp.int32, (GROUP, GROUP), 0)
    c = lax.broadcasted_iota(jnp.int32, (GROUP, GROUP), 1)
    return ((r >= c) if lower else (r <= c)).astype(f32).astype(bf16)


def lasts(cum3_ref, blocks):
    return jnp.concatenate(
        [cum3_ref[(b + 1) * GROUP - 1 : (b + 1) * GROUP, :] for b in range(blocks)], axis=0
    )


def front_kernel(
    blocks, p_ref, raw_ref, taps_ref, shift_ref, sb_ref, rate_ref,
    x_ref, w_ref, bs_ref, dev_ref, keys_ref, queries_ref, gmat_ref, gmat_t_ref,
    step3_ref, cum3_ref, cum_t_ref,
):
    length = blocks * GROUP
    at = pl.program_id(0)
    conv = conv_of(p_ref, taps_ref, shift_ref, length)
    act = conv * sigmoid(conv)

    @pl.when(at == 0)
    def _():
        keys = act[:, :STATE].astype(bf16)
        queries = act[:, STATE:].astype(bf16)
        keys_ref[...] = keys
        queries_ref[...] = queries
        z = raw_ref[EDGE:, :HEADS] + sb_ref[0:1, :]
        step = jnp.maximum(z, 0.0) + jnp.log1p(jnp.exp(-jnp.abs(z)))
        decays = -step * rate_ref[0:1, :]
        step3_ref[...] = jnp.concatenate(split3(step), axis=1)
        low = tri(True)
        for b in range(blocks):
            rows = slice(b * GROUP, (b + 1) * GROUP)
            gmat_ref[b] = mm(queries[rows], keys[rows], NT)
            gmat_t_ref[b] = mm(keys[rows], queries[rows], NT)
            parts = split3(decays[rows])
            cum = mm(low, parts[0]) + mm(low, parts[1]) + mm(low, parts[2])
            cum3_ref[rows, :] = jnp.concatenate(split3(cum), axis=1)
            cum_t_ref[:, rows] = sum(
                mm(part, low, ((0,), (1,))) for part in parts
            )

    @pl.when(at > 0)
    def _():
        spread = expander(at - 1)
        step = mm(step3_ref[...], spread)
        cum = mm(cum3_ref[...], spread)
        weighted = act * step
        x_ref[...] = act.astype(bf16)
        w_ref[...] = weighted.astype(bf16)
        ends = mm(spread, lasts(cum3_ref, blocks), ((0,), (1,)))
        total = None
        for b in range(blocks):
            rows = slice(b * GROUP, (b + 1) * GROUP)
            tails = jnp.exp(cum[(b + 1) * GROUP - 1 : (b + 1) * GROUP, :] - cum[rows])
            state = mm((weighted[rows] * tails).astype(bf16), keys_ref[rows, :], TN)
            bs_ref[b] = state
            total = state if total is None else jnp.exp(ends[:, b : b + 1]) * total + state
        dev_ref[0] = total.astype(bf16)
        whole = jnp.exp(sum(ends[:, b : b + 1] for b in range(blocks)))
        dev_ref[1] = jnp.broadcast_to(whole, total.shape).astype(bf16)


def front(p, taps, shift, sb, rate):
    length = p.shape[0] - EDGE
    blocks = length // GROUP
    tile = lambda g: (0, lax.rem(g + TILES, TILES + 1))
    xt = lambda g: (0, jnp.maximum(g - 1, 0))
    whole2 = lambda g: (0, 0)
    whole3 = lambda g: (0, 0, 0)
    return pl.pallas_call(
        functools.partial(front_kernel, blocks),
        grid=(TILES + 1,),
        in_specs=[
            pl.BlockSpec((length + EDGE, TILE), tile),
            pl.BlockSpec((length + EDGE, LANES), lambda g: (0, CONV_CH // LANES)),
            pl.BlockSpec((CONV, TILE), tile),
            pl.BlockSpec((1, TILE), tile),
            pl.BlockSpec((1, HEADS), whole2),
            pl.BlockSpec((1, HEADS), whole2),
        ],
        out_specs=[
            pl.BlockSpec((length, TILE), xt),
            pl.BlockSpec((length, TILE), xt),
            pl.BlockSpec((blocks, TILE, STATE), lambda g: (0, jnp.maximum(g - 1, 0), 0)),
            pl.BlockSpec((2, TILE, STATE), lambda g: (0, jnp.maximum(g - 1, 0), 0)),
            pl.BlockSpec((length, STATE), whole2),
            pl.BlockSpec((length, STATE), whole2),
            pl.BlockSpec((blocks, GROUP, GROUP), whole3),
            pl.BlockSpec((blocks, GROUP, GROUP), whole3),
            pl.BlockSpec((length, 3 * HEADS), whole2),
            pl.BlockSpec((length, 3 * HEADS), whole2),
            pl.BlockSpec((HEADS, length), whole2),
        ],
        out_shape=[
            jax.ShapeDtypeStruct((length, INNER), bf16),
            jax.ShapeDtypeStruct((length, INNER), bf16),
            jax.ShapeDtypeStruct((blocks, INNER, STATE), f32),
            jax.ShapeDtypeStruct((2, INNER, STATE), bf16),
            jax.ShapeDtypeStruct((length, STATE), bf16),
            jax.ShapeDtypeStruct((length, STATE), bf16),
            jax.ShapeDtypeStruct((blocks, GROUP, GROUP), f32),
            jax.ShapeDtypeStruct((blocks, GROUP, GROUP), f32),
            jax.ShapeDtypeStruct((length, 3 * HEADS), bf16),
            jax.ShapeDtypeStruct((length, 3 * HEADS), bf16),
            jax.ShapeDtypeStruct((HEADS, length), f32),
        ],
        compiler_params=params(),
        cost_estimate=pl.CostEstimate(flops=600_000_000, bytes_accessed=14_000_000, transcendentals=4_000_000),
        name="front",
    )(p, p, taps, shift, sb, rate)


def intra_kernel(blocks, w_ref, cum3_ref, cum_t_ref, gmat_ref, y_ref):
    at = pl.program_id(0)
    cum = mm(cum3_ref[...], expander(at))
    r = lax.broadcasted_iota(jnp.int32, (GROUP, GROUP), 0)
    c = lax.broadcasted_iota(jnp.int32, (GROUP, GROUP), 1)
    causal = r >= c
    first = lax.broadcasted_iota(jnp.int32, (GROUP, LANES), 1) < HEAD_DIM
    for b in range(blocks):
        rows = slice(b * GROUP, (b + 1) * GROUP)
        gmat = gmat_ref[b]
        for pair in range(HPT // 2):
            lanes = slice(pair * LANES, (pair + 1) * LANES)
            w = w_ref[rows, lanes]
            outs = []
            for side in range(2):
                j = 2 * pair + side
                col = cum[rows, j * HEAD_DIM : j * HEAD_DIM + 1]
                row = cum_t_ref[pl.ds(HPT * at + j, 1), rows]
                kernel = jnp.exp(jnp.where(causal, col - row, -1e30)) * gmat
                outs.append(mm(kernel.astype(bf16), w))
            y_ref[rows, lanes] = jnp.where(first, outs[0], outs[1])


def intra_of(w, cum3, cum_t, gmat):
    length = w.shape[0]
    blocks = length // GROUP
    tile = lambda g: (0, g)
    whole2 = lambda g: (0, 0)
    return pl.pallas_call(
        functools.partial(intra_kernel, blocks),
        grid=(TILES,),
        in_specs=[
            pl.BlockSpec((length, TILE), tile),
            pl.BlockSpec((length, 3 * HEADS), whole2),
            pl.BlockSpec((HEADS, length), whole2),
            pl.BlockSpec((blocks, GROUP, GROUP), lambda g: (0, 0, 0)),
        ],
        out_specs=pl.BlockSpec((length, TILE), tile),
        out_shape=jax.ShapeDtypeStruct((length, INNER), f32),
        compiler_params=params(),
        cost_estimate=pl.CostEstimate(flops=2_200_000_000, bytes_accessed=7_000_000, transcendentals=4_200_000),
        name="intra",
    )(w, cum3, cum_t, gmat)


def middle_kernel(
    blocks, y_ref, x_ref, gate_ref, gno_ref, q_ref, cum3_ref, start_ref, bs_ref, skip_ref, gain_ref,
    no_ref, dgate_ref, do_ref, dgain_ref, dskip_ref, rowsum_ref, dstart_ref, gdev_ref,
    y_s, sq_s, gt_s, r_s, m_s,
):
    length = blocks * GROUP
    phase, at = pl.program_id(0), pl.program_id(1)
    spread = expander(at)
    cum = mm(cum3_ref[...], spread)
    lanes = pl.ds(pl.multiple_of(at * TILE, TILE), TILE)
    x = x_ref[...].astype(f32)
    gate = gate_ref[...]
    sig = sigmoid(gate)
    gn = gno_ref[...]
    gain = gain_ref[0:1, :]
    skip = skip_ref[0:1, :]
    ends = jnp.exp(mm(spread, lasts(cum3_ref, blocks), ((0,), (1,))))

    @pl.when(phase == 0)
    def _():
        start = start_ref[...]
        for b in range(blocks):
            rows = slice(b * GROUP, (b + 1) * GROUP)
            inter = mm(q_ref[rows, :], start.astype(bf16), NT) * jnp.exp(cum[rows])
            y_s[rows, lanes] = y_ref[rows, :] + inter
            start = ends[:, b : b + 1] * start + bs_ref[b]
        gated = (y_s[:, lanes] + skip * x) * (gate * sig)
        sq = gated * gated
        gt = gated * gn * gain
        sq = sq[:, :LANES] + sq[:, LANES:]
        gt = gt[:, :LANES] + gt[:, LANES:]

        @pl.when(at == 0)
        def _():
            sq_s[...] = sq
            gt_s[...] = gt

        @pl.when(at > 0)
        def _():
            sq_s[...] += sq
            gt_s[...] += gt

    @pl.when(phase == 1)
    def _():
        @pl.when(at == 0)
        def _():
            r = lax.rsqrt(jnp.sum(sq_s[...], axis=1, keepdims=True) / INNER + epsilon)
            m = r * r * r * (jnp.sum(gt_s[...], axis=1, keepdims=True) / INNER)
            r_s[...] = jnp.broadcast_to(r, r_s.shape)
            m_s[...] = jnp.broadcast_to(m, m_s.shape)

        r = r_s[:, 0:1]
        m = m_s[:, 0:1]
        y = y_s[:, lanes]
        ssm = y + skip * x
        silu = gate * sig
        gated = ssm * silu
        scaled = gated * r
        no_ref[...] = (scaled * gain).astype(bf16)
        dgain_ref[...] = jnp.sum(gn * scaled, axis=0, keepdims=True)
        dgated = r * gn * gain - gated * m
        dgate_ref[...] = (dgated * ssm * (sig * (1.0 + gate * (1.0 - sig)))).astype(bf16)
        dof = dgated * silu
        dob = dof.astype(bf16)
        do_ref[...] = dob
        sums = head_sums(dob.astype(f32) * y, selector(at))
        skips = jnp.broadcast_to(jnp.sum(dof * x, axis=0, keepdims=True), (8, TILE))
        skips = head_sums(skips, selector(at))[0:1]

        @pl.when(at == 0)
        def _():
            rowsum_ref[...] = sums
            dskip_ref[...] = skips

        @pl.when(at > 0)
        def _():
            rowsum_ref[...] += sums
            dskip_ref[...] += skips

        scaled_do = (dof * jnp.exp(cum)).astype(bf16)
        total = None
        for b in reversed(range(blocks)):
            rows = slice(b * GROUP, (b + 1) * GROUP)
            d = mm(scaled_do[rows], q_ref[rows, :], TN)
            dstart_ref[b] = d
            total = d if total is None else ends[:, b : b + 1] * total + d
        gdev_ref[...] = total.astype(bf16)


def middle(y, x, gate, gno, q, cum3, start, bs, skip, gain):
    length = x.shape[0]
    blocks = length // GROUP
    both = lambda p, g: (0, g)
    ph0 = lambda p, g: (0, g * (1 - p) + (TILES - 1) * p)
    ph1 = lambda p, g: (0, g * p)
    whole2 = lambda p, g: (0, 0)
    return pl.pallas_call(
        functools.partial(middle_kernel, blocks),
        grid=(2, TILES),
        in_specs=[
            pl.BlockSpec((length, TILE), ph0),
            pl.BlockSpec((length, TILE), both),
            pl.BlockSpec((length, TILE), both),
            pl.BlockSpec((length, TILE), both),
            pl.BlockSpec((length, STATE), whole2),
            pl.BlockSpec((length, 3 * HEADS), whole2),
            pl.BlockSpec((TILE, STATE), lambda p, g: (g * (1 - p) + (TILES - 1) * p, 0)),
            pl.BlockSpec((blocks, TILE, STATE), lambda p, g: (0, g * (1 - p) + (TILES - 1) * p, 0)),
            pl.BlockSpec((1, TILE), both),
            pl.BlockSpec((1, TILE), both),
        ],
        out_specs=[
            pl.BlockSpec((length, TILE), ph1),
            pl.BlockSpec((length, TILE), ph1),
            pl.BlockSpec((length, TILE), ph1),
            pl.BlockSpec((1, TILE), ph1),
            pl.BlockSpec((1, LANES), whole2),
            pl.BlockSpec((length, LANES), whole2),
            pl.BlockSpec((blocks, TILE, STATE), lambda p, g: (0, g * p, 0)),
            pl.BlockSpec((TILE, STATE), lambda p, g: (g * p, 0)),
        ],
        out_shape=[
            jax.ShapeDtypeStruct((length, INNER), bf16),
            jax.ShapeDtypeStruct((length, INNER), bf16),
            jax.ShapeDtypeStruct((length, INNER), bf16),
            jax.ShapeDtypeStruct((1, INNER), f32),
            jax.ShapeDtypeStruct((1, LANES), f32),
            jax.ShapeDtypeStruct((length, LANES), f32),
            jax.ShapeDtypeStruct((blocks, INNER, STATE), f32),
            jax.ShapeDtypeStruct((INNER, STATE), bf16),
        ],
        scratch_shapes=[
            pltpu.VMEM((length, INNER), f32),
            pltpu.VMEM((length, LANES), f32),
            pltpu.VMEM((length, LANES), f32),
            pltpu.VMEM((length, LANES), f32),
            pltpu.VMEM((length, LANES), f32),
        ],
        compiler_params=params(),
        cost_estimate=pl.CostEstimate(flops=1_200_000_000, bytes_accessed=32_000_000, transcendentals=6_000_000),
        name="middle",
    )(y, x, gate, gno, q, cum3, start, bs, skip, gain)


def intra_back_kernel(
    blocks, w_ref, do_ref, cum3_ref, cum_t_ref, gmat_t_ref, k_ref, q_ref, dw_ref, dq_ref, dk_ref, dg_s
):
    at = pl.program_id(0)
    cum = mm(cum3_ref[...], expander(at))
    r = lax.broadcasted_iota(jnp.int32, (GROUP, GROUP), 0)
    c = lax.broadcasted_iota(jnp.int32, (GROUP, GROUP), 1)
    causal = c >= r
    first = lax.broadcasted_iota(jnp.int32, (GROUP, LANES), 1) < HEAD_DIM
    for b in range(blocks):
        rows = slice(b * GROUP, (b + 1) * GROUP)
        gmat = gmat_t_ref[b]
        dg = None
        for pair in range(HPT // 2):
            lanes = slice(pair * LANES, (pair + 1) * LANES)
            w = w_ref[rows, lanes]
            do = do_ref[rows, lanes]
            outs = []
            for side in range(2):
                j = 2 * pair + side
                col = cum[rows, j * HEAD_DIM : j * HEAD_DIM + 1]
                row = cum_t_ref[pl.ds(HPT * at + j, 1), rows]
                decay = jnp.exp(jnp.where(causal, row - col, -1e30))
                outs.append(mm((decay * gmat).astype(bf16), do))
                own = jnp.where(first if side == 0 else ~first, w, jnp.zeros_like(w))
                term = mm(own, do, NT) * decay
                dg = term if dg is None else dg + term
            dw_ref[rows, lanes] = jnp.where(first, outs[0], outs[1])

        @pl.when(at == 0)
        def _():
            dg_s[b] = dg

        @pl.when(at > 0)
        def _():
            dg_s[b] += dg

    @pl.when(at == TILES - 1)
    def _():
        for b in range(blocks):
            rows = slice(b * GROUP, (b + 1) * GROUP)
            dg = dg_s[b].astype(bf16)
            dk_ref[rows, :] = mm(dg, q_ref[rows, :])
            dq_ref[rows, :] = mm(dg, k_ref[rows, :], TN)


def intra_back(w, do, cum3, cum_t, gmat_t, k, q):
    length = w.shape[0]
    blocks = length // GROUP
    tile = lambda g: (0, g)
    whole2 = lambda g: (0, 0)
    return pl.pallas_call(
        functools.partial(intra_back_kernel, blocks),
        grid=(TILES,),
        in_specs=[
            pl.BlockSpec((length, TILE), tile),
            pl.BlockSpec((length, TILE), tile),
            pl.BlockSpec((length, 3 * HEADS), whole2),
            pl.BlockSpec((HEADS, length), whole2),
            pl.BlockSpec((blocks, GROUP, GROUP), lambda g: (0, 0, 0)),
            pl.BlockSpec((length, STATE), whole2),
            pl.BlockSpec((length, STATE), whole2),
        ],
        out_specs=[
            pl.BlockSpec((length, TILE), tile),
            pl.BlockSpec((length, STATE), whole2),
            pl.BlockSpec((length, STATE), whole2),
        ],
        out_shape=[
            jax.ShapeDtypeStruct((length, INNER), f32),
            jax.ShapeDtypeStruct((length, STATE), f32),
            jax.ShapeDtypeStruct((length, STATE), f32),
        ],
        scratch_shapes=[pltpu.VMEM((blocks, GROUP, GROUP), f32)],
        compiler_params=params(),
        cost_estimate=pl.CostEstimate(flops=4_400_000_000, bytes_accessed=10_000_000, transcendentals=4_200_000),
        name="intra_back",
    )(w, do, cum3, cum_t, gmat_t, k, q)


def back_kernel(
    blocks, p_ref, taps_ref, shift_ref, x_ref, w_ref, do_ref, dwi_ref, skip_ref,
    start_ref, bs_ref, adj_ref, dstart_ref,
    k_ref, q_ref, step3_ref, cum3_ref, dqi_ref, dki_ref, rowsum_ref, raw_ref, sb_ref, rate_ref,
    gp_ref, last_ref, before_ref, dtaps_ref, dshift_ref, draw_ref, dsb_ref, drate_ref,
    dq_s, dk_s, sx_s, sw_s, sv_s, dec_s, d_s,
):
    length = blocks * GROUP
    at = pl.program_id(0)

    @pl.when(at == 0)
    def _():
        dq_s[...] = dqi_ref[...]
        dk_s[...] = dki_ref[...]
        sx_s[...] = jnp.zeros_like(sx_s)
        sw_s[...] = jnp.zeros_like(sw_s)
        sv_s[...] = jnp.zeros_like(sv_s)
        dec_s[...] = jnp.zeros_like(dec_s)
        d_s[0:EDGE, :] = jnp.zeros((EDGE, TILE), f32)
        d_s[length + EDGE :, :] = jnp.zeros((EDGE, TILE), f32)

    def conv_back(dact):
        conv = conv_of(p_ref, taps_ref, shift_ref, length)
        sig = sigmoid(conv)
        dconv = dact * (sig * (1.0 + conv * (1.0 - sig)))
        d_s[EDGE : EDGE + length, :] = dconv
        dshift_ref[...] = jnp.sum(dconv, axis=0, keepdims=True)
        dp = None
        before = None
        for k in range(CONV):
            tap = taps_ref[k : k + 1, :]
            src = p_ref[pl.ds(EDGE - CONV + 1 + k, length), :]
            dtaps_ref[k : k + 1, :] = jnp.sum(dconv * src, axis=0, keepdims=True)
            term = tap * d_s[pl.ds(EDGE + CONV - 1 - k, length), :]
            dp = term if dp is None else dp + term
            edge = tap * d_s[pl.ds(CONV - 1 - k, EDGE), :]
            before = edge if before is None else before + edge
        gp_ref[...] = dp.astype(bf16)
        last_ref[...] = dp[length - EDGE :, :]
        before_ref[...] = before

    @pl.when(at < TILES)
    def _():
        spread = expander(at)
        sel = selector(at)
        cum = mm(cum3_ref[...], spread)
        step = mm(step3_ref[...], spread)
        ends = jnp.exp(mm(spread, lasts(cum3_ref, blocks), ((0,), (1,))))
        x = x_ref[...].astype(f32)
        w = w_ref[...].astype(f32)
        do = do_ref[...].astype(f32)
        scaled_do = (do * jnp.exp(cum)).astype(bf16)
        starts = [start_ref[...]]
        for b in range(blocks - 1):
            starts.append(ends[:, b : b + 1] * starts[b] + bs_ref[b])
        adjs = [None] * blocks
        adj = adj_ref[...]
        for b in reversed(range(blocks)):
            adjs[b] = adj
            adj = ends[:, b : b + 1] * adj + dstart_ref[b]
        dws = []
        for b in range(blocks):
            rows = slice(b * GROUP, (b + 1) * GROUP)
            tails = jnp.exp(cum[(b + 1) * GROUP - 1 : (b + 1) * GROUP, :] - cum[rows])
            ab = adjs[b].astype(bf16)
            dws.append(tails * mm(k_ref[rows, :], ab, NT))
            dk_s[rows, :] += mm((w[rows] * tails).astype(bf16), ab)
            dq_s[rows, :] += mm(scaled_do[rows], starts[b].astype(bf16))
            hi, lo = split2(ends[:, b : b + 1] * adjs[b] * starts[b])
            dec_s[b : b + 1, :] += jnp.sum(mm(hi, sel, TN) + mm(lo, sel, TN), axis=0, keepdims=True)
        dws = jnp.concatenate(dws, axis=0)
        dw = dwi_ref[...] + dws
        sx_s[...] += head_sums(dw * x, sel)
        sw_s[...] += head_sums(dw * w, sel)
        sv_s[...] += head_sums(dws * w, sel)
        conv_back(dw * step + do * skip_ref[0:1, :])

    @pl.when(at == TILES)
    def _():
        conv_back(jnp.concatenate([dk_s[...], dq_s[...]], axis=1))
        dcum = (rowsum_ref[...] - sw_s[...])[:, :HEADS]
        sv = sv_s[...][:, :HEADS]
        z = raw_ref[EDGE:, :HEADS] + sb_ref[0:1, :]
        step = jnp.maximum(z, 0.0) + jnp.log1p(jnp.exp(-jnp.abs(z)))
        rate = rate_ref[0:1, :]
        up = tri(False)
        decays = []
        for b in range(blocks):
            rows = slice(b * GROUP, (b + 1) * GROUP)
            parts = split3(dcum[rows])
            extra = jnp.sum(sv[rows], axis=0, keepdims=True) + dec_s[b : b + 1, :HEADS]
            decays.append(mm(up, parts[0]) + mm(up, parts[1]) + mm(up, parts[2]) + extra)
        ddecay = jnp.concatenate(decays, axis=0)
        dstep = sx_s[...][:, :HEADS] - ddecay * rate
        dz = dstep * sigmoid(z)
        draw_ref[...] = jnp.zeros_like(draw_ref)
        draw_ref[:, :HEADS] = dz.astype(bf16)
        dsb_ref[...] = jnp.sum(dz, axis=0, keepdims=True)
        drate_ref[...] = jnp.sum(-ddecay * step * rate, axis=0, keepdims=True)


def back(p, taps, shift, x, w, do, dwi, skip, start, bs, adj, dstart, k, q, step3, cum3, dqi, dki, rowsum, sb, rate):
    length = x.shape[0]
    blocks = length // GROUP
    tile = lambda g: (0, g)
    xt = lambda g: (0, jnp.minimum(g, TILES - 1))
    st = lambda g: (jnp.minimum(g, TILES - 1), 0)
    st3 = lambda g: (0, jnp.minimum(g, TILES - 1), 0)
    whole2 = lambda g: (0, 0)
    spec = pl.BlockSpec
    return pl.pallas_call(
        functools.partial(back_kernel, blocks),
        grid=(TILES + 1,),
        in_specs=[
            spec((length + EDGE, TILE), tile),
            spec((CONV, TILE), tile),
            spec((1, TILE), tile),
            spec((length, TILE), xt),
            spec((length, TILE), xt),
            spec((length, TILE), xt),
            spec((length, TILE), xt),
            spec((1, TILE), xt),
            spec((TILE, STATE), st),
            spec((blocks, TILE, STATE), st3),
            spec((TILE, STATE), st),
            spec((blocks, TILE, STATE), st3),
            spec((length, STATE), whole2),
            spec((length, STATE), whole2),
            spec((length, 3 * HEADS), whole2),
            spec((length, 3 * HEADS), whole2),
            spec((length, STATE), whole2),
            spec((length, STATE), whole2),
            spec((length, LANES), whole2),
            spec((length + EDGE, LANES), lambda g: (0, CONV_CH // LANES)),
            spec((1, HEADS), whole2),
            spec((1, HEADS), whole2),
        ],
        out_specs=[
            spec((length, TILE), tile),
            spec((EDGE, TILE), tile),
            spec((EDGE, TILE), tile),
            spec((CONV, TILE), tile),
            spec((1, TILE), tile),
            spec((length, LANES), whole2),
            spec((1, HEADS), whole2),
            spec((1, HEADS), whole2),
        ],
        out_shape=[
            jax.ShapeDtypeStruct((length, CONV_CH), bf16),
            jax.ShapeDtypeStruct((EDGE, CONV_CH), f32),
            jax.ShapeDtypeStruct((EDGE, CONV_CH), f32),
            jax.ShapeDtypeStruct((CONV, CONV_CH), f32),
            jax.ShapeDtypeStruct((1, CONV_CH), f32),
            jax.ShapeDtypeStruct((length, LANES), bf16),
            jax.ShapeDtypeStruct((1, HEADS), f32),
            jax.ShapeDtypeStruct((1, HEADS), f32),
        ],
        scratch_shapes=[
            pltpu.VMEM((length, STATE), f32),
            pltpu.VMEM((length, STATE), f32),
            pltpu.VMEM((length, LANES), f32),
            pltpu.VMEM((length, LANES), f32),
            pltpu.VMEM((length, LANES), f32),
            pltpu.VMEM((8, LANES), f32),
            pltpu.VMEM((length + 2 * EDGE, TILE), f32),
        ],
        compiler_params=params(),
        cost_estimate=pl.CostEstimate(flops=2_500_000_000, bytes_accessed=32_000_000, transcendentals=6_000_000),
        name="back",
    )(p, taps, shift, x, w, do, dwi, skip, start, bs, adj, dstart, k, q, step3, cum3, dqi, dki, rowsum, p, sb, rate)


def ring_ok():
    return lax.axis_size("dp") == 8 and lax.axis_size("seq") == 4


def spots():
    dp, seq = lax.axis_index("dp"), lax.axis_index("seq")
    return dp // 2, dp % 2, seq // 2, seq % 2


def over_y(a):
    return lax.ppermute(a, "dp", [(i, i ^ 1) for i in range(8)])


def over_z(a, k):
    return lax.ppermute(a, "dp", [(i, (i + 2 * k) % 8) for i in range(8)])


def over_x(a):
    return lax.ppermute(a, "seq", [(i, i ^ 2) for i in range(4)])


def over_core(a):
    return lax.ppermute(a, "seq", [(i, i ^ 1) for i in range(4)])


def assemble_kernel(rows, parts, own, a3, ay, b3, by, xb3, xby, ca3, cay, cb3, cby, cxb3, cxby, *rest):
    outs, sem = rest[:-1], rest[-1]
    z, y, x, c = spots()
    copies = []

    def put(src, dp, row, size):
        for out, (col, width, factor, base) in zip(outs_of, parts):
            copies.append(
                pltpu.make_async_copy(
                    src.at[:, pl.ds(col, width)],
                    out.at[pl.ds(pl.multiple_of(dp * (rows * factor) + base + row, 16), size), :],
                    sem.at[len(copies)],
                )
            )

    outs_of = [outs[part[4]] for part in parts]
    parts = [part[:4] for part in parts]
    put(own, z * 2 + y, 0, rows)
    half, fourth, eighth = rows // 2, rows // 4, rows // 8
    for k in range(4):
        zz = lax.rem(z + 4 - k, 4)
        for side in range(2):
            if k == 0 and side == 0:
                continue
            yy = y if side == 0 else 1 - y
            dp = zz * 2 + yy
            for core in range(2):
                cc = c if core == 0 else 1 - c
                src = ((a3, ay), (ca3, cay))[core][side]
                put(src.at[k - 1 if side == 0 else k], dp, cc * half, fourth)
                for far in range(2):
                    xx = x if far == 0 else 1 - x
                    src = (((b3, by), (xb3, xby)), ((cb3, cby), (cxb3, cxby)))[core][far][side]
                    put(
                        src.at[k - 1 if side == 0 else k],
                        dp,
                        cc * half + fourth + xx * eighth,
                        eighth,
                    )
    for copy in copies:
        copy.start()
    for copy in copies:
        copy.wait()


def gather_plain(pieces, parts):
    full = lax.all_gather(jnp.concatenate(pieces, axis=1), "dp")
    outs = []
    for out in sorted({part[4] for part in parts}):
        chosen = [full[:, :, p[0] : p[0] + p[1]] for p in parts if p[4] == out]
        outs.append(jnp.concatenate(chosen, axis=1).reshape(-1, chosen[0].shape[2]))
    return outs


def cut(pieces, start, size):
    return jnp.concatenate([lax.dynamic_slice_in_dim(p, start, size, 0) for p in pieces], axis=1)


def along_z(pieces, fourth_part):
    rows = pieces[0].shape[0]
    z, y, x, c = spots()
    if fourth_part:
        own = cut(pieces, c * (rows // 2), rows // 4)
    else:
        own = cut(pieces, c * (rows // 2) + rows // 4 + x * (rows // 8), rows // 8)
    return own, [over_z(own, k) for k in (1, 2, 3)]


def gather_end(pieces, parts, a3, ay, b3, by, xb3, xby):
    rows = pieces[0].shape[0]
    shard = jnp.concatenate(pieces, axis=1)
    sent = [a3, ay, b3, by, xb3, xby]
    got = [over_core(a) for a in sent]
    widths = {part[4]: part[1:3] for part in parts}
    shapes = [
        jax.ShapeDtypeStruct((8 * rows * widths[out][1], widths[out][0]), shard.dtype)
        for out in sorted(widths)
    ]
    anywhere = pl.BlockSpec(memory_space=pl.ANY)
    return pl.pallas_call(
        functools.partial(assemble_kernel, rows, parts),
        in_specs=[anywhere] * 13,
        out_specs=[pl.BlockSpec(memory_space=pltpu.VMEM)] * len(shapes),
        out_shape=shapes,
        scratch_shapes=[pltpu.SemaphoreType.DMA((len(parts) * (1 + 7 * 6),))],
        compiler_params=params(),
        cost_estimate=pl.CostEstimate(flops=0, bytes_accessed=32 * shard.size, transcendentals=0),
        name="assemble",
    )(shard, *sent, *got)


SIDE = LANES - HEADS


def side_plan():
    plan = []
    for k in range(CONV):
        plan += [("taps", k, SIDE * j, SIDE, 3 * k + j) for j in range(3)]
    plan += [("shift", 0, SIDE * j, SIDE, 12 + j) for j in range(3)]
    plan += [("pre", 0, 0, SIDE, 15), ("pre", 0, SIDE, 32, 16)]
    plan += [("norm", 0, 0, SIDE, 17), ("norm", 0, SIDE, SIDE, 18), ("norm", 0, 2 * SIDE, 64, 19)]
    plan += [(name, 0, 0, 4, 20 + j) for j, name in enumerate(("bias", "rate", "skip"))]
    return plan


SIDE_WIDTH = {"taps": 288, "shift": 288, "pre": 128, "norm": 256, "bias": 4, "rate": 4, "skip": 4}


def pack_kernel(shards_in, names, left, *refs):
    out = refs[-1]
    out[...] = jnp.zeros_like(out)
    values = {name: ref[...].astype(f32) for name, ref in zip(names, refs)}
    for i in range(shards_in):
        for name, k, col, width, row in side_plan():
            if name in values:
                start = i * SIDE_WIDTH[name] + col
                out[i * 128 + row : i * 128 + row + 1, left : left + width] = values[name][
                    k : k + 1, start : start + width
                ]


def pack(shards_in, left, named):
    names = tuple(named)
    return pl.pallas_call(
        functools.partial(pack_kernel, shards_in, names, left),
        out_shape=jax.ShapeDtypeStruct((shards_in * 128, left + SIDE), f32),
        name="pack",
    )(*named.values())


def unpack_kernel(shards_in, names, in_ref, *refs):
    outs = dict(zip(names, refs))
    block = in_ref[...].astype(f32)
    for i in range(shards_in):
        for name, k, col, width, row in side_plan():
            start = i * SIDE_WIDTH[name] + col
            outs[name][k : k + 1, start : start + width] = block[
                i * 128 + row : i * 128 + row + 1, HEADS : HEADS + width
            ]
    if "lanes" in outs:
        outs["rate"][...] = jnp.exp(outs["rate"][...])
        three = jnp.concatenate(split3(jnp.broadcast_to(outs["skip"][...], (8, HEADS))), axis=1)
        for tile in range(TILES):
            outs["lanes"][:, tile * TILE : (tile + 1) * TILE] = mm(three, expander(tile))[0:1]


def unpack(shards_in, full, names):
    shapes = []
    for name in names:
        width = INNER if name == "lanes" else shards_in * SIDE_WIDTH[name]
        shapes.append(jax.ShapeDtypeStruct((CONV if name == "taps" else 1, width), f32))
    whole = [pl.BlockSpec(shape.shape, lambda g: (0, 0)) for shape in shapes]
    return pl.pallas_call(
        functools.partial(unpack_kernel, shards_in, names),
        grid=(1,),
        in_specs=[pl.BlockSpec((shards_in * 128, LANES), lambda g: (0, CONV_CH // LANES))],
        out_specs=whole,
        out_shape=shapes,
        name="unpack",
    )(full)


def weight_grad_kernel(rows, plan, spot_ref, *refs):
    ka_ref, kb_ref, sa_ref, sb_ref, res = refs[-5:]
    y, x, c = spot_ref[1], spot_ref[2], spot_ref[3]
    at = 0
    for lhs, rhs, add, col, folds in plan:
        width = refs[rhs].shape[1]
        product = mm(refs[lhs][...], refs[rhs][...], TN)
        if add is not None:
            product = product + refs[add][...]
        for side in range(2):
            for fold in range(folds):
                top = (side * folds + fold) * rows
                left = col + fold * width
                res[side * rows : (side + 1) * rows, left : left + width] = product[top : top + rows]
    half, fourth, eighth = rows // 2, rows // 4, rows // 8
    for core, (a_ref, b_ref) in enumerate(((ka_ref, kb_ref), (sa_ref, sb_ref))):
        cc = c if core == 0 else 1 - c
        for side in range(2):
            yy = y if side == 0 else 1 - y
            at = yy * rows + cc * half
            a_ref[side, 0] = res[pl.ds(pl.multiple_of(at, fourth), fourth), :].astype(bf16)
            for far in range(2):
                xx = x if far == 0 else 1 - x
                b_ref[far, side, 0] = res[
                    pl.ds(pl.multiple_of(at + fourth + xx * eighth, eighth), eighth), :
                ].astype(bf16)


def weight_grads(rows, cols, arrays, plan):
    z, y, x, c = spots()
    spot = jnp.stack([z, y, x, c]).astype(jnp.int32)
    fourth, eighth = rows // 4, rows // 8
    a_spec = pl.BlockSpec((2, 1, fourth, cols), lambda k, s: (0, k, 0, 0))
    b_spec = pl.BlockSpec((2, 2, 1, eighth, cols), lambda k, s: (0, 0, k, 0, 0))
    a_shape = jax.ShapeDtypeStruct((2, 4, fourth, cols), bf16)
    b_shape = jax.ShapeDtypeStruct((2, 2, 4, eighth, cols), bf16)
    specs = []
    for array, kind in arrays:
        if kind == "lhs":
            specs.append(
                pl.BlockSpec((array.shape[0], array.shape[1] // 4), lambda k, s: (0, lax.rem(s[0] + k, 4)))
            )
        elif kind == "rhs":
            specs.append(pl.BlockSpec(array.shape, lambda k, s: (0, 0)))
        else:
            specs.append(
                pl.BlockSpec((array.shape[0] // 4, array.shape[1]), lambda k, s: (lax.rem(s[0] + k, 4), 0))
            )
    length = arrays[0][0].shape[0]
    return pl.pallas_call(
        functools.partial(weight_grad_kernel, rows, plan),
        grid_spec=pltpu.PrefetchScalarGridSpec(
            num_scalar_prefetch=1,
            grid=(4,),
            in_specs=specs,
            out_specs=[a_spec, b_spec, a_spec, b_spec],
            scratch_shapes=[pltpu.VMEM((2 * rows, cols), f32)],
        ),
        out_shape=[a_shape, b_shape, a_shape, b_shape],
        compiler_params=params(),
        cost_estimate=pl.CostEstimate(
            flops=2 * length * 8 * rows * cols, bytes_accessed=20 * rows * cols, transcendentals=0
        ),
        name="weight_grads",
    )(spot, *[array for array, kind in arrays])


def plus(*terms):
    return sum(term.astype(f32) for term in terms).astype(bf16)


def sum_begin(ka, kb, sa, sb):
    ra, rb = over_core(sa), over_core(sb)
    return (plus(ka[1], ra[1]), plus(kb[1], rb[1])), (ka, kb, ra, rb)


def sum_next(got, held):
    ka, kb, ra, rb = held
    got_a, got_b = got
    u = [plus(ka[0, k], ra[0, k], got_a[k]) for k in range(4)]
    b_send = plus(kb[0, 1], rb[0, 1], got_b[1])
    return (u, b_send), (kb, rb, got_b)


def sum_third(sends):
    u, b_send = sends
    return over_y(b_send), u[0], [over_z(u[k], k) for k in (1, 2, 3)]


def sum_fourth(got, held):
    b_far, own, got_u = got
    kb, rb, got_b = held
    v = [plus(kb[0, 0, k], rb[0, 0, k], got_b[0, k], b_far[k]) for k in range(4)]
    fin_a = plus(own, *got_u)
    return fin_a, over_x(fin_a), v[0], [over_z(v[k], k) for k in (1, 2, 3)]


def sum_end(got):
    fin_a, other_a, v, got_v = got
    x, c = spots()[2:]
    eighth, cols = v.shape
    fin_b = plus(v, *got_v)
    other_b = over_x(fin_b)
    b_rows = jnp.where(x == 0, jnp.stack([fin_b, other_b]), jnp.stack([other_b, fin_b]))
    mine = jnp.concatenate([plus(fin_a, other_a), b_rows.reshape(2 * eighth, cols)], axis=0)
    other = over_core(mine)
    both = jnp.where(c == 0, jnp.stack([mine, other]), jnp.stack([other, mine]))
    return both.reshape(8 * eighth, cols).astype(f32)


def plain_sum(lhs, rhs):
    full = lax.dot_general(lhs, rhs, (TN, ((), ())), preferred_element_type=f32)
    part = lax.psum_scatter(full.astype(bf16), "dp", scatter_dimension=0, tiled=True)
    return lax.psum(part, "seq").astype(f32)


def carried(state, decay, mate_decay, axis, reverse):
    size, here = lax.axis_size(axis), lax.axis_index(axis)
    if mate_decay is not None:
        core = here % 2
        own, other = state.astype(f32), over_core(state).astype(f32)
        ahead = (core == 0) if reverse else (core == 1)
        mate_decay = mate_decay.astype(f32)
        pair = jnp.where(ahead, decay.astype(f32) * other + own, mate_decay * own + other).astype(bf16)
        route = [(2, 0), (3, 1)] if reverse else [(0, 2), (1, 3)]
        far = lax.ppermute(pair, axis, route).astype(f32)
        return jnp.where(ahead, other + mate_decay * far, far)
    states = lax.all_gather(state, axis)
    decays = lax.all_gather(decay[:, :1], axis).astype(f32)

    def one(lap, total):
        at = size - 1 - lap if reverse else lap
        use = at > here if reverse else at < here
        new = decays[at] * total + states[at].astype(f32)
        return jnp.where(use, new, total)

    return lax.fori_loop(0, size, one, jnp.zeros(state.shape, f32))


def rms_scale(values, gains):
    return values * lax.rsqrt(jnp.mean(values * values, axis=-1, keepdims=True) + epsilon) * gains


def shards(
    tokens, cotangent, in_weight, out_weight, conv_weight, conv_bias,
    pre_gain, norm_gain, step_bias, decay_log, skip_gain,
):
    dp = lax.axis_size("dp")
    seq = lax.axis_size("seq")
    ring = ring_ok()
    high = in_weight.shape[0]
    out_rows = out_weight.shape[0] // 2
    wide = out_weight.shape[1]
    first_parts = [(0, CONV_CH + LANES, 1, 0, 0)]
    then = [in_weight[:, :INNER], out_weight[:out_rows], out_weight[out_rows:]]
    then_parts = [(0, INNER, 1, 0, 0), (INNER, wide, 2, 0, 1), (INNER + wide, wide, 2, out_rows, 1)]
    if ring:
        named = {
            "taps": conv_weight, "shift": conv_bias[None], "pre": pre_gain[None], "norm": norm_gain[None],
            "bias": step_bias[None], "rate": decay_log[None], "skip": skip_gain[None],
        }
        first = [in_weight[:, INNER:], pack(1, 0, named).astype(bf16)]
        b0, bz = along_z(first, False)
        held = lax.optimization_barrier((*first, *bz))
        a0, az = along_z(held[:2], True)
        bz = list(held[2:])
        b3 = jnp.stack(bz)
        xb3 = over_x(b3)
        by = over_y(jnp.stack([b0] + bz))
        late_b = lax.optimization_barrier((*then, *az))
        az = list(late_b[3:])
        b0_2, bz_2 = along_z(late_b[:3], False)
        a3 = jnp.stack(az)
        ay = over_y(jnp.stack([a0] + az))
        late_a = lax.optimization_barrier((*then, by))
        by = late_a[3]
        a0_2, az_2 = along_z(late_a[:3], True)
        xby = over_x(by)
        ay, bz_2 = lax.optimization_barrier((ay, bz_2))
        (conv_full,) = gather_end(first, first_parts, a3, ay, b3, by, xb3, xby)
        b3_2 = jnp.stack(bz_2)
        xb3_2 = over_x(b3_2)
        by_2 = over_y(jnp.stack([b0_2] + bz_2))
        conv_full, az_2 = lax.optimization_barrier((conv_full, az_2))
        a3_2 = jnp.stack(az_2)
        ay_2 = over_y(jnp.stack([a0_2] + az_2))
        names = ("taps", "shift", "pre", "norm", "bias", "rate", "skip", "lanes")
        taps, shift, gains_pre, gains_norm, bias_step, rate, _, skip_lanes = unpack(8, conv_full, names)
    else:
        pieces = [conv_weight, conv_bias, pre_gain, norm_gain, step_bias, decay_log, skip_gain]
        shapes = [piece.shape for piece in pieces]
        sizes = [piece.size for piece in pieces]
        used = sum(sizes)
        lanes = -(-used // high)
        flat = jnp.concatenate(
            [piece.reshape(-1) for piece in pieces] + [jnp.zeros((high * lanes - used,), bf16)]
        )
        first = [
            in_weight[:, INNER:],
            flat.reshape(high, lanes),
            jnp.zeros((high, LANES - HEADS - lanes), bf16),
        ]
        (conv_full,) = gather_plain(first, first_parts)
        gate_full, out_full = gather_plain(then, then_parts)
        small = conv_full[:, CONV_CH + HEADS : CONV_CH + HEADS + lanes].reshape(dp, high * lanes)
        got, at = [], 0
        for shape, size in zip(shapes, sizes):
            got.append(small[:, at : at + size].reshape((dp,) + shape))
            at += size
        taps = jnp.moveaxis(got[0], 0, 1).reshape(CONV, CONV_CH).astype(f32)
        shift, gains_pre, gains_norm, bias_step, log_rates, skip = [
            piece.reshape(1, -1).astype(f32) for piece in got[1:]
        ]
        rate = jnp.exp(log_rates)
        skip_lanes = jnp.repeat(skip[0], HEAD_DIM)[None]

    toks = tokens[0]
    length = toks.shape[0]
    edge = lax.ppermute(toks[length - EDGE :], "seq", [(i, i + 1) for i in range(seq - 1)])
    normed_ext = rms_scale(jnp.concatenate([edge, toks], axis=0).astype(f32), gains_pre).astype(bf16)
    normed = normed_ext[EDGE:]
    p = jnp.dot(normed_ext, conv_full, preferred_element_type=f32)
    if ring:
        p, by_2 = lax.optimization_barrier((p, by_2))
        xby_2 = over_x(by_2)
    fronts = front(p, taps, shift, bias_step, rate)
    if ring:
        fronts, ay_2, xb3_2, xby_2 = lax.optimization_barrier((fronts, ay_2, xb3_2, xby_2))
    x, w, bs, dev, k, q, gmat, gmat_t, step3, cum3, cum_t = fronts
    mate_decay = over_core(dev[1]) if ring else None
    start = carried(dev[0], dev[1], mate_decay, "seq", False)
    y = intra_of(w, cum3, cum_t, gmat)
    if ring:
        gate_full, out_full = gather_end(then, then_parts, a3_2, ay_2, b3_2, by_2, xb3_2, xby_2)
    gate = jnp.dot(normed, gate_full, preferred_element_type=f32)
    cot = cotangent[0]
    gno = lax.dot_general(cot, out_full, (((1,), (1,)), ((), ())), preferred_element_type=f32)
    no, dgate, do, dgain, dskip, rowsum, dstart, gdev = middle(
        y, x, gate, gno, q, cum3, start, bs, skip_lanes, gains_norm
    )
    adj = carried(gdev, dev[1], mate_decay, "seq", True)
    rows = toks.astype(f32)
    mixed = (rows + jnp.dot(no, out_full, preferred_element_type=f32)).astype(bf16)
    if ring:
        early = weight_grads(
            high, INNER + 2 * wide,
            [(normed, "lhs"), (dgate, "rhs"), (no, "lhs"), (cot, "rhs")],
            [(0, 1, None, 0, 1), (2, 3, None, INNER, 2)],
        )
        sends, held = sum_begin(*early)
        (w, sends) = lax.optimization_barrier((w, sends))
        got = over_y(sends[0]), over_x(sends[1])
    inside = intra_back(w, do, cum3, cum_t, gmat_t, k, q)
    if ring:
        (inside, got) = lax.optimization_barrier((inside, got))
        sends, held = sum_next(got, held)
        (inside, sends) = lax.optimization_barrier((inside, sends))
        got = sum_third(sends)
    dwi, dqi, dki = inside
    backs = back(
        p, taps, shift, x, w, do, dwi, skip_lanes, start, bs, adj, dstart,
        k, q, step3, cum3, dqi, dki, rowsum, bias_step, rate,
    )
    if ring:
        (backs, got) = lax.optimization_barrier((backs, got))
        got = sum_fourth(got, held)
    gp, last, before, dtaps, dshift, draw, dsb, drate = backs
    returned = lax.ppermute(before, "seq", [(i + 1, i) for i in range(seq - 1)])
    gp = gp.at[length - EDGE :].set((last + returned).astype(bf16))
    over_cols = (((1,), (1,)), ((), ()))
    if ring:
        named = {"taps": dtaps, "shift": dshift, "norm": dgain, "bias": dsb, "rate": drate, "skip": dskip}
        late = weight_grads(
            high, CONV_CH + LANES,
            [(normed, "lhs"), (gp, "rhs"), (draw, "rhs"), (pack(8, HEADS, named), "add")],
            [(0, 1, None, 0, 1), (0, 2, 3, CONV_CH, 1)],
        )
        late, got, gp, dgate, draw = lax.optimization_barrier((late, got, gp, dgate, draw))
        sends, late_held = sum_begin(*late)
        sends, gp, dgate, draw = lax.optimization_barrier((sends, gp, dgate, draw))
        late_got = over_y(sends[0]), over_x(sends[1])
    dnormed = (
        lax.dot_general(gp, conv_full[:, :CONV_CH], over_cols, preferred_element_type=f32)
        + lax.dot_general(dgate, gate_full, over_cols, preferred_element_type=f32)
        + lax.dot_general(draw, conv_full[:, CONV_CH:], over_cols, preferred_element_type=f32)
    )
    r = lax.rsqrt(jnp.mean(rows * rows, axis=-1, keepdims=True) + epsilon)
    t = dnormed * gains_pre
    drows = r * t - rows * (r * r * r * jnp.mean(rows * t, axis=-1, keepdims=True))
    grad_tokens = (cot.astype(f32) + drows).astype(bf16)
    dpre = jnp.sum(dnormed * rows * r, axis=0)
    if ring:
        (late_got, dpre, grad_tokens) = lax.optimization_barrier((late_got, dpre, grad_tokens))
        sends, late_held = sum_next(late_got, late_held)
        late_got = sum_third(sends)
        early = sum_end(got)
        grad_gate = early[:, :INNER]
        grad_out = jnp.concatenate([early[:, INNER : INNER + wide], early[:, INNER + wide :]], axis=0)
        grad_conv = sum_end(sum_fourth(late_got, late_held))
        total = dpre.reshape(dp, high)
        total = total + over_core(total)
        total = total + over_x(total)
        total = total + over_y(total)
        total = total + over_z(total, 1) + over_z(total, 2) + over_z(total, 3)
        dpre = lax.dynamic_index_in_dim(total, lax.axis_index("dp"), 0, False)
        names = ("taps", "shift", "pre", "norm", "bias", "rate", "skip")
        outs = unpack(1, grad_conv, names)
        outs = [outs[0], outs[1][0], dpre, outs[3][0], outs[4][0], outs[5][0], outs[6][0]]
    else:
        smalls = [
            jnp.moveaxis(dtaps.reshape(CONV, dp, -1), 1, 0).reshape(dp, -1),
            dshift.reshape(dp, -1),
            dpre.reshape(dp, -1),
            dgain.reshape(dp, -1),
            dsb.reshape(dp, -1),
            drate.reshape(dp, -1),
            dskip[:, :HEADS].reshape(dp, -1),
        ]
        bundle = jnp.concatenate(smalls + [jnp.zeros((dp, high * lanes - used), f32)], axis=1)
        grad_gate = plain_sum(normed, dgate)
        grad_out = plain_sum(no, cot)
        mine = lax.psum(lax.psum_scatter(bundle, "dp", scatter_dimension=0), "seq")
        grad_conv = jnp.concatenate([plain_sum(normed, gp), plain_sum(normed, draw)], axis=1)
        outs, at = [], 0
        for shape, size in zip(shapes, sizes):
            outs.append(mine[at : at + size].reshape(shape))
            at += size
    grad_in = jnp.concatenate([grad_gate, grad_conv[:, : CONV_CH + HEADS]], axis=1)
    return (
        mixed[None], grad_tokens[None], grad_in, grad_out, outs[0], outs[1],
        outs[2], outs[3], outs[4], outs[5], outs[6],
    )


def solution(mesh):
    return jax.shard_map(
        shards,
        mesh=mesh,
        in_specs=(
            P("dp", "seq", None), P("dp", "seq", None), P("dp", None), P("dp", None),
            P(None, "dp"), P("dp"), P("dp"), P("dp"), P("dp"), P("dp"), P("dp"),
        ),
        out_specs=(
            P("dp", "seq", None), P("dp", "seq", None), P("dp", None), P("dp", None),
            P(None, "dp"), P("dp"), P("dp"), P("dp"), P("dp"), P("dp"), P("dp"),
        ),
        check_vma=False,
    )
```

```python
import functools

import jax
import jax.numpy as jnp
from jax import lax
from jax.experimental import pallas as pl
from jax.experimental.pallas import tpu as pltpu
from jax.sharding import PartitionSpec as P

HEADS = 32
HEAD_DIM = 64
STATE = 128
CONV = 4
GROUP = 256
INNER = 2048
CONV_CH = 2304
EDGE = 16
TILE = 256
HPT = TILE // HEAD_DIM
TILES = INNER // TILE
LANES = 128

bf16 = jnp.bfloat16
f32 = jnp.float32
epsilon = 1e-05
VMEM_LIMIT = 24 * 1024 * 1024


def params(vmem=VMEM_LIMIT):
    return pltpu.CompilerParams(vmem_limit_bytes=vmem)


def mm(a, b, dims=((1,), (0,))):
    return lax.dot_general(a, b, (dims, ((), ())), preferred_element_type=f32)


NT = ((1,), (1,))
TN = ((0,), (0,))


def split3(v):
    hi = v.astype(bf16)
    rest = v - hi.astype(f32)
    mid = rest.astype(bf16)
    lo = (rest - mid.astype(f32)).astype(bf16)
    return hi, mid, lo


def split2(v):
    hi = v.astype(bf16)
    return hi, (v - hi.astype(f32)).astype(bf16)


def expander(tile):
    head = lax.broadcasted_iota(jnp.int32, (3 * HEADS, TILE), 0) % HEADS
    lane = lax.broadcasted_iota(jnp.int32, (3 * HEADS, TILE), 1)
    return (head == HPT * tile + lane // HEAD_DIM).astype(f32).astype(bf16)


def selector(tile):
    lane = lax.broadcasted_iota(jnp.int32, (TILE, LANES), 0)
    head = lax.broadcasted_iota(jnp.int32, (TILE, LANES), 1)
    return (head == HPT * tile + lane // HEAD_DIM).astype(f32).astype(bf16)


def head_sums(v, sel):
    hi, lo = split2(v)
    return mm(hi, sel) + mm(lo, sel)


def sigmoid(v):
    return 0.5 * jnp.tanh(0.5 * v) + 0.5


def conv_of(p_ref, taps, shift, length):
    out = shift
    for k in range(CONV):
        out = out + p_ref[pl.ds(EDGE - CONV + 1 + k, length), :] * taps[k : k + 1, :]
    return out


def tri(lower):
    r = lax.broadcasted_iota(jnp.int32, (GROUP, GROUP), 0)
    c = lax.broadcasted_iota(jnp.int32, (GROUP, GROUP), 1)
    return ((r >= c) if lower else (r <= c)).astype(f32).astype(bf16)


def lasts(cum3_ref, blocks):
    return jnp.concatenate(
        [cum3_ref[(b + 1) * GROUP - 1 : (b + 1) * GROUP, :] for b in range(blocks)], axis=0
    )


def front_kernel(blocks, p_ref, raw_ref, taps_ref, shift_ref, sb_ref, rate_ref, *outs):
    front_body(blocks, p_ref, raw_ref, taps_ref[...], shift_ref[...], sb_ref, rate_ref, *outs)


def front_body(
    blocks, p_ref, raw_ref, taps, shift, sb_ref, rate_ref,
    x_ref, w_ref, bs_ref, dev_ref, keys_ref, queries_ref, gmat_ref, gmat_t_ref,
    step3_ref, cum3_ref, cum_t_ref,
):
    length = blocks * GROUP
    at = pl.program_id(0)
    conv = conv_of(p_ref, taps, shift, length)
    act = conv * sigmoid(conv)

    @pl.when(at == 0)
    def _():
        keys = act[:, :STATE].astype(bf16)
        queries = act[:, STATE:].astype(bf16)
        keys_ref[...] = keys
        queries_ref[...] = queries
        z = raw_ref[EDGE:, :HEADS] + sb_ref[0:1, :]
        step = jnp.maximum(z, 0.0) + jnp.log1p(jnp.exp(-jnp.abs(z)))
        decays = -step * rate_ref[0:1, :]
        step3_ref[...] = jnp.concatenate(split3(step), axis=1)
        low = tri(True)
        for b in range(blocks):
            rows = slice(b * GROUP, (b + 1) * GROUP)
            gmat_ref[b] = mm(queries[rows], keys[rows], NT)
            gmat_t_ref[b] = mm(keys[rows], queries[rows], NT)
            parts = split3(decays[rows])
            cum = mm(low, parts[0]) + mm(low, parts[1]) + mm(low, parts[2])
            cum3_ref[rows, :] = jnp.concatenate(split3(cum), axis=1)
            cum_t_ref[:, rows] = sum(
                mm(part, low, ((0,), (1,))) for part in parts
            )

    @pl.when(at > 0)
    def _():
        spread = expander(at - 1)
        step = mm(step3_ref[...], spread)
        cum = mm(cum3_ref[...], spread)
        weighted = act * step
        x_ref[...] = act.astype(bf16)
        w_ref[...] = weighted.astype(bf16)
        ends = mm(spread, lasts(cum3_ref, blocks), ((0,), (1,)))
        total = None
        for b in range(blocks):
            rows = slice(b * GROUP, (b + 1) * GROUP)
            tails = jnp.exp(cum[(b + 1) * GROUP - 1 : (b + 1) * GROUP, :] - cum[rows])
            state = mm((weighted[rows] * tails).astype(bf16), keys_ref[rows, :], TN)
            bs_ref[b] = state
            total = state if total is None else jnp.exp(ends[:, b : b + 1]) * total + state
        dev_ref[0] = total.astype(bf16)
        whole = jnp.exp(sum(ends[:, b : b + 1] for b in range(blocks)))
        dev_ref[1] = jnp.broadcast_to(whole, total.shape).astype(bf16)


def front_outs(length):
    blocks = length // GROUP
    spec = pl.BlockSpec
    xt = lambda g: (0, jnp.maximum(g - 1, 0))
    whole2 = lambda g: (0, 0)
    whole3 = lambda g: (0, 0, 0)
    specs = [
        spec((length, TILE), xt),
        spec((length, TILE), xt),
        spec((blocks, TILE, STATE), lambda g: (0, jnp.maximum(g - 1, 0), 0)),
        spec((2, TILE, STATE), lambda g: (0, jnp.maximum(g - 1, 0), 0)),
        spec((length, STATE), whole2),
        spec((length, STATE), whole2),
        spec((blocks, GROUP, GROUP), whole3),
        spec((blocks, GROUP, GROUP), whole3),
        spec((length, 3 * HEADS), whole2),
        spec((length, 3 * HEADS), whole2),
        spec((HEADS, length), whole2),
    ]
    shapes = [
        jax.ShapeDtypeStruct((length, INNER), bf16),
        jax.ShapeDtypeStruct((length, INNER), bf16),
        jax.ShapeDtypeStruct((blocks, INNER, STATE), f32),
        jax.ShapeDtypeStruct((2, INNER, STATE), bf16),
        jax.ShapeDtypeStruct((length, STATE), bf16),
        jax.ShapeDtypeStruct((length, STATE), bf16),
        jax.ShapeDtypeStruct((blocks, GROUP, GROUP), f32),
        jax.ShapeDtypeStruct((blocks, GROUP, GROUP), f32),
        jax.ShapeDtypeStruct((length, 3 * HEADS), bf16),
        jax.ShapeDtypeStruct((length, 3 * HEADS), bf16),
        jax.ShapeDtypeStruct((HEADS, length), f32),
    ]
    return specs, shapes


def front(p, raw, taps, shift, sb, rate):
    length = p.shape[0] - EDGE
    tile = lambda g: (0, lax.rem(g + TILES, TILES + 1))
    whole2 = lambda g: (0, 0)
    specs, shapes = front_outs(length)
    return pl.pallas_call(
        functools.partial(front_kernel, length // GROUP),
        grid=(TILES + 1,),
        in_specs=[
            pl.BlockSpec((length + EDGE, TILE), tile),
            pl.BlockSpec((length + EDGE, LANES), whole2),
            pl.BlockSpec((CONV, TILE), tile),
            pl.BlockSpec((1, TILE), tile),
            pl.BlockSpec((1, HEADS), whole2),
            pl.BlockSpec((1, HEADS), whole2),
        ],
        out_specs=specs,
        out_shape=shapes,
        compiler_params=params(),
        cost_estimate=pl.CostEstimate(flops=600_000_000, bytes_accessed=14_000_000, transcendentals=4_000_000),
        name="front",
    )(p, raw, taps, shift, sb, rate)


def intra_kernel(blocks, w_ref, cum3_ref, cum_t_ref, gmat_ref, y_ref):
    at = pl.program_id(0)
    cum = mm(cum3_ref[...], expander(at))
    r = lax.broadcasted_iota(jnp.int32, (GROUP, GROUP), 0)
    c = lax.broadcasted_iota(jnp.int32, (GROUP, GROUP), 1)
    causal = r >= c
    first = lax.broadcasted_iota(jnp.int32, (GROUP, LANES), 1) < HEAD_DIM
    for b in range(blocks):
        rows = slice(b * GROUP, (b + 1) * GROUP)
        gmat = gmat_ref[b]
        for pair in range(HPT // 2):
            lanes = slice(pair * LANES, (pair + 1) * LANES)
            w = w_ref[rows, lanes]
            outs = []
            for side in range(2):
                j = 2 * pair + side
                col = cum[rows, j * HEAD_DIM : j * HEAD_DIM + 1]
                row = cum_t_ref[pl.ds(HPT * at + j, 1), rows]
                kernel = jnp.exp(jnp.where(causal, col - row, -1e30)) * gmat
                outs.append(mm(kernel.astype(bf16), w))
            y_ref[rows, lanes] = jnp.where(first, outs[0], outs[1])


def intra_of(w, cum3, cum_t, gmat):
    length = w.shape[0]
    blocks = length // GROUP
    tile = lambda g: (0, g)
    whole2 = lambda g: (0, 0)
    return pl.pallas_call(
        functools.partial(intra_kernel, blocks),
        grid=(TILES,),
        in_specs=[
            pl.BlockSpec((length, TILE), tile),
            pl.BlockSpec((length, 3 * HEADS), whole2),
            pl.BlockSpec((HEADS, length), whole2),
            pl.BlockSpec((blocks, GROUP, GROUP), lambda g: (0, 0, 0)),
        ],
        out_specs=pl.BlockSpec((length, TILE), tile),
        out_shape=jax.ShapeDtypeStruct((length, INNER), f32),
        compiler_params=params(),
        cost_estimate=pl.CostEstimate(flops=2_200_000_000, bytes_accessed=7_000_000, transcendentals=4_200_000),
        name="intra",
    )(w, cum3, cum_t, gmat)


def middle_kernel(
    blocks, y_ref, x_ref, gate_ref, gno_ref, q_ref, cum3_ref, start_ref, bs_ref, skip_ref, gain_ref,
    no_ref, dgate_ref, do_ref, dgain_ref, dskip_ref, rowsum_ref, dstart_ref, gdev_ref,
    y_s, sq_s, gt_s, r_s, m_s,
):
    length = blocks * GROUP
    phase, at = pl.program_id(0), pl.program_id(1)
    spread = expander(at)
    cum = mm(cum3_ref[...], spread)
    lanes = pl.ds(pl.multiple_of(at * TILE, TILE), TILE)
    x = x_ref[...].astype(f32)
    gate = gate_ref[...]
    sig = sigmoid(gate)
    gn = gno_ref[...]
    gain = gain_ref[0:1, :]
    skip = skip_ref[0:1, :]
    ends = jnp.exp(mm(spread, lasts(cum3_ref, blocks), ((0,), (1,))))

    @pl.when(phase == 0)
    def _():
        start = start_ref[...]
        for b in range(blocks):
            rows = slice(b * GROUP, (b + 1) * GROUP)
            inter = mm(q_ref[rows, :], start.astype(bf16), NT) * jnp.exp(cum[rows])
            y_s[rows, lanes] = y_ref[rows, :] + inter
            start = ends[:, b : b + 1] * start + bs_ref[b]
        gated = (y_s[:, lanes] + skip * x) * (gate * sig)
        sq = gated * gated
        gt = gated * gn * gain
        sq = sq[:, :LANES] + sq[:, LANES:]
        gt = gt[:, :LANES] + gt[:, LANES:]

        @pl.when(at == 0)
        def _():
            sq_s[...] = sq
            gt_s[...] = gt

        @pl.when(at > 0)
        def _():
            sq_s[...] += sq
            gt_s[...] += gt

    @pl.when(phase == 1)
    def _():
        @pl.when(at == 0)
        def _():
            r = lax.rsqrt(jnp.sum(sq_s[...], axis=1, keepdims=True) / INNER + epsilon)
            m = r * r * r * (jnp.sum(gt_s[...], axis=1, keepdims=True) / INNER)
            r_s[...] = jnp.broadcast_to(r, r_s.shape)
            m_s[...] = jnp.broadcast_to(m, m_s.shape)

        r = r_s[:, 0:1]
        m = m_s[:, 0:1]
        y = y_s[:, lanes]
        ssm = y + skip * x
        silu = gate * sig
        gated = ssm * silu
        scaled = gated * r
        no_ref[...] = (scaled * gain).astype(bf16)
        dgain_ref[...] = jnp.sum(gn * scaled, axis=0, keepdims=True)
        dgated = r * gn * gain - gated * m
        dgate_ref[...] = (dgated * ssm * (sig * (1.0 + gate * (1.0 - sig)))).astype(bf16)
        dof = dgated * silu
        dob = dof.astype(bf16)
        do_ref[...] = dob
        sums = head_sums(dob.astype(f32) * y, selector(at))
        skips = jnp.broadcast_to(jnp.sum(dof * x, axis=0, keepdims=True), (8, TILE))
        skips = head_sums(skips, selector(at))[0:1]

        @pl.when(at == 0)
        def _():
            rowsum_ref[...] = sums
            dskip_ref[...] = skips

        @pl.when(at > 0)
        def _():
            rowsum_ref[...] += sums
            dskip_ref[...] += skips

        scaled_do = (dof * jnp.exp(cum)).astype(bf16)
        total = None
        for b in reversed(range(blocks)):
            rows = slice(b * GROUP, (b + 1) * GROUP)
            d = mm(scaled_do[rows], q_ref[rows, :], TN)
            dstart_ref[b] = d
            total = d if total is None else ends[:, b : b + 1] * total + d
        gdev_ref[...] = total.astype(bf16)


def middle(y, x, gate, gno, q, cum3, start, bs, skip, gain):
    length = x.shape[0]
    blocks = length // GROUP
    both = lambda p, g: (0, g)
    ph0 = lambda p, g: (0, g * (1 - p) + (TILES - 1) * p)
    ph1 = lambda p, g: (0, g * p)
    whole2 = lambda p, g: (0, 0)
    return pl.pallas_call(
        functools.partial(middle_kernel, blocks),
        grid=(2, TILES),
        in_specs=[
            pl.BlockSpec((length, TILE), ph0),
            pl.BlockSpec((length, TILE), both),
            pl.BlockSpec((length, TILE), both),
            pl.BlockSpec((length, TILE), both),
            pl.BlockSpec((length, STATE), whole2),
            pl.BlockSpec((length, 3 * HEADS), whole2),
            pl.BlockSpec((TILE, STATE), lambda p, g: (g * (1 - p) + (TILES - 1) * p, 0)),
            pl.BlockSpec((blocks, TILE, STATE), lambda p, g: (0, g * (1 - p) + (TILES - 1) * p, 0)),
            pl.BlockSpec((1, TILE), both),
            pl.BlockSpec((1, TILE), both),
        ],
        out_specs=[
            pl.BlockSpec((length, TILE), ph1),
            pl.BlockSpec((length, TILE), ph1),
            pl.BlockSpec((length, TILE), ph1),
            pl.BlockSpec((1, TILE), ph1),
            pl.BlockSpec((1, LANES), whole2),
            pl.BlockSpec((length, LANES), whole2),
            pl.BlockSpec((blocks, TILE, STATE), lambda p, g: (0, g * p, 0)),
            pl.BlockSpec((TILE, STATE), lambda p, g: (g * p, 0)),
        ],
        out_shape=[
            jax.ShapeDtypeStruct((length, INNER), bf16),
            jax.ShapeDtypeStruct((length, INNER), bf16),
            jax.ShapeDtypeStruct((length, INNER), bf16),
            jax.ShapeDtypeStruct((1, INNER), f32),
            jax.ShapeDtypeStruct((1, LANES), f32),
            jax.ShapeDtypeStruct((length, LANES), f32),
            jax.ShapeDtypeStruct((blocks, INNER, STATE), f32),
            jax.ShapeDtypeStruct((INNER, STATE), bf16),
        ],
        scratch_shapes=[
            pltpu.VMEM((length, INNER), f32),
            pltpu.VMEM((length, LANES), f32),
            pltpu.VMEM((length, LANES), f32),
            pltpu.VMEM((length, LANES), f32),
            pltpu.VMEM((length, LANES), f32),
        ],
        compiler_params=params(),
        cost_estimate=pl.CostEstimate(flops=1_200_000_000, bytes_accessed=32_000_000, transcendentals=6_000_000),
        name="middle",
    )(y, x, gate, gno, q, cum3, start, bs, skip, gain)


def intra_back_kernel(
    blocks, w_ref, do_ref, cum3_ref, cum_t_ref, gmat_t_ref, k_ref, q_ref, dw_ref, dq_ref, dk_ref, dg_s
):
    at = pl.program_id(0)
    cum = mm(cum3_ref[...], expander(at))
    r = lax.broadcasted_iota(jnp.int32, (GROUP, GROUP), 0)
    c = lax.broadcasted_iota(jnp.int32, (GROUP, GROUP), 1)
    causal = c >= r
    first = lax.broadcasted_iota(jnp.int32, (GROUP, LANES), 1) < HEAD_DIM
    for b in range(blocks):
        rows = slice(b * GROUP, (b + 1) * GROUP)
        gmat = gmat_t_ref[b]
        dg = None
        for pair in range(HPT // 2):
            lanes = slice(pair * LANES, (pair + 1) * LANES)
            w = w_ref[rows, lanes]
            do = do_ref[rows, lanes]
            outs = []
            for side in range(2):
                j = 2 * pair + side
                col = cum[rows, j * HEAD_DIM : j * HEAD_DIM + 1]
                row = cum_t_ref[pl.ds(HPT * at + j, 1), rows]
                decay = jnp.exp(jnp.where(causal, row - col, -1e30))
                outs.append(mm((decay * gmat).astype(bf16), do))
                own = jnp.where(first if side == 0 else ~first, w, jnp.zeros_like(w))
                term = mm(own, do, NT) * decay
                dg = term if dg is None else dg + term
            dw_ref[rows, lanes] = jnp.where(first, outs[0], outs[1])

        @pl.when(at == 0)
        def _():
            dg_s[b] = dg

        @pl.when(at > 0)
        def _():
            dg_s[b] += dg

    @pl.when(at == TILES - 1)
    def _():
        for b in range(blocks):
            rows = slice(b * GROUP, (b + 1) * GROUP)
            dg = dg_s[b].astype(bf16)
            dk_ref[rows, :] = mm(dg, q_ref[rows, :])
            dq_ref[rows, :] = mm(dg, k_ref[rows, :], TN)


def intra_back(w, do, cum3, cum_t, gmat_t, k, q):
    length = w.shape[0]
    blocks = length // GROUP
    tile = lambda g: (0, g)
    whole2 = lambda g: (0, 0)
    return pl.pallas_call(
        functools.partial(intra_back_kernel, blocks),
        grid=(TILES,),
        in_specs=[
            pl.BlockSpec((length, TILE), tile),
            pl.BlockSpec((length, TILE), tile),
            pl.BlockSpec((length, 3 * HEADS), whole2),
            pl.BlockSpec((HEADS, length), whole2),
            pl.BlockSpec((blocks, GROUP, GROUP), lambda g: (0, 0, 0)),
            pl.BlockSpec((length, STATE), whole2),
            pl.BlockSpec((length, STATE), whole2),
        ],
        out_specs=[
            pl.BlockSpec((length, TILE), tile),
            pl.BlockSpec((length, STATE), whole2),
            pl.BlockSpec((length, STATE), whole2),
        ],
        out_shape=[
            jax.ShapeDtypeStruct((length, INNER), f32),
            jax.ShapeDtypeStruct((length, STATE), f32),
            jax.ShapeDtypeStruct((length, STATE), f32),
        ],
        scratch_shapes=[pltpu.VMEM((blocks, GROUP, GROUP), f32)],
        compiler_params=params(),
        cost_estimate=pl.CostEstimate(flops=4_400_000_000, bytes_accessed=10_000_000, transcendentals=4_200_000),
        name="intra_back",
    )(w, do, cum3, cum_t, gmat_t, k, q)


def back_kernel(
    blocks, p_ref, taps_ref, shift_ref, x_ref, w_ref, do_ref, dwi_ref, skip_ref,
    start_ref, bs_ref, adj_ref, dstart_ref,
    k_ref, q_ref, step3_ref, cum3_ref, dqi_ref, dki_ref, rowsum_ref, raw_ref, sb_ref, rate_ref,
    gp_ref, last_ref, before_ref, dtaps_ref, dshift_ref, draw_ref, dsb_ref, drate_ref,
    dq_s, dk_s, sx_s, sw_s, sv_s, dec_s, d_s,
):
    length = blocks * GROUP
    at = pl.program_id(0)

    @pl.when(at == 0)
    def _():
        dq_s[...] = dqi_ref[...]
        dk_s[...] = dki_ref[...]
        sx_s[...] = jnp.zeros_like(sx_s)
        sw_s[...] = jnp.zeros_like(sw_s)
        sv_s[...] = jnp.zeros_like(sv_s)
        dec_s[...] = jnp.zeros_like(dec_s)
        d_s[0:EDGE, :] = jnp.zeros((EDGE, TILE), f32)
        d_s[length + EDGE :, :] = jnp.zeros((EDGE, TILE), f32)

    def conv_back(dact):
        conv = conv_of(p_ref, taps_ref[...], shift_ref[...], length)
        sig = sigmoid(conv)
        dconv = dact * (sig * (1.0 + conv * (1.0 - sig)))
        d_s[EDGE : EDGE + length, :] = dconv
        dshift_ref[...] = jnp.sum(dconv, axis=0, keepdims=True)
        dp = None
        before = None
        for k in range(CONV):
            tap = taps_ref[k : k + 1, :]
            src = p_ref[pl.ds(EDGE - CONV + 1 + k, length), :]
            dtaps_ref[k : k + 1, :] = jnp.sum(dconv * src, axis=0, keepdims=True)
            term = tap * d_s[pl.ds(EDGE + CONV - 1 - k, length), :]
            dp = term if dp is None else dp + term
            edge = tap * d_s[pl.ds(CONV - 1 - k, EDGE), :]
            before = edge if before is None else before + edge
        gp_ref[...] = dp.astype(bf16)
        last_ref[...] = dp[length - EDGE :, :]
        before_ref[...] = before

    @pl.when(at < TILES)
    def _():
        spread = expander(at)
        sel = selector(at)
        cum = mm(cum3_ref[...], spread)
        step = mm(step3_ref[...], spread)
        ends = jnp.exp(mm(spread, lasts(cum3_ref, blocks), ((0,), (1,))))
        x = x_ref[...].astype(f32)
        w = w_ref[...].astype(f32)
        do = do_ref[...].astype(f32)
        scaled_do = (do * jnp.exp(cum)).astype(bf16)
        starts = [start_ref[...]]
        for b in range(blocks - 1):
            starts.append(ends[:, b : b + 1] * starts[b] + bs_ref[b])
        adjs = [None] * blocks
        adj = adj_ref[...]
        for b in reversed(range(blocks)):
            adjs[b] = adj
            adj = ends[:, b : b + 1] * adj + dstart_ref[b]
        dws = []
        for b in range(blocks):
            rows = slice(b * GROUP, (b + 1) * GROUP)
            tails = jnp.exp(cum[(b + 1) * GROUP - 1 : (b + 1) * GROUP, :] - cum[rows])
            ab = adjs[b].astype(bf16)
            dws.append(tails * mm(k_ref[rows, :], ab, NT))
            dk_s[rows, :] += mm((w[rows] * tails).astype(bf16), ab)
            dq_s[rows, :] += mm(scaled_do[rows], starts[b].astype(bf16))
            both = jnp.sum(dws[b] * w[rows], axis=0, keepdims=True)
            sv_s[b : b + 1, :] += head_sums(jnp.broadcast_to(both, (8, TILE)), sel)[0:1]
            hi, lo = split2(ends[:, b : b + 1] * adjs[b] * starts[b])
            dec_s[b : b + 1, :] += jnp.sum(mm(hi, sel, TN) + mm(lo, sel, TN), axis=0, keepdims=True)
        dws = jnp.concatenate(dws, axis=0)
        dw = dwi_ref[...] + dws
        sx_s[...] += head_sums(dw * x, sel)
        sw_s[...] += head_sums(dw * w, sel)
        conv_back(dw * step + do * skip_ref[0:1, :])

    @pl.when(at == TILES)
    def _():
        conv_back(jnp.concatenate([dk_s[...], dq_s[...]], axis=1))
        dcum = (rowsum_ref[...] - sw_s[...])[:, :HEADS]
        z = raw_ref[EDGE:, :HEADS] + sb_ref[0:1, :]
        step = jnp.maximum(z, 0.0) + jnp.log1p(jnp.exp(-jnp.abs(z)))
        rate = rate_ref[0:1, :]
        up = tri(False)
        decays = []
        for b in range(blocks):
            rows = slice(b * GROUP, (b + 1) * GROUP)
            parts = split3(dcum[rows])
            extra = sv_s[b : b + 1, :HEADS] + dec_s[b : b + 1, :HEADS]
            decays.append(mm(up, parts[0]) + mm(up, parts[1]) + mm(up, parts[2]) + extra)
        ddecay = jnp.concatenate(decays, axis=0)
        dstep = sx_s[...][:, :HEADS] - ddecay * rate
        dz = dstep * sigmoid(z)
        draw_ref[...] = jnp.zeros_like(draw_ref)
        draw_ref[:, :HEADS] = dz.astype(bf16)
        dsb_ref[...] = jnp.sum(dz, axis=0, keepdims=True)
        drate_ref[...] = jnp.sum(-ddecay * step * rate, axis=0, keepdims=True)


def back(p, taps, shift, x, w, do, dwi, skip, start, bs, adj, dstart, k, q, step3, cum3, dqi, dki, rowsum, raw, sb, rate):
    length = x.shape[0]
    blocks = length // GROUP
    tile = lambda g: (0, g)
    xt = lambda g: (0, jnp.minimum(g, TILES - 1))
    st = lambda g: (jnp.minimum(g, TILES - 1), 0)
    st3 = lambda g: (0, jnp.minimum(g, TILES - 1), 0)
    whole2 = lambda g: (0, 0)
    spec = pl.BlockSpec
    return pl.pallas_call(
        functools.partial(back_kernel, blocks),
        grid=(TILES + 1,),
        in_specs=[
            spec((length + EDGE, TILE), tile),
            spec((CONV, TILE), tile),
            spec((1, TILE), tile),
            spec((length, TILE), xt),
            spec((length, TILE), xt),
            spec((length, TILE), xt),
            spec((length, TILE), xt),
            spec((1, TILE), xt),
            spec((TILE, STATE), st),
            spec((blocks, TILE, STATE), st3),
            spec((TILE, STATE), st),
            spec((blocks, TILE, STATE), st3),
            spec((length, STATE), whole2),
            spec((length, STATE), whole2),
            spec((length, 3 * HEADS), whole2),
            spec((length, 3 * HEADS), whole2),
            spec((length, STATE), whole2),
            spec((length, STATE), whole2),
            spec((length, LANES), whole2),
            spec((length + EDGE, LANES), lambda g: (0, 0)),
            spec((1, HEADS), whole2),
            spec((1, HEADS), whole2),
        ],
        out_specs=[
            spec((length, TILE), tile),
            spec((EDGE, TILE), tile),
            spec((EDGE, TILE), tile),
            spec((CONV, TILE), tile),
            spec((1, TILE), tile),
            spec((length, LANES), whole2),
            spec((1, HEADS), whole2),
            spec((1, HEADS), whole2),
        ],
        out_shape=[
            jax.ShapeDtypeStruct((length, CONV_CH), bf16),
            jax.ShapeDtypeStruct((EDGE, CONV_CH), f32),
            jax.ShapeDtypeStruct((EDGE, CONV_CH), f32),
            jax.ShapeDtypeStruct((CONV, CONV_CH), f32),
            jax.ShapeDtypeStruct((1, CONV_CH), f32),
            jax.ShapeDtypeStruct((length, LANES), bf16),
            jax.ShapeDtypeStruct((1, HEADS), f32),
            jax.ShapeDtypeStruct((1, HEADS), f32),
        ],
        scratch_shapes=[
            pltpu.VMEM((length, STATE), f32),
            pltpu.VMEM((length, STATE), f32),
            pltpu.VMEM((length, LANES), f32),
            pltpu.VMEM((length, LANES), f32),
            pltpu.VMEM((8, LANES), f32),
            pltpu.VMEM((8, LANES), f32),
            pltpu.VMEM((length + 2 * EDGE, TILE), f32),
        ],
        compiler_params=params(),
        cost_estimate=pl.CostEstimate(flops=2_500_000_000, bytes_accessed=32_000_000, transcendentals=6_000_000),
        name="back",
    )(p, taps, shift, x, w, do, dwi, skip, start, bs, adj, dstart, k, q, step3, cum3, dqi, dki, rowsum, raw, sb, rate)


def ring_ok():
    return lax.axis_size("dp") == 8 and lax.axis_size("seq") == 4


def spots():
    dp, seq = lax.axis_index("dp"), lax.axis_index("seq")
    return dp // 2, dp % 2, seq // 2, seq % 2


def over_y(a):
    return lax.ppermute(a, "dp", [(i, i ^ 1) for i in range(8)])


def over_z(a, k):
    return lax.ppermute(a, "dp", [(i, (i + 2 * k) % 8) for i in range(8)])


def over_x(a):
    return lax.ppermute(a, "seq", [(i, i ^ 2) for i in range(4)])


def over_core(a):
    return lax.ppermute(a, "seq", [(i, i ^ 1) for i in range(4)])


def assemble_kernel(rows, parts, *refs):
    assemble(rows, parts, refs[:13], refs[13:-1], refs[-1])


def assemble(rows, parts, pieces, outs, sem):
    own, a3, ay, b3, by, xb3, xby, ca3, cay, cb3, cby, cxb3, cxby = pieces
    z, y, x, c = spots()
    copies = []

    def put(src, dp, row, size):
        for out, (col, width, factor, base) in zip(outs_of, parts):
            copies.append(
                pltpu.make_async_copy(
                    src.at[:, pl.ds(col, width)],
                    out.at[pl.ds(pl.multiple_of(dp * (rows * factor) + base + row, 16), size), :],
                    sem.at[len(copies)],
                )
            )

    outs_of = [outs[part[4]] for part in parts]
    parts = [part[:4] for part in parts]
    put(own, z * 2 + y, 0, rows)
    half, fourth, eighth = rows // 2, rows // 4, rows // 8
    for k in range(4):
        zz = lax.rem(z + 4 - k, 4)
        for side in range(2):
            if k == 0 and side == 0:
                continue
            yy = y if side == 0 else 1 - y
            dp = zz * 2 + yy
            for core in range(2):
                cc = c if core == 0 else 1 - c
                src = ((a3, ay), (ca3, cay))[core][side]
                put(src.at[k - 1 if side == 0 else k], dp, cc * half, fourth)
                for far in range(2):
                    xx = x if far == 0 else 1 - x
                    src = (((b3, by), (xb3, xby)), ((cb3, cby), (cxb3, cxby)))[core][far][side]
                    put(
                        src.at[k - 1 if side == 0 else k],
                        dp,
                        cc * half + fourth + xx * eighth,
                        eighth,
                    )
    for copy in copies:
        copy.start()
    for copy in copies:
        copy.wait()


def gather_plain(pieces, parts):
    full = lax.all_gather(jnp.concatenate(pieces, axis=1), "dp")
    outs = []
    for out in sorted({part[4] for part in parts}):
        chosen = [full[:, :, p[0] : p[0] + p[1]] for p in parts if p[4] == out]
        outs.append(jnp.concatenate(chosen, axis=1).reshape(-1, chosen[0].shape[2]))
    return outs


def cut(pieces, start, size):
    return jnp.concatenate([lax.dynamic_slice_in_dim(p, start, size, 0) for p in pieces], axis=1)


def along_z(pieces, fourth_part):
    rows = pieces[0].shape[0]
    z, y, x, c = spots()
    if fourth_part:
        own = cut(pieces, c * (rows // 2), rows // 4)
    else:
        own = cut(pieces, c * (rows // 2) + rows // 4 + x * (rows // 8), rows // 8)
    return own, [over_z(own, k) for k in (1, 2, 3)]


def gather_pieces(pieces, a3, ay, b3, by, xb3, xby):
    sent = [a3, ay, b3, by, xb3, xby]
    return [jnp.concatenate(pieces, axis=1), *sent, *[over_core(a) for a in sent]]


def gather_end(pieces, parts, *staged):
    rows = pieces[0].shape[0]
    arrays = gather_pieces(pieces, *staged)
    shard = arrays[0]
    widths = {part[4]: part[1:3] for part in parts}
    shapes = [
        jax.ShapeDtypeStruct((8 * rows * widths[out][1], widths[out][0]), shard.dtype)
        for out in sorted(widths)
    ]
    anywhere = pl.BlockSpec(memory_space=pl.ANY)
    return pl.pallas_call(
        functools.partial(assemble_kernel, rows, parts),
        in_specs=[anywhere] * 13,
        out_specs=[pl.BlockSpec(memory_space=pltpu.VMEM)] * len(shapes),
        out_shape=shapes,
        scratch_shapes=[pltpu.SemaphoreType.DMA((len(parts) * (1 + 7 * 6),))],
        compiler_params=params(),
        cost_estimate=pl.CostEstimate(flops=0, bytes_accessed=32 * shard.size, transcendentals=0),
        name="assemble",
    )(*arrays)


SIDE = LANES - HEADS


def side_plan():
    plan = []
    for k in range(CONV):
        plan += [("taps", k, SIDE * j, SIDE, 3 * k + j) for j in range(3)]
    plan += [("shift", 0, SIDE * j, SIDE, 12 + j) for j in range(3)]
    plan += [("pre", 0, 0, SIDE, 15), ("pre", 0, SIDE, 32, 16)]
    plan += [("norm", 0, 0, SIDE, 17), ("norm", 0, SIDE, SIDE, 18), ("norm", 0, 2 * SIDE, 64, 19)]
    plan += [(name, 0, 0, 4, 20 + j) for j, name in enumerate(("bias", "rate", "skip"))]
    return plan


SIDE_WIDTH = {"taps": 288, "shift": 288, "pre": 128, "norm": 256, "bias": 4, "rate": 4, "skip": 4}


def pack_kernel(shards_in, names, left, *refs):
    out = refs[-1]
    out[...] = jnp.zeros_like(out)
    values = {name: ref[...].astype(f32) for name, ref in zip(names, refs)}
    for i in range(shards_in):
        for name, k, col, width, row in side_plan():
            if name in values:
                start = i * SIDE_WIDTH[name] + col
                out[i * 128 + row : i * 128 + row + 1, left : left + width] = values[name][
                    k : k + 1, start : start + width
                ]


def pack(shards_in, left, named):
    names = tuple(named)
    return pl.pallas_call(
        functools.partial(pack_kernel, shards_in, names, left),
        out_shape=jax.ShapeDtypeStruct((shards_in * 128, left + SIDE), f32),
        name="pack",
    )(*named.values())


def unpack_kernel(shards_in, names, in_ref, *refs):
    unpack_side(shards_in, dict(zip(names, refs)), in_ref[...].astype(f32))


def unpack_side(shards_in, outs, block):
    for i in range(shards_in):
        for name, k, col, width, row in side_plan():
            start = i * SIDE_WIDTH[name] + col
            outs[name][k : k + 1, start : start + width] = block[
                i * 128 + row : i * 128 + row + 1, HEADS : HEADS + width
            ]
    if "lanes" in outs:
        outs["rate"][...] = jnp.exp(outs["rate"][...])
        three = jnp.concatenate(split3(jnp.broadcast_to(outs["skip"][...], (8, HEADS))), axis=1)
        for tile in range(TILES):
            outs["lanes"][:, tile * TILE : (tile + 1) * TILE] = mm(three, expander(tile))[0:1]


SIDE_NAMES = ("taps", "shift", "pre", "norm", "bias", "rate", "skip", "lanes")


def enter_kernel(blocks, *refs):
    w_ref, side_ref, edge_ref, tok_ref, normed_ref, p_ref, raw_ref = refs[:7]
    side = dict(zip(SIDE_NAMES, refs[7:15]))
    fronts = refs[15:26]
    ext_s = refs[26]
    at = pl.program_id(0)

    @pl.when(at == 0)
    def _():
        unpack_side(8, side, side_ref[...].astype(f32))
        for ref, rows_at in ((edge_ref, slice(0, EDGE)), (tok_ref, slice(EDGE, None))):
            tok = ref[...].astype(f32)
            scale = lax.rsqrt(jnp.mean(tok * tok, axis=1, keepdims=True) + epsilon)
            ext_s[rows_at, :] = (tok * scale * side["pre"][...]).astype(bf16)
        normed_ref[...] = ext_s[EDGE:, :]
        raw_ref[...] = mm(ext_s[...], side_ref[...])

    lanes = pl.ds(pl.multiple_of(lax.rem(at + TILES, TILES + 1) * TILE, TILE), TILE)
    p_ref[...] = mm(ext_s[...], w_ref[...])
    front_body(
        blocks, p_ref, raw_ref, side["taps"][:, lanes], side["shift"][:, lanes], side["bias"], side["rate"],
        *fronts,
    )


def enter(weights, edge, toks):
    length, width = toks.shape
    whole2 = lambda g: (0, 0)
    tile = lambda g: (0, lax.rem(g + TILES, TILES + 1))
    shapes = [
        jax.ShapeDtypeStruct((length, width), bf16),
        jax.ShapeDtypeStruct((length + EDGE, CONV_CH), f32),
        jax.ShapeDtypeStruct((length + EDGE, LANES), f32),
    ]
    for name in SIDE_NAMES:
        lanes = INNER if name == "lanes" else 8 * SIDE_WIDTH[name]
        shapes.append(jax.ShapeDtypeStruct((CONV if name == "taps" else 1, lanes), f32))
    specs = [pl.BlockSpec(shape.shape, whole2) for shape in shapes]
    specs[1] = pl.BlockSpec((length + EDGE, TILE), tile)
    more_specs, more_shapes = front_outs(length)
    return pl.pallas_call(
        functools.partial(enter_kernel, length // GROUP),
        grid=(TILES + 1,),
        in_specs=[
            pl.BlockSpec((width, TILE), tile),
            pl.BlockSpec((width, LANES), lambda g: (0, CONV_CH // LANES)),
            pl.BlockSpec(edge.shape, whole2),
            pl.BlockSpec(toks.shape, whole2),
        ],
        out_specs=specs + more_specs,
        out_shape=shapes + more_shapes,
        scratch_shapes=[pltpu.VMEM((length + EDGE, width), bf16)],
        compiler_params=params(),
        cost_estimate=pl.CostEstimate(
            flops=3_200_000_000, bytes_accessed=36_000_000, transcendentals=4_000_000
        ),
        name="enter",
    )(weights, weights, edge, toks)


def unpack(shards_in, full, names):
    shapes = []
    for name in names:
        width = INNER if name == "lanes" else shards_in * SIDE_WIDTH[name]
        shapes.append(jax.ShapeDtypeStruct((CONV if name == "taps" else 1, width), f32))
    whole = [pl.BlockSpec(shape.shape, lambda g: (0, 0)) for shape in shapes]
    return pl.pallas_call(
        functools.partial(unpack_kernel, shards_in, names),
        grid=(1,),
        in_specs=[pl.BlockSpec((shards_in * 128, LANES), lambda g: (0, CONV_CH // LANES))],
        out_specs=whole,
        out_shape=shapes,
        name="unpack",
    )(full)


def weight_grad_kernel(rows, plan, spot_ref, *refs):
    ka_ref, kb_ref, sa_ref, sb_ref, res = refs[-5:]
    y, x, c = spot_ref[1], spot_ref[2], spot_ref[3]
    at = 0
    for lhs, rhs, add, col, folds in plan:
        width = refs[rhs].shape[1]
        product = mm(refs[lhs][...], refs[rhs][...], TN)
        if add is not None:
            product = product + refs[add][...]
        for side in range(2):
            for fold in range(folds):
                top = (side * folds + fold) * rows
                left = col + fold * width
                res[side * rows : (side + 1) * rows, left : left + width] = product[top : top + rows]
    half, fourth, eighth = rows // 2, rows // 4, rows // 8
    for core, (a_ref, b_ref) in enumerate(((ka_ref, kb_ref), (sa_ref, sb_ref))):
        cc = c if core == 0 else 1 - c
        for side in range(2):
            yy = y if side == 0 else 1 - y
            at = yy * rows + cc * half
            a_ref[side, 0] = res[pl.ds(pl.multiple_of(at, fourth), fourth), :].astype(bf16)
            for far in range(2):
                xx = x if far == 0 else 1 - x
                b_ref[far, side, 0] = res[
                    pl.ds(pl.multiple_of(at + fourth + xx * eighth, eighth), eighth), :
                ].astype(bf16)


def weight_grads(rows, cols, arrays, plan):
    z, y, x, c = spots()
    spot = jnp.stack([z, y, x, c]).astype(jnp.int32)
    fourth, eighth = rows // 4, rows // 8
    a_spec = pl.BlockSpec((2, 1, fourth, cols), lambda k, s: (0, k, 0, 0))
    b_spec = pl.BlockSpec((2, 2, 1, eighth, cols), lambda k, s: (0, 0, k, 0, 0))
    a_shape = jax.ShapeDtypeStruct((2, 4, fourth, cols), bf16)
    b_shape = jax.ShapeDtypeStruct((2, 2, 4, eighth, cols), bf16)
    specs = []
    for array, kind in arrays:
        if kind == "lhs":
            specs.append(
                pl.BlockSpec((array.shape[0], array.shape[1] // 4), lambda k, s: (0, lax.rem(s[0] + k, 4)))
            )
        elif kind == "rhs":
            specs.append(pl.BlockSpec(array.shape, lambda k, s: (0, 0)))
        else:
            specs.append(
                pl.BlockSpec((array.shape[0] // 4, array.shape[1]), lambda k, s: (lax.rem(s[0] + k, 4), 0))
            )
    length = arrays[0][0].shape[0]
    return pl.pallas_call(
        functools.partial(weight_grad_kernel, rows, plan),
        grid_spec=pltpu.PrefetchScalarGridSpec(
            num_scalar_prefetch=1,
            grid=(4,),
            in_specs=specs,
            out_specs=[a_spec, b_spec, a_spec, b_spec],
            scratch_shapes=[pltpu.VMEM((2 * rows, cols), f32)],
        ),
        out_shape=[a_shape, b_shape, a_shape, b_shape],
        compiler_params=params((20 if cols > 3000 else 16) * 1024 * 1024),
        cost_estimate=pl.CostEstimate(
            flops=2 * length * 8 * rows * cols, bytes_accessed=20 * rows * cols, transcendentals=0
        ),
        name="weight_grads",
    )(spot, *[array for array, kind in arrays])


def plus(*terms):
    return sum(term.astype(f32) for term in terms).astype(bf16)


def sum_begin(ka, kb, sa, sb):
    ra, rb = over_core(sa), over_core(sb)
    return (plus(ka[1], ra[1]), plus(kb[1], rb[1])), (ka, kb, ra, rb)


def sum_next(got, held):
    ka, kb, ra, rb = held
    got_a, got_b = got
    u = [plus(ka[0, k], ra[0, k], got_a[k]) for k in range(4)]
    b_send = plus(kb[0, 1], rb[0, 1], got_b[1])
    return (u, b_send), (kb, rb, got_b)


def sum_third(sends):
    u, b_send = sends
    return over_y(b_send), u[0], [over_z(u[k], k) for k in (1, 2, 3)]


def sum_fourth(got, held):
    b_far, own, got_u = got
    kb, rb, got_b = held
    v = [plus(kb[0, 0, k], rb[0, 0, k], got_b[0, k], b_far[k]) for k in range(4)]
    fin_a = plus(own, *got_u)
    return fin_a, over_x(fin_a), v[0], [over_z(v[k], k) for k in (1, 2, 3)]


def sum_end(got):
    fin_a, other_a, v, got_v = got
    x, c = spots()[2:]
    eighth, cols = v.shape
    fin_b = plus(v, *got_v)
    other_b = over_x(fin_b)
    b_rows = jnp.where(x == 0, jnp.stack([fin_b, other_b]), jnp.stack([other_b, fin_b]))
    mine = jnp.concatenate([plus(fin_a, other_a), b_rows.reshape(2 * eighth, cols)], axis=0)
    other = over_core(mine)
    both = jnp.where(c == 0, jnp.stack([mine, other]), jnp.stack([other, mine]))
    return both.reshape(8 * eighth, cols).astype(f32)


def plain_sum(lhs, rhs):
    full = lax.dot_general(lhs, rhs, (TN, ((), ())), preferred_element_type=f32)
    part = lax.psum_scatter(full.astype(bf16), "dp", scatter_dimension=0, tiled=True)
    return lax.psum(part, "seq").astype(f32)


def carried(state, decay, mate_decay, axis, reverse):
    size, here = lax.axis_size(axis), lax.axis_index(axis)
    if mate_decay is not None:
        core = here % 2
        own, other = state.astype(f32), over_core(state).astype(f32)
        ahead = (core == 0) if reverse else (core == 1)
        mate_decay = mate_decay.astype(f32)
        pair = jnp.where(ahead, decay.astype(f32) * other + own, mate_decay * own + other).astype(bf16)
        route = [(2, 0), (3, 1)] if reverse else [(0, 2), (1, 3)]
        far = lax.ppermute(pair, axis, route).astype(f32)
        return jnp.where(ahead, other + mate_decay * far, far)
    states = lax.all_gather(state, axis)
    decays = lax.all_gather(decay[:, :1], axis).astype(f32)

    def one(lap, total):
        at = size - 1 - lap if reverse else lap
        use = at > here if reverse else at < here
        new = decays[at] * total + states[at].astype(f32)
        return jnp.where(use, new, total)

    return lax.fori_loop(0, size, one, jnp.zeros(state.shape, f32))


def rms_scale(values, gains):
    return values * lax.rsqrt(jnp.mean(values * values, axis=-1, keepdims=True) + epsilon) * gains


def shards(
    tokens, cotangent, in_weight, out_weight, conv_weight, conv_bias,
    pre_gain, norm_gain, step_bias, decay_log, skip_gain,
):
    dp = lax.axis_size("dp")
    seq = lax.axis_size("seq")
    toks = tokens[0]
    length = toks.shape[0]
    edge = lax.ppermute(toks[length - EDGE :], "seq", [(i, i + 1) for i in range(seq - 1)])
    ring = ring_ok()
    high = in_weight.shape[0]
    out_rows = out_weight.shape[0] // 2
    wide = out_weight.shape[1]
    first_parts = [(0, CONV_CH + LANES, 1, 0, 0)]
    then = [in_weight[:, :INNER], out_weight[:out_rows], out_weight[out_rows:]]
    then_parts = [(0, INNER, 1, 0, 0), (INNER, wide, 2, 0, 1), (INNER + wide, wide, 2, out_rows, 1)]
    if ring:
        named = {
            "taps": conv_weight, "shift": conv_bias[None], "pre": pre_gain[None], "norm": norm_gain[None],
            "bias": step_bias[None], "rate": decay_log[None], "skip": skip_gain[None],
        }
        first = [in_weight[:, INNER:], pack(1, 0, named).astype(bf16)]
        b0, bz = along_z(first, False)
        held = lax.optimization_barrier((*first, *bz))
        a0, az = along_z(held[:2], True)
        bz = list(held[2:])
        b3 = jnp.stack(bz)
        xb3 = over_x(b3)
        by = over_y(jnp.stack([b0] + bz))
        late_b = lax.optimization_barrier((*then, *az))
        az = list(late_b[3:])
        b0_2, bz_2 = along_z(late_b[:3], False)
        a3 = jnp.stack(az)
        ay = over_y(jnp.stack([a0] + az))
        late_a = lax.optimization_barrier((*then, by))
        by = late_a[3]
        a0_2, az_2 = along_z(late_a[:3], True)
        xby = over_x(by)
        ay, xb3, xby, bz_2, az_2[0] = lax.optimization_barrier((ay, xb3, xby, bz_2, az_2[0]))
        (conv_full,) = gather_end(first, first_parts, a3, ay, b3, by, xb3, xby)
        b3_2 = jnp.stack(bz_2)
        xb3_2 = over_x(b3_2)
        by_2 = over_y(jnp.stack([b0_2] + bz_2))
        conv_full, az_2, by_2 = lax.optimization_barrier((conv_full, az_2, by_2))
        xby_2 = over_x(by_2)
        a3_2 = jnp.stack(az_2)
        a4_2 = jnp.stack([a0_2] + az_2)
        ay_2 = over_y(a4_2)
    else:
        pieces = [conv_weight, conv_bias, pre_gain, norm_gain, step_bias, decay_log, skip_gain]
        shapes = [piece.shape for piece in pieces]
        sizes = [piece.size for piece in pieces]
        used = sum(sizes)
        lanes = -(-used // high)
        flat = jnp.concatenate(
            [piece.reshape(-1) for piece in pieces] + [jnp.zeros((high * lanes - used,), bf16)]
        )
        first = [
            in_weight[:, INNER:],
            flat.reshape(high, lanes),
            jnp.zeros((high, LANES - HEADS - lanes), bf16),
        ]
        (conv_full,) = gather_plain(first, first_parts)
        gate_full, out_full = gather_plain(then, then_parts)
        small = conv_full[:, CONV_CH + HEADS : CONV_CH + HEADS + lanes].reshape(dp, high * lanes)
        got, at = [], 0
        for shape, size in zip(shapes, sizes):
            got.append(small[:, at : at + size].reshape((dp,) + shape))
            at += size
        taps = jnp.moveaxis(got[0], 0, 1).reshape(CONV, CONV_CH).astype(f32)
        shift, gains_pre, gains_norm, bias_step, log_rates, skip = [
            piece.reshape(1, -1).astype(f32) for piece in got[1:]
        ]
        rate = jnp.exp(log_rates)
        skip_lanes = jnp.repeat(skip[0], HEAD_DIM)[None]

    if ring:
        entered = enter(conv_full, edge, toks)
        entered = list(entered)
        held = lax.optimization_barrier((entered[12], entered[14], ay_2, xb3_2, xby_2))
        entered[12], entered[14], ay_2, xb3_2, xby_2 = held
        normed, p, raw, taps, shift, gains_pre, gains_norm, bias_step, rate, _, skip_lanes = entered[:11]
        fronts = entered[11:]
    else:
        toks_ext = jnp.concatenate([edge, toks], axis=0)
        normed_ext = rms_scale(toks_ext.astype(f32), gains_pre).astype(bf16)
        normed = normed_ext[EDGE:]
        p = jnp.dot(normed_ext, conv_full[:, :CONV_CH], preferred_element_type=f32)
        raw = jnp.dot(normed_ext, conv_full[:, CONV_CH:], preferred_element_type=f32)
        fronts = front(p, raw, taps, shift, bias_step, rate)
    x, w, bs, dev, k, q, gmat, gmat_t, step3, cum3, cum_t = fronts
    mate_decay = over_core(dev[1]) if ring else None
    start = carried(dev[0], dev[1], mate_decay, "seq", False)
    y = intra_of(w, cum3, cum_t, gmat)
    if ring:
        gate_full, out_full = gather_end(then, then_parts, a3_2, ay_2, b3_2, by_2, xb3_2, xby_2)
    gate = jnp.dot(normed, gate_full, preferred_element_type=f32)
    cot = cotangent[0]
    gno = lax.dot_general(cot, out_full, (((1,), (1,)), ((), ())), preferred_element_type=f32)
    no, dgate, do, dgain, dskip, rowsum, dstart, gdev = middle(
        y, x, gate, gno, q, cum3, start, bs, skip_lanes, gains_norm
    )
    adj = carried(gdev, dev[1], mate_decay, "seq", True)
    rows = toks.astype(f32)
    mixed = (rows + jnp.dot(no, out_full, preferred_element_type=f32)).astype(bf16)
    if ring:
        early = weight_grads(
            high, INNER + 2 * wide,
            [(normed, "lhs"), (dgate, "rhs"), (no, "lhs"), (cot, "rhs")],
            [(0, 1, None, 0, 1), (2, 3, None, INNER, 2)],
        )
        sends, held = sum_begin(*early)
        (cum_t, sends) = lax.optimization_barrier((cum_t, sends))
        got = over_y(sends[0]), over_x(sends[1])
    over_cols = (((1,), (1,)), ((), ()))
    dnormed_gate = lax.dot_general(dgate, gate_full, over_cols, preferred_element_type=f32)
    inside = intra_back(w, do, cum3, cum_t, gmat_t, k, q)
    if ring:
        (dqi, got, mixed, dnormed_gate) = lax.optimization_barrier((inside[1], got, mixed, dnormed_gate))
        sends, held = sum_next(got, held)
        (dqi, sends) = lax.optimization_barrier((dqi, sends))
        got = sum_third(sends)
        inside = (inside[0], dqi, inside[2])
    dwi, dqi, dki = inside
    backs = back(
        p, taps, shift, x, w, do, dwi, skip_lanes, start, bs, adj, dstart,
        k, q, step3, cum3, dqi, dki, rowsum, raw, bias_step, rate,
    )
    if ring:
        backs = list(backs)
        (backs[1], backs[2], backs[3], got) = lax.optimization_barrier((backs[1], backs[2], backs[3], got))
        got = sum_fourth(got, held)
    gp, last, before, dtaps, dshift, draw, dsb, drate = backs
    returned = lax.ppermute(before, "seq", [(i + 1, i) for i in range(seq - 1)])
    gp = gp.at[length - EDGE :].set((last + returned).astype(bf16))
    if ring:
        named = {"taps": dtaps, "shift": dshift, "norm": dgain, "bias": dsb, "rate": drate, "skip": dskip}
        addend = pack(8, HEADS, named)
        late = weight_grads(
            high, CONV_CH + LANES,
            [(normed, "lhs"), (gp, "rhs"), (draw, "rhs"), (addend, "add")],
            [(0, 1, None, 0, 1), (0, 2, 3, CONV_CH, 1)],
        )
        late = list(late)
        late[2], late[3], got_v = lax.optimization_barrier((late[2], late[3], got[3]))
        got = (*got[:3], got_v)
        sends, late_held = sum_begin(*late)
        sends, gp, draw = lax.optimization_barrier((sends, gp, draw))
        late_got = over_y(sends[0]), over_x(sends[1])
    dnormed = (
        lax.dot_general(gp, conv_full[:, :CONV_CH], over_cols, preferred_element_type=f32)
        + dnormed_gate
        + lax.dot_general(draw, conv_full[:, CONV_CH:], over_cols, preferred_element_type=f32)
    )
    r = lax.rsqrt(jnp.mean(rows * rows, axis=-1, keepdims=True) + epsilon)
    t = dnormed * gains_pre
    drows = r * t - rows * (r * r * r * jnp.mean(rows * t, axis=-1, keepdims=True))
    grad_tokens = (cot.astype(f32) + drows).astype(bf16)
    if ring:
        (late_got, grad_tokens, got) = lax.optimization_barrier((late_got, grad_tokens, got))
        sends, late_held = sum_next(late_got, late_held)
        late_got = sum_third(sends)
        early = sum_end(got)
        grad_gate = early[:, :INNER]
        grad_out = jnp.concatenate([early[:, INNER : INNER + wide], early[:, INNER + wide :]], axis=0)
        grad_conv = sum_end(sum_fourth(late_got, late_held))
        own_gate, own_conv = in_weight[:, :INNER], in_weight[:, INNER:]
        dpre = jnp.sum(own_gate.astype(f32) * grad_gate, axis=1) + jnp.sum(
            own_conv.astype(f32) * grad_conv[:, : CONV_CH + HEADS], axis=1
        )
        dpre = dpre / pre_gain.astype(f32)
        names = ("taps", "shift", "pre", "norm", "bias", "rate", "skip")
        outs = unpack(1, grad_conv, names)
        outs = [outs[0], outs[1][0], dpre, outs[3][0], outs[4][0], outs[5][0], outs[6][0]]
    else:
        dpre = jnp.sum(dnormed * rows * r, axis=0)
        smalls = [
            jnp.moveaxis(dtaps.reshape(CONV, dp, -1), 1, 0).reshape(dp, -1),
            dshift.reshape(dp, -1),
            dpre.reshape(dp, -1),
            dgain.reshape(dp, -1),
            dsb.reshape(dp, -1),
            drate.reshape(dp, -1),
            dskip[:, :HEADS].reshape(dp, -1),
        ]
        bundle = jnp.concatenate(smalls + [jnp.zeros((dp, high * lanes - used), f32)], axis=1)
        grad_gate = plain_sum(normed, dgate)
        grad_out = plain_sum(no, cot)
        mine = lax.psum(lax.psum_scatter(bundle, "dp", scatter_dimension=0), "seq")
        grad_conv = jnp.concatenate([plain_sum(normed, gp), plain_sum(normed, draw)], axis=1)
        outs, at = [], 0
        for shape, size in zip(shapes, sizes):
            outs.append(mine[at : at + size].reshape(shape))
            at += size
    grad_in = jnp.concatenate([grad_gate, grad_conv[:, : CONV_CH + HEADS]], axis=1)
    return (
        mixed[None], grad_tokens[None], grad_in, grad_out, outs[0], outs[1],
        outs[2], outs[3], outs[4], outs[5], outs[6],
    )


def solution(mesh):
    return jax.shard_map(
        shards,
        mesh=mesh,
        in_specs=(
            P("dp", "seq", None), P("dp", "seq", None), P("dp", None), P("dp", None),
            P(None, "dp"), P("dp"), P("dp"), P("dp"), P("dp"), P("dp"), P("dp"),
        ),
        out_specs=(
            P("dp", "seq", None), P("dp", "seq", None), P("dp", None), P("dp", None),
            P(None, "dp"), P("dp"), P("dp"), P("dp"), P("dp"), P("dp"), P("dp"),
        ),
        check_vma=False,
    )
```

```python
import functools

import jax
import jax.numpy as jnp
from jax import lax
from jax.experimental import pallas as pl
from jax.experimental.pallas import tpu as pltpu
from jax.sharding import PartitionSpec as P

HEADS = 32
HEAD_DIM = 64
STATE = 128
CONV = 4
GROUP = 256
INNER = 2048
CONV_CH = 2304
EDGE = 16
TILE = 256
HPT = TILE // HEAD_DIM
TILES = INNER // TILE
LANES = 128

bf16 = jnp.bfloat16
f32 = jnp.float32
epsilon = 1e-05
VMEM_LIMIT = 24 * 1024 * 1024


def params(vmem=VMEM_LIMIT):
    return pltpu.CompilerParams(vmem_limit_bytes=vmem)


def mm(a, b, dims=((1,), (0,))):
    return lax.dot_general(a, b, (dims, ((), ())), preferred_element_type=f32)


NT = ((1,), (1,))
TN = ((0,), (0,))


def split3(v):
    hi = v.astype(bf16)
    rest = v - hi.astype(f32)
    mid = rest.astype(bf16)
    lo = (rest - mid.astype(f32)).astype(bf16)
    return hi, mid, lo


def split2(v):
    hi = v.astype(bf16)
    return hi, (v - hi.astype(f32)).astype(bf16)


def expander(tile):
    head = lax.broadcasted_iota(jnp.int32, (3 * HEADS, TILE), 0) % HEADS
    lane = lax.broadcasted_iota(jnp.int32, (3 * HEADS, TILE), 1)
    return (head == HPT * tile + lane // HEAD_DIM).astype(f32).astype(bf16)


def selector(tile):
    lane = lax.broadcasted_iota(jnp.int32, (TILE, LANES), 0)
    head = lax.broadcasted_iota(jnp.int32, (TILE, LANES), 1)
    return (head == HPT * tile + lane // HEAD_DIM).astype(f32).astype(bf16)


def head_sums(v, sel):
    hi, lo = split2(v)
    return mm(hi, sel) + mm(lo, sel)


def sigmoid(v):
    return 0.5 * jnp.tanh(0.5 * v) + 0.5


def shifted(p_ref, length):
    return [p_ref[pl.ds(EDGE - CONV + 1 + k, length), :] for k in range(CONV)]


def conv_of(rows, taps, shift):
    out = shift
    for k in range(CONV):
        out = out + rows[k] * taps[k : k + 1, :]
    return out


def tri(lower):
    r = lax.broadcasted_iota(jnp.int32, (GROUP, GROUP), 0)
    c = lax.broadcasted_iota(jnp.int32, (GROUP, GROUP), 1)
    return ((r >= c) if lower else (r <= c)).astype(f32).astype(bf16)


def lasts(cum3_ref, blocks):
    return jnp.concatenate(
        [cum3_ref[(b + 1) * GROUP - 1 : (b + 1) * GROUP, :] for b in range(blocks)], axis=0
    )


def front_kernel(blocks, p_ref, raw_ref, taps_ref, shift_ref, sb_ref, rate_ref, *outs):
    front_body(blocks, p_ref, raw_ref, taps_ref[...], shift_ref[...], sb_ref, rate_ref, *outs)


def front_body(
    blocks, p_ref, raw_ref, taps, shift, sb_ref, rate_ref,
    x_ref, w_ref, bs_ref, dev_ref, keys_ref, queries_ref, gmat_ref, gmat_t_ref,
    step3_ref, cum3_ref, cum_t_ref,
):
    length = blocks * GROUP
    at = pl.program_id(0)
    conv = conv_of(shifted(p_ref, length), taps, shift)
    act = conv * sigmoid(conv)

    @pl.when(at == 0)
    def _():
        keys = act[:, :STATE].astype(bf16)
        queries = act[:, STATE:].astype(bf16)
        keys_ref[...] = keys
        queries_ref[...] = queries
        z = raw_ref[EDGE:, :HEADS] + sb_ref[0:1, :]
        step = jnp.maximum(z, 0.0) + jnp.log1p(jnp.exp(-jnp.abs(z)))
        decays = -step * rate_ref[0:1, :]
        step3_ref[...] = jnp.concatenate(split3(step), axis=1)
        low = tri(True)
        for b in range(blocks):
            rows = slice(b * GROUP, (b + 1) * GROUP)
            gmat_ref[b] = mm(queries[rows], keys[rows], NT)
            gmat_t_ref[b] = mm(keys[rows], queries[rows], NT)
            parts = split3(decays[rows])
            cum = mm(low, parts[0]) + mm(low, parts[1]) + mm(low, parts[2])
            cum3_ref[rows, :] = jnp.concatenate(split3(cum), axis=1)
            cum_t_ref[:, rows] = sum(
                mm(part, low, ((0,), (1,))) for part in parts
            )

    @pl.when(at > 0)
    def _():
        spread = expander(at - 1)
        step = mm(step3_ref[...], spread)
        cum = mm(cum3_ref[...], spread)
        weighted = act * step
        x_ref[...] = act.astype(bf16)
        w_ref[...] = weighted.astype(bf16)
        ends = mm(spread, lasts(cum3_ref, blocks), ((0,), (1,)))
        total = None
        for b in range(blocks):
            rows = slice(b * GROUP, (b + 1) * GROUP)
            tails = jnp.exp(cum[(b + 1) * GROUP - 1 : (b + 1) * GROUP, :] - cum[rows])
            state = mm((weighted[rows] * tails).astype(bf16), keys_ref[rows, :], TN)
            bs_ref[b] = state
            total = state if total is None else jnp.exp(ends[:, b : b + 1]) * total + state
        dev_ref[0] = total.astype(bf16)
        whole = jnp.exp(sum(ends[:, b : b + 1] for b in range(blocks)))
        dev_ref[1] = jnp.broadcast_to(whole, total.shape).astype(bf16)


def front_outs(length):
    blocks = length // GROUP
    spec = pl.BlockSpec
    xt = lambda g: (0, jnp.maximum(g - 1, 0))
    whole2 = lambda g: (0, 0)
    whole3 = lambda g: (0, 0, 0)
    specs = [
        spec((length, TILE), xt),
        spec((length, TILE), xt),
        spec((blocks, TILE, STATE), lambda g: (0, jnp.maximum(g - 1, 0), 0)),
        spec((2, TILE, STATE), lambda g: (0, jnp.maximum(g - 1, 0), 0)),
        spec((length, STATE), whole2),
        spec((length, STATE), whole2),
        spec((blocks, GROUP, GROUP), whole3),
        spec((blocks, GROUP, GROUP), whole3),
        spec((length, 3 * HEADS), whole2),
        spec((length, 3 * HEADS), whole2),
        spec((HEADS, length), whole2),
    ]
    shapes = [
        jax.ShapeDtypeStruct((length, INNER), bf16),
        jax.ShapeDtypeStruct((length, INNER), bf16),
        jax.ShapeDtypeStruct((blocks, INNER, STATE), f32),
        jax.ShapeDtypeStruct((2, INNER, STATE), bf16),
        jax.ShapeDtypeStruct((length, STATE), bf16),
        jax.ShapeDtypeStruct((length, STATE), bf16),
        jax.ShapeDtypeStruct((blocks, GROUP, GROUP), f32),
        jax.ShapeDtypeStruct((blocks, GROUP, GROUP), f32),
        jax.ShapeDtypeStruct((length, 3 * HEADS), bf16),
        jax.ShapeDtypeStruct((length, 3 * HEADS), bf16),
        jax.ShapeDtypeStruct((HEADS, length), f32),
    ]
    return specs, shapes


def front(p, raw, taps, shift, sb, rate):
    length = p.shape[0] - EDGE
    tile = lambda g: (0, lax.rem(g + TILES, TILES + 1))
    whole2 = lambda g: (0, 0)
    specs, shapes = front_outs(length)
    return pl.pallas_call(
        functools.partial(front_kernel, length // GROUP),
        grid=(TILES + 1,),
        in_specs=[
            pl.BlockSpec((length + EDGE, TILE), tile),
            pl.BlockSpec((length + EDGE, LANES), whole2),
            pl.BlockSpec((CONV, TILE), tile),
            pl.BlockSpec((1, TILE), tile),
            pl.BlockSpec((1, HEADS), whole2),
            pl.BlockSpec((1, HEADS), whole2),
        ],
        out_specs=specs,
        out_shape=shapes,
        compiler_params=params(),
        cost_estimate=pl.CostEstimate(flops=600_000_000, bytes_accessed=14_000_000, transcendentals=4_000_000),
        name="front",
    )(p, raw, taps, shift, sb, rate)


def intra_kernel(blocks, w_ref, cum3_ref, cum_t_ref, gmat_ref, y_ref):
    at = pl.program_id(0)
    cum = mm(cum3_ref[...], expander(at))
    r = lax.broadcasted_iota(jnp.int32, (GROUP, GROUP), 0)
    c = lax.broadcasted_iota(jnp.int32, (GROUP, GROUP), 1)
    causal = r >= c
    first = lax.broadcasted_iota(jnp.int32, (GROUP, LANES), 1) < HEAD_DIM
    for b in range(blocks):
        rows = slice(b * GROUP, (b + 1) * GROUP)
        gmat = gmat_ref[b]
        for pair in range(HPT // 2):
            lanes = slice(pair * LANES, (pair + 1) * LANES)
            w = w_ref[rows, lanes]
            outs = []
            for side in range(2):
                j = 2 * pair + side
                col = cum[rows, j * HEAD_DIM : j * HEAD_DIM + 1]
                row = cum_t_ref[pl.ds(HPT * at + j, 1), rows]
                kernel = jnp.exp(jnp.where(causal, col - row, -1e30)) * gmat
                outs.append(mm(kernel.astype(bf16), w))
            y_ref[rows, lanes] = jnp.where(first, outs[0], outs[1])


def intra_of(w, cum3, cum_t, gmat):
    length = w.shape[0]
    blocks = length // GROUP
    tile = lambda g: (0, g)
    whole2 = lambda g: (0, 0)
    return pl.pallas_call(
        functools.partial(intra_kernel, blocks),
        grid=(TILES,),
        in_specs=[
            pl.BlockSpec((length, TILE), tile),
            pl.BlockSpec((length, 3 * HEADS), whole2),
            pl.BlockSpec((HEADS, length), whole2),
            pl.BlockSpec((blocks, GROUP, GROUP), lambda g: (0, 0, 0)),
        ],
        out_specs=pl.BlockSpec((length, TILE), tile),
        out_shape=jax.ShapeDtypeStruct((length, INNER), f32),
        compiler_params=params(),
        cost_estimate=pl.CostEstimate(flops=2_200_000_000, bytes_accessed=7_000_000, transcendentals=4_200_000),
        name="intra",
    )(w, cum3, cum_t, gmat)


def middle_kernel(
    blocks, y_ref, x_ref, gate_ref, gno_ref, q_ref, cum3_ref, start_ref, bs_ref, skip_ref, gain_ref,
    no_ref, dgate_ref, do_ref, dgain_ref, dskip_ref, rowsum_ref, dstart_ref, gdev_ref,
    y_s, sq_s, gt_s, r_s, m_s,
):
    length = blocks * GROUP
    phase, at = pl.program_id(0), pl.program_id(1)
    spread = expander(at)
    cum = mm(cum3_ref[...], spread)
    lanes = pl.ds(pl.multiple_of(at * TILE, TILE), TILE)
    x = x_ref[...].astype(f32)
    gate = gate_ref[...]
    sig = sigmoid(gate)
    gn = gno_ref[...]
    gain = gain_ref[0:1, :]
    skip = skip_ref[0:1, :]
    ends = jnp.exp(mm(spread, lasts(cum3_ref, blocks), ((0,), (1,))))

    @pl.when(phase == 0)
    def _():
        start = start_ref[...]
        for b in range(blocks):
            rows = slice(b * GROUP, (b + 1) * GROUP)
            inter = mm(q_ref[rows, :], start.astype(bf16), NT) * jnp.exp(cum[rows])
            y_s[rows, lanes] = y_ref[rows, :] + inter
            start = ends[:, b : b + 1] * start + bs_ref[b]
        gated = (y_s[:, lanes] + skip * x) * (gate * sig)
        sq = gated * gated
        gt = gated * gn * gain
        sq = sq[:, :LANES] + sq[:, LANES:]
        gt = gt[:, :LANES] + gt[:, LANES:]

        @pl.when(at == 0)
        def _():
            sq_s[...] = sq
            gt_s[...] = gt

        @pl.when(at > 0)
        def _():
            sq_s[...] += sq
            gt_s[...] += gt

    @pl.when(phase == 1)
    def _():
        @pl.when(at == 0)
        def _():
            r = lax.rsqrt(jnp.sum(sq_s[...], axis=1, keepdims=True) / INNER + epsilon)
            m = r * r * r * (jnp.sum(gt_s[...], axis=1, keepdims=True) / INNER)
            r_s[...] = jnp.broadcast_to(r, r_s.shape)
            m_s[...] = jnp.broadcast_to(m, m_s.shape)

        r = r_s[:, 0:1]
        m = m_s[:, 0:1]
        y = y_s[:, lanes]
        ssm = y + skip * x
        silu = gate * sig
        gated = ssm * silu
        scaled = gated * r
        no_ref[...] = (scaled * gain).astype(bf16)
        dgain_ref[...] = jnp.sum(gn * scaled, axis=0, keepdims=True)
        dgated = r * gn * gain - gated * m
        dgate_ref[...] = (dgated * ssm * (sig * (1.0 + gate * (1.0 - sig)))).astype(bf16)
        dof = dgated * silu
        dob = dof.astype(bf16)
        do_ref[...] = dob
        sums = head_sums(dob.astype(f32) * y, selector(at))
        skips = jnp.broadcast_to(jnp.sum(dof * x, axis=0, keepdims=True), (8, TILE))
        skips = head_sums(skips, selector(at))[0:1]

        @pl.when(at == 0)
        def _():
            rowsum_ref[...] = sums
            dskip_ref[...] = skips

        @pl.when(at > 0)
        def _():
            rowsum_ref[...] += sums
            dskip_ref[...] += skips

        scaled_do = (dof * jnp.exp(cum)).astype(bf16)
        total = None
        for b in reversed(range(blocks)):
            rows = slice(b * GROUP, (b + 1) * GROUP)
            d = mm(scaled_do[rows], q_ref[rows, :], TN)
            dstart_ref[b] = d
            total = d if total is None else ends[:, b : b + 1] * total + d
        gdev_ref[...] = total.astype(bf16)


def middle(y, x, gate, gno, q, cum3, start, bs, skip, gain):
    length = x.shape[0]
    blocks = length // GROUP
    both = lambda p, g: (0, g)
    ph0 = lambda p, g: (0, g * (1 - p) + (TILES - 1) * p)
    ph1 = lambda p, g: (0, g * p)
    whole2 = lambda p, g: (0, 0)
    return pl.pallas_call(
        functools.partial(middle_kernel, blocks),
        grid=(2, TILES),
        in_specs=[
            pl.BlockSpec((length, TILE), ph0),
            pl.BlockSpec((length, TILE), both),
            pl.BlockSpec((length, TILE), both),
            pl.BlockSpec((length, TILE), both),
            pl.BlockSpec((length, STATE), whole2),
            pl.BlockSpec((length, 3 * HEADS), whole2),
            pl.BlockSpec((TILE, STATE), lambda p, g: (g * (1 - p) + (TILES - 1) * p, 0)),
            pl.BlockSpec((blocks, TILE, STATE), lambda p, g: (0, g * (1 - p) + (TILES - 1) * p, 0)),
            pl.BlockSpec((1, TILE), both),
            pl.BlockSpec((1, TILE), both),
        ],
        out_specs=[
            pl.BlockSpec((length, TILE), ph1),
            pl.BlockSpec((length, TILE), ph1),
            pl.BlockSpec((length, TILE), ph1),
            pl.BlockSpec((1, TILE), ph1),
            pl.BlockSpec((1, LANES), whole2),
            pl.BlockSpec((length, LANES), whole2),
            pl.BlockSpec((blocks, TILE, STATE), lambda p, g: (0, g * p, 0)),
            pl.BlockSpec((TILE, STATE), lambda p, g: (g * p, 0)),
        ],
        out_shape=[
            jax.ShapeDtypeStruct((length, INNER), bf16),
            jax.ShapeDtypeStruct((length, INNER), bf16),
            jax.ShapeDtypeStruct((length, INNER), bf16),
            jax.ShapeDtypeStruct((1, INNER), f32),
            jax.ShapeDtypeStruct((1, LANES), f32),
            jax.ShapeDtypeStruct((length, LANES), f32),
            jax.ShapeDtypeStruct((blocks, INNER, STATE), f32),
            jax.ShapeDtypeStruct((INNER, STATE), bf16),
        ],
        scratch_shapes=[
            pltpu.VMEM((length, INNER), f32),
            pltpu.VMEM((length, LANES), f32),
            pltpu.VMEM((length, LANES), f32),
            pltpu.VMEM((length, LANES), f32),
            pltpu.VMEM((length, LANES), f32),
        ],
        compiler_params=params(),
        cost_estimate=pl.CostEstimate(flops=1_200_000_000, bytes_accessed=32_000_000, transcendentals=6_000_000),
        name="middle",
    )(y, x, gate, gno, q, cum3, start, bs, skip, gain)


def intra_back_kernel(
    blocks, w_ref, do_ref, cum3_ref, cum_t_ref, gmat_t_ref, k_ref, q_ref, dw_ref, dq_ref, dk_ref, dg_s
):
    at = pl.program_id(0)
    cum = mm(cum3_ref[...], expander(at))
    r = lax.broadcasted_iota(jnp.int32, (GROUP, GROUP), 0)
    c = lax.broadcasted_iota(jnp.int32, (GROUP, GROUP), 1)
    causal = c >= r
    first = lax.broadcasted_iota(jnp.int32, (GROUP, LANES), 1) < HEAD_DIM
    for b in range(blocks):
        rows = slice(b * GROUP, (b + 1) * GROUP)
        gmat = gmat_t_ref[b]
        dg = None
        for pair in range(HPT // 2):
            lanes = slice(pair * LANES, (pair + 1) * LANES)
            w = w_ref[rows, lanes]
            do = do_ref[rows, lanes]
            outs = []
            for side in range(2):
                j = 2 * pair + side
                col = cum[rows, j * HEAD_DIM : j * HEAD_DIM + 1]
                row = cum_t_ref[pl.ds(HPT * at + j, 1), rows]
                decay = jnp.exp(jnp.where(causal, row - col, -1e30))
                outs.append(mm((decay * gmat).astype(bf16), do))
                own = jnp.where(first if side == 0 else ~first, w, jnp.zeros_like(w))
                term = mm(own, do, NT) * decay
                dg = term if dg is None else dg + term
            dw_ref[rows, lanes] = jnp.where(first, outs[0], outs[1])

        @pl.when(at == 0)
        def _():
            dg_s[b] = dg

        @pl.when(at > 0)
        def _():
            dg_s[b] += dg

    @pl.when(at == TILES - 1)
    def _():
        for b in range(blocks):
            rows = slice(b * GROUP, (b + 1) * GROUP)
            dg = dg_s[b].astype(bf16)
            dk_ref[rows, :] = mm(dg, q_ref[rows, :])
            dq_ref[rows, :] = mm(dg, k_ref[rows, :], TN)


def intra_back(w, do, cum3, cum_t, gmat_t, k, q):
    length = w.shape[0]
    blocks = length // GROUP
    tile = lambda g: (0, g)
    whole2 = lambda g: (0, 0)
    return pl.pallas_call(
        functools.partial(intra_back_kernel, blocks),
        grid=(TILES,),
        in_specs=[
            pl.BlockSpec((length, TILE), tile),
            pl.BlockSpec((length, TILE), tile),
            pl.BlockSpec((length, 3 * HEADS), whole2),
            pl.BlockSpec((HEADS, length), whole2),
            pl.BlockSpec((blocks, GROUP, GROUP), lambda g: (0, 0, 0)),
            pl.BlockSpec((length, STATE), whole2),
            pl.BlockSpec((length, STATE), whole2),
        ],
        out_specs=[
            pl.BlockSpec((length, TILE), tile),
            pl.BlockSpec((length, STATE), whole2),
            pl.BlockSpec((length, STATE), whole2),
        ],
        out_shape=[
            jax.ShapeDtypeStruct((length, INNER), f32),
            jax.ShapeDtypeStruct((length, STATE), f32),
            jax.ShapeDtypeStruct((length, STATE), f32),
        ],
        scratch_shapes=[pltpu.VMEM((blocks, GROUP, GROUP), f32)],
        compiler_params=params(),
        cost_estimate=pl.CostEstimate(flops=4_400_000_000, bytes_accessed=10_000_000, transcendentals=4_200_000),
        name="intra_back",
    )(w, do, cum3, cum_t, gmat_t, k, q)


def back_kernel(
    blocks, p_ref, taps_ref, shift_ref, x_ref, w_ref, do_ref, dwi_ref, skip_ref,
    start_ref, bs_ref, adj_ref, dstart_ref,
    k_ref, q_ref, step3_ref, cum3_ref, dqi_ref, dki_ref, rowsum_ref, raw_ref, sb_ref, rate_ref,
    gp_ref, last_ref, before_ref, dtaps_ref, dshift_ref, draw_ref, dsb_ref, drate_ref,
    dq_s, dk_s, sx_s, sw_s, sv_s, dec_s, d_s,
):
    length = blocks * GROUP
    at = pl.program_id(0)

    @pl.when(at == 0)
    def _():
        dq_s[...] = dqi_ref[...]
        dk_s[...] = dki_ref[...]
        sx_s[...] = jnp.zeros_like(sx_s)
        sw_s[...] = jnp.zeros_like(sw_s)
        sv_s[...] = jnp.zeros_like(sv_s)
        dec_s[...] = jnp.zeros_like(dec_s)
        d_s[0:EDGE, :] = jnp.zeros((EDGE, TILE), f32)
        d_s[length + EDGE :, :] = jnp.zeros((EDGE, TILE), f32)

    def conv_back(dact):
        sources = shifted(p_ref, length)
        conv = conv_of(sources, taps_ref[...], shift_ref[...])
        sig = sigmoid(conv)
        dconv = dact * (sig * (1.0 + conv * (1.0 - sig)))
        d_s[EDGE : EDGE + length, :] = dconv
        dshift_ref[...] = jnp.sum(dconv, axis=0, keepdims=True)
        dp = None
        before = None
        for k in range(CONV):
            tap = taps_ref[k : k + 1, :]
            dtaps_ref[k : k + 1, :] = jnp.sum(dconv * sources[k], axis=0, keepdims=True)
            term = tap * d_s[pl.ds(EDGE + CONV - 1 - k, length), :]
            dp = term if dp is None else dp + term
            edge = tap * d_s[pl.ds(CONV - 1 - k, EDGE), :]
            before = edge if before is None else before + edge
        gp_ref[...] = dp.astype(bf16)
        last_ref[...] = dp[length - EDGE :, :]
        before_ref[...] = before

    @pl.when(at < TILES)
    def _():
        spread = expander(at)
        sel = selector(at)
        cum = mm(cum3_ref[...], spread)
        step = mm(step3_ref[...], spread)
        ends = jnp.exp(mm(spread, lasts(cum3_ref, blocks), ((0,), (1,))))
        x = x_ref[...].astype(f32)
        w = w_ref[...].astype(f32)
        do = do_ref[...].astype(f32)
        scaled_do = (do * jnp.exp(cum)).astype(bf16)
        starts = [start_ref[...]]
        for b in range(blocks - 1):
            starts.append(ends[:, b : b + 1] * starts[b] + bs_ref[b])
        adjs = [None] * blocks
        adj = adj_ref[...]
        for b in reversed(range(blocks)):
            adjs[b] = adj
            adj = ends[:, b : b + 1] * adj + dstart_ref[b]
        dws = []
        for b in range(blocks):
            rows = slice(b * GROUP, (b + 1) * GROUP)
            tails = jnp.exp(cum[(b + 1) * GROUP - 1 : (b + 1) * GROUP, :] - cum[rows])
            ab = adjs[b].astype(bf16)
            dws.append(tails * mm(k_ref[rows, :], ab, NT))
            dk_s[rows, :] += mm((w[rows] * tails).astype(bf16), ab)
            dq_s[rows, :] += mm(scaled_do[rows], starts[b].astype(bf16))
            both = jnp.sum(dws[b] * w[rows], axis=0, keepdims=True)
            sv_s[b : b + 1, :] += head_sums(jnp.broadcast_to(both, (8, TILE)), sel)[0:1]
            hi, lo = split2(ends[:, b : b + 1] * adjs[b] * starts[b])
            dec_s[b : b + 1, :] += jnp.sum(mm(hi, sel, TN) + mm(lo, sel, TN), axis=0, keepdims=True)
        dws = jnp.concatenate(dws, axis=0)
        dw = dwi_ref[...] + dws
        sx_s[...] += head_sums(dw * x, sel)
        sw_s[...] += head_sums(dw * w, sel)
        conv_back(dw * step + do * skip_ref[0:1, :])

    @pl.when(at == TILES)
    def _():
        conv_back(jnp.concatenate([dk_s[...], dq_s[...]], axis=1))
        dcum = (rowsum_ref[...] - sw_s[...])[:, :HEADS]
        z = raw_ref[EDGE:, :HEADS] + sb_ref[0:1, :]
        step = jnp.maximum(z, 0.0) + jnp.log1p(jnp.exp(-jnp.abs(z)))
        rate = rate_ref[0:1, :]
        up = tri(False)
        decays = []
        for b in range(blocks):
            rows = slice(b * GROUP, (b + 1) * GROUP)
            parts = split3(dcum[rows])
            extra = sv_s[b : b + 1, :HEADS] + dec_s[b : b + 1, :HEADS]
            decays.append(mm(up, parts[0]) + mm(up, parts[1]) + mm(up, parts[2]) + extra)
        ddecay = jnp.concatenate(decays, axis=0)
        dstep = sx_s[...][:, :HEADS] - ddecay * rate
        dz = dstep * sigmoid(z)
        draw_ref[...] = jnp.zeros_like(draw_ref)
        draw_ref[:, :HEADS] = dz.astype(bf16)
        dsb_ref[...] = jnp.sum(dz, axis=0, keepdims=True)
        drate_ref[...] = jnp.sum(-ddecay * step * rate, axis=0, keepdims=True)


def back(p, taps, shift, x, w, do, dwi, skip, start, bs, adj, dstart, k, q, step3, cum3, dqi, dki, rowsum, raw, sb, rate):
    length = x.shape[0]
    blocks = length // GROUP
    tile = lambda g: (0, g)
    xt = lambda g: (0, jnp.minimum(g, TILES - 1))
    st = lambda g: (jnp.minimum(g, TILES - 1), 0)
    st3 = lambda g: (0, jnp.minimum(g, TILES - 1), 0)
    whole2 = lambda g: (0, 0)
    spec = pl.BlockSpec
    return pl.pallas_call(
        functools.partial(back_kernel, blocks),
        grid=(TILES + 1,),
        in_specs=[
            spec((length + EDGE, TILE), tile),
            spec((CONV, TILE), tile),
            spec((1, TILE), tile),
            spec((length, TILE), xt),
            spec((length, TILE), xt),
            spec((length, TILE), xt),
            spec((length, TILE), xt),
            spec((1, TILE), xt),
            spec((TILE, STATE), st),
            spec((blocks, TILE, STATE), st3),
            spec((TILE, STATE), st),
            spec((blocks, TILE, STATE), st3),
            spec((length, STATE), whole2),
            spec((length, STATE), whole2),
            spec((length, 3 * HEADS), whole2),
            spec((length, 3 * HEADS), whole2),
            spec((length, STATE), whole2),
            spec((length, STATE), whole2),
            spec((length, LANES), whole2),
            spec((length + EDGE, LANES), lambda g: (0, 0)),
            spec((1, HEADS), whole2),
            spec((1, HEADS), whole2),
        ],
        out_specs=[
            spec((length, TILE), tile),
            spec((EDGE, TILE), tile),
            spec((EDGE, TILE), tile),
            spec((CONV, TILE), tile),
            spec((1, TILE), tile),
            spec((length, LANES), whole2),
            spec((1, HEADS), whole2),
            spec((1, HEADS), whole2),
        ],
        out_shape=[
            jax.ShapeDtypeStruct((length, CONV_CH), bf16),
            jax.ShapeDtypeStruct((EDGE, CONV_CH), f32),
            jax.ShapeDtypeStruct((EDGE, CONV_CH), f32),
            jax.ShapeDtypeStruct((CONV, CONV_CH), f32),
            jax.ShapeDtypeStruct((1, CONV_CH), f32),
            jax.ShapeDtypeStruct((length, LANES), bf16),
            jax.ShapeDtypeStruct((1, HEADS), f32),
            jax.ShapeDtypeStruct((1, HEADS), f32),
        ],
        scratch_shapes=[
            pltpu.VMEM((length, STATE), f32),
            pltpu.VMEM((length, STATE), f32),
            pltpu.VMEM((length, LANES), f32),
            pltpu.VMEM((length, LANES), f32),
            pltpu.VMEM((8, LANES), f32),
            pltpu.VMEM((8, LANES), f32),
            pltpu.VMEM((length + 2 * EDGE, TILE), f32),
        ],
        compiler_params=params(),
        cost_estimate=pl.CostEstimate(flops=2_500_000_000, bytes_accessed=32_000_000, transcendentals=6_000_000),
        name="back",
    )(p, taps, shift, x, w, do, dwi, skip, start, bs, adj, dstart, k, q, step3, cum3, dqi, dki, rowsum, raw, sb, rate)


def ring_ok():
    return lax.axis_size("dp") == 8 and lax.axis_size("seq") == 4


def spots():
    dp, seq = lax.axis_index("dp"), lax.axis_index("seq")
    return dp // 2, dp % 2, seq // 2, seq % 2


def over_y(a):
    return lax.ppermute(a, "dp", [(i, i ^ 1) for i in range(8)])


def over_z(a, k):
    return lax.ppermute(a, "dp", [(i, (i + 2 * k) % 8) for i in range(8)])


def over_x(a):
    return lax.ppermute(a, "seq", [(i, i ^ 2) for i in range(4)])


def over_core(a):
    return lax.ppermute(a, "seq", [(i, i ^ 1) for i in range(4)])


def assemble_kernel(rows, parts, *refs):
    assemble(rows, parts, refs[:13], refs[13:-1], refs[-1])


def assemble(rows, parts, pieces, outs, sem):
    own, a3, ay, b3, by, xb3, xby, ca3, cay, cb3, cby, cxb3, cxby = pieces
    z, y, x, c = spots()
    copies = []

    def put(src, dp, row, size):
        for out, (col, width, factor, base) in zip(outs_of, parts):
            copies.append(
                pltpu.make_async_copy(
                    src.at[:, pl.ds(col, width)],
                    out.at[pl.ds(pl.multiple_of(dp * (rows * factor) + base + row, 16), size), :],
                    sem.at[len(copies)],
                )
            )

    outs_of = [outs[part[4]] for part in parts]
    parts = [part[:4] for part in parts]
    put(own, z * 2 + y, 0, rows)
    half, fourth, eighth = rows // 2, rows // 4, rows // 8
    for k in range(4):
        zz = lax.rem(z + 4 - k, 4)
        for side in range(2):
            if k == 0 and side == 0:
                continue
            yy = y if side == 0 else 1 - y
            dp = zz * 2 + yy
            for core in range(2):
                cc = c if core == 0 else 1 - c
                src = ((a3, ay), (ca3, cay))[core][side]
                put(src.at[k - 1 if side == 0 else k], dp, cc * half, fourth)
                for far in range(2):
                    xx = x if far == 0 else 1 - x
                    src = (((b3, by), (xb3, xby)), ((cb3, cby), (cxb3, cxby)))[core][far][side]
                    put(
                        src.at[k - 1 if side == 0 else k],
                        dp,
                        cc * half + fourth + xx * eighth,
                        eighth,
                    )
    for copy in copies:
        copy.start()
    for copy in copies:
        copy.wait()


def gather_plain(pieces, parts):
    full = lax.all_gather(jnp.concatenate(pieces, axis=1), "dp")
    outs = []
    for out in sorted({part[4] for part in parts}):
        chosen = [full[:, :, p[0] : p[0] + p[1]] for p in parts if p[4] == out]
        outs.append(jnp.concatenate(chosen, axis=1).reshape(-1, chosen[0].shape[2]))
    return outs


def cut(pieces, start, size):
    return jnp.concatenate([lax.dynamic_slice_in_dim(p, start, size, 0) for p in pieces], axis=1)


def along_z(pieces, fourth_part):
    rows = pieces[0].shape[0]
    z, y, x, c = spots()
    if fourth_part:
        own = cut(pieces, c * (rows // 2), rows // 4)
    else:
        own = cut(pieces, c * (rows // 2) + rows // 4 + x * (rows // 8), rows // 8)
    return own, [over_z(own, k) for k in (1, 2, 3)]


def gather_pieces(pieces, a3, ay, b3, by, xb3, xby):
    sent = [a3, ay, b3, by, xb3, xby]
    return [jnp.concatenate(pieces, axis=1), *sent, *[over_core(a) for a in sent]]


def gather_end(pieces, parts, *staged):
    rows = pieces[0].shape[0]
    arrays = gather_pieces(pieces, *staged)
    shard = arrays[0]
    widths = {part[4]: part[1:3] for part in parts}
    shapes = [
        jax.ShapeDtypeStruct((8 * rows * widths[out][1], widths[out][0]), shard.dtype)
        for out in sorted(widths)
    ]
    anywhere = pl.BlockSpec(memory_space=pl.ANY)
    return pl.pallas_call(
        functools.partial(assemble_kernel, rows, parts),
        in_specs=[anywhere] * 13,
        out_specs=[pl.BlockSpec(memory_space=pltpu.VMEM)] * len(shapes),
        out_shape=shapes,
        scratch_shapes=[pltpu.SemaphoreType.DMA((len(parts) * (1 + 7 * 6),))],
        compiler_params=params(),
        cost_estimate=pl.CostEstimate(flops=0, bytes_accessed=32 * shard.size, transcendentals=0),
        name="assemble",
    )(*arrays)


SIDE = LANES - HEADS


def side_plan():
    plan = []
    for k in range(CONV):
        plan += [("taps", k, SIDE * j, SIDE, 3 * k + j) for j in range(3)]
    plan += [("shift", 0, SIDE * j, SIDE, 12 + j) for j in range(3)]
    plan += [("pre", 0, 0, SIDE, 15), ("pre", 0, SIDE, 32, 16)]
    plan += [("norm", 0, 0, SIDE, 17), ("norm", 0, SIDE, SIDE, 18), ("norm", 0, 2 * SIDE, 64, 19)]
    plan += [(name, 0, 0, 4, 20 + j) for j, name in enumerate(("bias", "rate", "skip"))]
    return plan


SIDE_WIDTH = {"taps": 288, "shift": 288, "pre": 128, "norm": 256, "bias": 4, "rate": 4, "skip": 4}


def pack_kernel(shards_in, names, left, *refs):
    out = refs[-1]
    out[...] = jnp.zeros_like(out)
    values = {name: ref[...].astype(f32) for name, ref in zip(names, refs)}
    values = {name: v if v.ndim == 2 else v.reshape(1, -1) for name, v in values.items()}
    for i in range(shards_in):
        for name, k, col, width, row in side_plan():
            if name in values:
                start = i * SIDE_WIDTH[name] + col
                out[i * 128 + row : i * 128 + row + 1, left : left + width] = values[name][
                    k : k + 1, start : start + width
                ]


def pack(shards_in, left, named):
    names = tuple(named)
    return pl.pallas_call(
        functools.partial(pack_kernel, shards_in, names, left),
        out_shape=jax.ShapeDtypeStruct((shards_in * 128, left + SIDE), f32),
        name="pack",
    )(*named.values())


def unpack_kernel(shards_in, names, in_ref, *refs):
    unpack_side(shards_in, dict(zip(names, refs)), in_ref[...].astype(f32))


def unpack_side(shards_in, outs, block):
    for i in range(shards_in):
        for name, k, col, width, row in side_plan():
            start = i * SIDE_WIDTH[name] + col
            outs[name][k : k + 1, start : start + width] = block[
                i * 128 + row : i * 128 + row + 1, HEADS : HEADS + width
            ]
    if "lanes" in outs:
        outs["rate"][...] = jnp.exp(outs["rate"][...])
        three = jnp.concatenate(split3(jnp.broadcast_to(outs["skip"][...], (8, HEADS))), axis=1)
        for tile in range(TILES):
            outs["lanes"][:, tile * TILE : (tile + 1) * TILE] = mm(three, expander(tile))[0:1]


SIDE_NAMES = ("taps", "shift", "pre", "norm", "bias", "rate", "skip", "lanes")


def enter_kernel(blocks, *refs):
    w_ref, side_ref, edge_ref, tok_ref, normed_ref, p_ref, raw_ref = refs[:7]
    side = dict(zip(SIDE_NAMES, refs[7:15]))
    fronts = refs[15:26]
    ext_s = refs[26]
    at = pl.program_id(0)

    @pl.when(at == 0)
    def _():
        unpack_side(8, side, side_ref[...].astype(f32))
        for ref, rows_at in ((edge_ref, slice(0, EDGE)), (tok_ref, slice(EDGE, None))):
            tok = ref[...].astype(f32)
            scale = lax.rsqrt(jnp.mean(tok * tok, axis=1, keepdims=True) + epsilon)
            ext_s[rows_at, :] = (tok * scale * side["pre"][...]).astype(bf16)
        normed_ref[...] = ext_s[EDGE:, :]
        raw_ref[...] = mm(ext_s[...], side_ref[...])

    lanes = pl.ds(pl.multiple_of(lax.rem(at + TILES, TILES + 1) * TILE, TILE), TILE)
    p_ref[...] = mm(ext_s[...], w_ref[...])
    front_body(
        blocks, p_ref, raw_ref, side["taps"][:, lanes], side["shift"][:, lanes], side["bias"], side["rate"],
        *fronts,
    )


def enter(weights, edge, toks):
    length, width = toks.shape
    whole2 = lambda g: (0, 0)
    tile = lambda g: (0, lax.rem(g + TILES, TILES + 1))
    shapes = [
        jax.ShapeDtypeStruct((length, width), bf16),
        jax.ShapeDtypeStruct((length + EDGE, CONV_CH), f32),
        jax.ShapeDtypeStruct((length + EDGE, LANES), f32),
    ]
    for name in SIDE_NAMES:
        lanes = INNER if name == "lanes" else 8 * SIDE_WIDTH[name]
        shapes.append(jax.ShapeDtypeStruct((CONV if name == "taps" else 1, lanes), f32))
    specs = [pl.BlockSpec(shape.shape, whole2) for shape in shapes]
    specs[1] = pl.BlockSpec((length + EDGE, TILE), tile)
    more_specs, more_shapes = front_outs(length)
    return pl.pallas_call(
        functools.partial(enter_kernel, length // GROUP),
        grid=(TILES + 1,),
        in_specs=[
            pl.BlockSpec((width, TILE), tile),
            pl.BlockSpec((width, LANES), lambda g: (0, CONV_CH // LANES)),
            pl.BlockSpec(edge.shape, whole2),
            pl.BlockSpec(toks.shape, whole2),
        ],
        out_specs=specs + more_specs,
        out_shape=shapes + more_shapes,
        scratch_shapes=[pltpu.VMEM((length + EDGE, width), bf16)],
        compiler_params=params(36 * 1024 * 1024),
        cost_estimate=pl.CostEstimate(
            flops=3_200_000_000, bytes_accessed=36_000_000, transcendentals=4_000_000
        ),
        name="enter",
    )(weights, weights, edge, toks)


def unpack(shards_in, side, names):
    shapes = []
    for name in names:
        width = INNER if name == "lanes" else shards_in * SIDE_WIDTH[name]
        shapes.append(jax.ShapeDtypeStruct((CONV if name == "taps" else 1, width), f32))
    whole = [pl.BlockSpec(shape.shape, lambda g: (0, 0)) for shape in shapes]
    return pl.pallas_call(
        functools.partial(unpack_kernel, shards_in, names),
        grid=(1,),
        in_specs=[pl.BlockSpec((shards_in * 128, LANES), lambda g: (0, 0))],
        out_specs=whole,
        out_shape=shapes,
        name="unpack",
    )(side)


def weight_grad_kernel(rows, plan, spot_ref, *refs):
    ka_ref, kb_ref, sa_ref, sb_ref, res = refs[-5:]
    y, x, c = spot_ref[1], spot_ref[2], spot_ref[3]
    at = 0
    for lhs, rhs, add, col, folds in plan:
        width = refs[rhs].shape[1]
        product = mm(refs[lhs][...], refs[rhs][...], TN)
        if add is not None:
            product = product + refs[add][...]
        for side in range(2):
            for fold in range(folds):
                top = (side * folds + fold) * rows
                left = col + fold * width
                res[side * rows : (side + 1) * rows, left : left + width] = product[top : top + rows]
    half, fourth, eighth = rows // 2, rows // 4, rows // 8
    for core, (a_ref, b_ref) in enumerate(((ka_ref, kb_ref), (sa_ref, sb_ref))):
        cc = c if core == 0 else 1 - c
        for side in range(2):
            yy = y if side == 0 else 1 - y
            at = yy * rows + cc * half
            a_ref[side, 0] = res[pl.ds(pl.multiple_of(at, fourth), fourth), :].astype(bf16)
            for far in range(2):
                xx = x if far == 0 else 1 - x
                b_ref[far, side, 0] = res[
                    pl.ds(pl.multiple_of(at + fourth + xx * eighth, eighth), eighth), :
                ].astype(bf16)


def weight_grads(rows, cols, arrays, plan):
    z, y, x, c = spots()
    spot = jnp.stack([z, y, x, c]).astype(jnp.int32)
    fourth, eighth = rows // 4, rows // 8
    a_spec = pl.BlockSpec((2, 1, fourth, cols), lambda k, s: (0, k, 0, 0))
    b_spec = pl.BlockSpec((2, 2, 1, eighth, cols), lambda k, s: (0, 0, k, 0, 0))
    a_shape = jax.ShapeDtypeStruct((2, 4, fourth, cols), bf16)
    b_shape = jax.ShapeDtypeStruct((2, 2, 4, eighth, cols), bf16)
    specs = []
    for array, kind in arrays:
        if kind == "lhs":
            specs.append(
                pl.BlockSpec((array.shape[0], array.shape[1] // 4), lambda k, s: (0, lax.rem(s[0] + k, 4)))
            )
        elif kind == "rhs":
            specs.append(pl.BlockSpec(array.shape, lambda k, s: (0, 0)))
        else:
            specs.append(
                pl.BlockSpec((array.shape[0] // 4, array.shape[1]), lambda k, s: (lax.rem(s[0] + k, 4), 0))
            )
    length = arrays[0][0].shape[0]
    return pl.pallas_call(
        functools.partial(weight_grad_kernel, rows, plan),
        grid_spec=pltpu.PrefetchScalarGridSpec(
            num_scalar_prefetch=1,
            grid=(4,),
            in_specs=specs,
            out_specs=[a_spec, b_spec, a_spec, b_spec],
            scratch_shapes=[pltpu.VMEM((2 * rows, cols), f32)],
        ),
        out_shape=[a_shape, b_shape, a_shape, b_shape],
        compiler_params=params((20 if cols > 3000 else 16) * 1024 * 1024),
        cost_estimate=pl.CostEstimate(
            flops=2 * length * 8 * rows * cols, bytes_accessed=20 * rows * cols, transcendentals=0
        ),
        name="weight_grads",
    )(spot, *[array for array, kind in arrays])


def plus(*terms):
    return sum(term.astype(f32) for term in terms).astype(bf16)


def sum_begin(ka, kb, sa, sb):
    ra, rb = over_core(sa), over_core(sb)
    return (plus(ka[1], ra[1]), plus(kb[1], rb[1])), (ka, kb, ra, rb)


def sum_next(got, held):
    ka, kb, ra, rb = held
    got_a, got_b = got
    u = [plus(ka[0, k], ra[0, k], got_a[k]) for k in range(4)]
    b_send = plus(kb[0, 1], rb[0, 1], got_b[1])
    return (u, b_send), (kb, rb, got_b)


def sum_third(sends):
    u, b_send = sends
    return over_y(b_send), u[0], [over_z(u[k], k) for k in (1, 2, 3)]


def sum_fourth(got, held):
    b_far, own, got_u = got
    kb, rb, got_b = held
    v = [plus(kb[0, 0, k], rb[0, 0, k], got_b[0, k], b_far[k]) for k in range(4)]
    fin_a = plus(own, *got_u)
    return fin_a, over_x(fin_a), v[0], [over_z(v[k], k) for k in (1, 2, 3)]


def sum_end(got):
    fin_a, other_a, v, got_v = got
    x, c = spots()[2:]
    eighth, cols = v.shape
    fin_b = plus(v, *got_v)
    other_b = over_x(fin_b)
    b_rows = jnp.where(x == 0, jnp.stack([fin_b, other_b]), jnp.stack([other_b, fin_b]))
    mine = jnp.concatenate([plus(fin_a, other_a), b_rows.reshape(2 * eighth, cols)], axis=0)
    other = over_core(mine)
    both = jnp.where(c == 0, jnp.stack([mine, other]), jnp.stack([other, mine]))
    return both.reshape(8 * eighth, cols).astype(f32)


def plain_sum(lhs, rhs):
    full = lax.dot_general(lhs, rhs, (TN, ((), ())), preferred_element_type=f32)
    part = lax.psum_scatter(full.astype(bf16), "dp", scatter_dimension=0, tiled=True)
    return lax.psum(part, "seq").astype(f32)


def carried(state, decay, mate_decay, axis, reverse):
    size, here = lax.axis_size(axis), lax.axis_index(axis)
    if mate_decay is not None:
        core = here % 2
        own, other = state.astype(f32), over_core(state).astype(f32)
        ahead = (core == 0) if reverse else (core == 1)
        mate_decay = mate_decay.astype(f32)
        pair = jnp.where(ahead, decay.astype(f32) * other + own, mate_decay * own + other).astype(bf16)
        route = [(2, 0), (3, 1)] if reverse else [(0, 2), (1, 3)]
        far = lax.ppermute(pair, axis, route).astype(f32)
        return jnp.where(ahead, other + mate_decay * far, far)
    states = lax.all_gather(state, axis)
    decays = lax.all_gather(decay[:, :1], axis).astype(f32)

    def one(lap, total):
        at = size - 1 - lap if reverse else lap
        use = at > here if reverse else at < here
        new = decays[at] * total + states[at].astype(f32)
        return jnp.where(use, new, total)

    return lax.fori_loop(0, size, one, jnp.zeros(state.shape, f32))


def rms_scale(values, gains):
    return values * lax.rsqrt(jnp.mean(values * values, axis=-1, keepdims=True) + epsilon) * gains


def shards(
    tokens, cotangent, in_weight, out_weight, conv_weight, conv_bias,
    pre_gain, norm_gain, step_bias, decay_log, skip_gain,
):
    dp = lax.axis_size("dp")
    seq = lax.axis_size("seq")
    toks = tokens[0]
    length = toks.shape[0]
    edge = lax.ppermute(toks[length - EDGE :], "seq", [(i, i + 1) for i in range(seq - 1)])
    ring = ring_ok()
    high = in_weight.shape[0]
    out_rows = out_weight.shape[0] // 2
    wide = out_weight.shape[1]
    first_parts = [(0, CONV_CH + LANES, 1, 0, 0)]
    then = [in_weight[:, :INNER], out_weight[:out_rows], out_weight[out_rows:]]
    then_parts = [(0, INNER, 1, 0, 0), (INNER, wide, 2, 0, 1), (INNER + wide, wide, 2, out_rows, 1)]
    if ring:
        named = {
            "taps": conv_weight, "shift": conv_bias, "pre": pre_gain, "norm": norm_gain,
            "bias": step_bias, "rate": decay_log, "skip": skip_gain,
        }
        first = [in_weight[:, INNER:], pack(1, 0, named).astype(bf16)]
        b0, bz = along_z(first, False)
        held = lax.optimization_barrier((*first, *bz))
        a0, az = along_z(held[:2], True)
        bz = list(held[2:])
        b3 = jnp.stack(bz)
        xb3 = over_x(b3)
        by = over_y(jnp.stack([b0] + bz))
        late_b = lax.optimization_barrier((*then, *az))
        az = list(late_b[3:])
        b0_2, bz_2 = along_z(late_b[:3], False)
        a3 = jnp.stack(az)
        ay = over_y(jnp.stack([a0] + az))
        late_a = lax.optimization_barrier((*then, by))
        by = late_a[3]
        a0_2, az_2 = along_z(late_a[:3], True)
        xby = over_x(by)
        ay, xb3, xby, bz_2, az_2[0] = lax.optimization_barrier((ay, xb3, xby, bz_2, az_2[0]))
        (conv_full,) = gather_end(first, first_parts, a3, ay, b3, by, xb3, xby)
        b3_2 = jnp.stack(bz_2)
        xb3_2 = over_x(b3_2)
        by_2 = over_y(jnp.stack([b0_2] + bz_2))
        conv_full, az_2, by_2 = lax.optimization_barrier((conv_full, az_2, by_2))
        xby_2 = over_x(by_2)
        a3_2 = jnp.stack(az_2)
        a4_2 = jnp.stack([a0_2] + az_2)
        ay_2 = over_y(a4_2)
    else:
        pieces = [conv_weight, conv_bias, pre_gain, norm_gain, step_bias, decay_log, skip_gain]
        shapes = [piece.shape for piece in pieces]
        sizes = [piece.size for piece in pieces]
        used = sum(sizes)
        lanes = -(-used // high)
        flat = jnp.concatenate(
            [piece.reshape(-1) for piece in pieces] + [jnp.zeros((high * lanes - used,), bf16)]
        )
        first = [
            in_weight[:, INNER:],
            flat.reshape(high, lanes),
            jnp.zeros((high, LANES - HEADS - lanes), bf16),
        ]
        (conv_full,) = gather_plain(first, first_parts)
        gate_full, out_full = gather_plain(then, then_parts)
        small = conv_full[:, CONV_CH + HEADS : CONV_CH + HEADS + lanes].reshape(dp, high * lanes)
        got, at = [], 0
        for shape, size in zip(shapes, sizes):
            got.append(small[:, at : at + size].reshape((dp,) + shape))
            at += size
        taps = jnp.moveaxis(got[0], 0, 1).reshape(CONV, CONV_CH).astype(f32)
        shift, gains_pre, gains_norm, bias_step, log_rates, skip = [
            piece.reshape(1, -1).astype(f32) for piece in got[1:]
        ]
        rate = jnp.exp(log_rates)
        skip_lanes = jnp.repeat(skip[0], HEAD_DIM)[None]

    if ring:
        entered = enter(conv_full, edge, toks)
        entered = list(entered)
        held = lax.optimization_barrier((entered[12], entered[14], ay_2, xb3_2, xby_2))
        entered[12], entered[14], ay_2, xb3_2, xby_2 = held
        normed, p, raw, taps, shift, gains_pre, gains_norm, bias_step, rate, _, skip_lanes = entered[:11]
        fronts = entered[11:]
    else:
        toks_ext = jnp.concatenate([edge, toks], axis=0)
        normed_ext = rms_scale(toks_ext.astype(f32), gains_pre).astype(bf16)
        normed = normed_ext[EDGE:]
        p = jnp.dot(normed_ext, conv_full[:, :CONV_CH], preferred_element_type=f32)
        raw = jnp.dot(normed_ext, conv_full[:, CONV_CH:], preferred_element_type=f32)
        fronts = front(p, raw, taps, shift, bias_step, rate)
    x, w, bs, dev, k, q, gmat, gmat_t, step3, cum3, cum_t = fronts
    mate_decay = over_core(dev[1]) if ring else None
    start = carried(dev[0], dev[1], mate_decay, "seq", False)
    y = intra_of(w, cum3, cum_t, gmat)
    if ring:
        gate_full, out_full = gather_end(then, then_parts, a3_2, ay_2, b3_2, by_2, xb3_2, xby_2)
    gate = jnp.dot(normed, gate_full, preferred_element_type=f32)
    cot = cotangent[0]
    gno = lax.dot_general(cot, out_full, (((1,), (1,)), ((), ())), preferred_element_type=f32)
    no, dgate, do, dgain, dskip, rowsum, dstart, gdev = middle(
        y, x, gate, gno, q, cum3, start, bs, skip_lanes, gains_norm
    )
    adj = carried(gdev, dev[1], mate_decay, "seq", True)
    rows = toks.astype(f32)
    mixed = (rows + jnp.dot(no, out_full, preferred_element_type=f32)).astype(bf16)
    if ring:
        early = weight_grads(
            high, INNER + 2 * wide,
            [(normed, "lhs"), (dgate, "rhs"), (no, "lhs"), (cot, "rhs")],
            [(0, 1, None, 0, 1), (2, 3, None, INNER, 2)],
        )
        sends, held = sum_begin(*early)
        (cum_t, sends) = lax.optimization_barrier((cum_t, sends))
        got = over_y(sends[0]), over_x(sends[1])
    over_cols = (((1,), (1,)), ((), ()))
    dnormed_gate = lax.dot_general(dgate, gate_full, over_cols, preferred_element_type=f32)
    inside = intra_back(w, do, cum3, cum_t, gmat_t, k, q)
    if ring:
        (dqi, got, mixed, dnormed_gate) = lax.optimization_barrier((inside[1], got, mixed, dnormed_gate))
        sends, held = sum_next(got, held)
        (dqi, sends) = lax.optimization_barrier((dqi, sends))
        got = sum_third(sends)
        inside = (inside[0], dqi, inside[2])
    dwi, dqi, dki = inside
    backs = back(
        p, taps, shift, x, w, do, dwi, skip_lanes, start, bs, adj, dstart,
        k, q, step3, cum3, dqi, dki, rowsum, raw, bias_step, rate,
    )
    if ring:
        backs = list(backs)
        (backs[1], backs[2], backs[3], got) = lax.optimization_barrier((backs[1], backs[2], backs[3], got))
        got = sum_fourth(got, held)
    gp, last, before, dtaps, dshift, draw, dsb, drate = backs
    returned = lax.ppermute(before, "seq", [(i + 1, i) for i in range(seq - 1)])
    gp = gp.at[length - EDGE :].set((last + returned).astype(bf16))
    if ring:
        named = {"taps": dtaps, "shift": dshift, "norm": dgain, "bias": dsb, "rate": drate, "skip": dskip}
        addend = pack(8, HEADS, named)
        late = weight_grads(
            high, CONV_CH + LANES,
            [(normed, "lhs"), (gp, "rhs"), (draw, "rhs"), (addend, "add")],
            [(0, 1, None, 0, 1), (0, 2, 3, CONV_CH, 1)],
        )
        late = list(late)
        late[2], late[3], got_v = lax.optimization_barrier((late[2], late[3], got[3]))
        got = (*got[:3], got_v)
        sends, late_held = sum_begin(*late)
        sends, gp, draw = lax.optimization_barrier((sends, gp, draw))
        late_got = over_y(sends[0]), over_x(sends[1])
    dnormed = (
        lax.dot_general(gp, conv_full[:, :CONV_CH], over_cols, preferred_element_type=f32)
        + dnormed_gate
        + lax.dot_general(draw, conv_full[:, CONV_CH:], over_cols, preferred_element_type=f32)
    )
    r = lax.rsqrt(jnp.mean(rows * rows, axis=-1, keepdims=True) + epsilon)
    t = dnormed * gains_pre
    drows = r * t - rows * (r * r * r * jnp.mean(rows * t, axis=-1, keepdims=True))
    grad_tokens = (cot.astype(f32) + drows).astype(bf16)
    if ring:
        (late_got, grad_tokens) = lax.optimization_barrier((late_got, grad_tokens))
        sends, late_held = sum_next(late_got, late_held)
        sends, got = lax.optimization_barrier((sends, got))
        late_got = sum_third(sends)
        early = sum_end(got)
        grad_gate = early[:, :INNER]
        grad_out = jnp.concatenate([early[:, INNER : INNER + wide], early[:, INNER + wide :]], axis=0)
        grad_conv = sum_end(sum_fourth(late_got, late_held))
        own_gate, own_conv = in_weight[:, :INNER], in_weight[:, INNER:]
        dpre = jnp.sum(own_gate.astype(f32) * grad_gate, axis=1) + jnp.sum(
            own_conv.astype(f32) * grad_conv[:, : CONV_CH + HEADS], axis=1
        )
        dpre = dpre / pre_gain.astype(f32)
        names = ("taps", "shift", "pre", "norm", "bias", "rate", "skip")
        outs = unpack(1, grad_conv[:, CONV_CH:], names)
        outs = [outs[0], outs[1][0], dpre, outs[3][0], outs[4][0], outs[5][0], outs[6][0]]
    else:
        dpre = jnp.sum(dnormed * rows * r, axis=0)
        smalls = [
            jnp.moveaxis(dtaps.reshape(CONV, dp, -1), 1, 0).reshape(dp, -1),
            dshift.reshape(dp, -1),
            dpre.reshape(dp, -1),
            dgain.reshape(dp, -1),
            dsb.reshape(dp, -1),
            drate.reshape(dp, -1),
            dskip[:, :HEADS].reshape(dp, -1),
        ]
        bundle = jnp.concatenate(smalls + [jnp.zeros((dp, high * lanes - used), f32)], axis=1)
        grad_gate = plain_sum(normed, dgate)
        grad_out = plain_sum(no, cot)
        mine = lax.psum(lax.psum_scatter(bundle, "dp", scatter_dimension=0), "seq")
        grad_conv = jnp.concatenate([plain_sum(normed, gp), plain_sum(normed, draw)], axis=1)
        outs, at = [], 0
        for shape, size in zip(shapes, sizes):
            outs.append(mine[at : at + size].reshape(shape))
            at += size
    grad_in = jnp.concatenate([grad_gate, grad_conv[:, : CONV_CH + HEADS]], axis=1)
    return (
        mixed[None], grad_tokens[None], grad_in, grad_out, outs[0], outs[1],
        outs[2], outs[3], outs[4], outs[5], outs[6],
    )


def solution(mesh):
    return jax.shard_map(
        shards,
        mesh=mesh,
        in_specs=(
            P("dp", "seq", None), P("dp", "seq", None), P("dp", None), P("dp", None),
            P(None, "dp"), P("dp"), P("dp"), P("dp"), P("dp"), P("dp"), P("dp"),
        ),
        out_specs=(
            P("dp", "seq", None), P("dp", "seq", None), P("dp", None), P("dp", None),
            P(None, "dp"), P("dp"), P("dp"), P("dp"), P("dp"), P("dp"), P("dp"),
        ),
        check_vma=False,
    )
```

```python
import functools

import jax
import jax.numpy as jnp
from jax import lax
from jax.experimental import pallas as pl
from jax.experimental.pallas import tpu as pltpu
from jax.sharding import PartitionSpec as P

HEADS = 32
HEAD_DIM = 64
STATE = 128
CONV = 4
GROUP = 256
INNER = 2048
CONV_CH = 2304
EDGE = 16
TILE = 256
HPT = TILE // HEAD_DIM
TILES = INNER // TILE
LANES = 128

bf16 = jnp.bfloat16
f32 = jnp.float32
epsilon = 1e-05
VMEM_LIMIT = 24 * 1024 * 1024


def params(vmem=VMEM_LIMIT):
    return pltpu.CompilerParams(vmem_limit_bytes=vmem)


def mm(a, b, dims=((1,), (0,))):
    return lax.dot_general(a, b, (dims, ((), ())), preferred_element_type=f32)


NT = ((1,), (1,))
TN = ((0,), (0,))


def split3(v):
    hi = v.astype(bf16)
    rest = v - hi.astype(f32)
    mid = rest.astype(bf16)
    lo = (rest - mid.astype(f32)).astype(bf16)
    return hi, mid, lo


def split2(v):
    hi = v.astype(bf16)
    return hi, (v - hi.astype(f32)).astype(bf16)


def expander(tile):
    head = lax.broadcasted_iota(jnp.int32, (3 * HEADS, TILE), 0) % HEADS
    lane = lax.broadcasted_iota(jnp.int32, (3 * HEADS, TILE), 1)
    return (head == HPT * tile + lane // HEAD_DIM).astype(f32).astype(bf16)


def selector(tile):
    lane = lax.broadcasted_iota(jnp.int32, (TILE, LANES), 0)
    head = lax.broadcasted_iota(jnp.int32, (TILE, LANES), 1)
    return (head == HPT * tile + lane // HEAD_DIM).astype(f32).astype(bf16)


def head_sums(v, sel):
    hi, lo = split2(v)
    return mm(hi, sel) + mm(lo, sel)


def sigmoid(v):
    return 0.5 * jnp.tanh(0.5 * v) + 0.5


def shifted(p_ref, length):
    return [p_ref[pl.ds(EDGE - CONV + 1 + k, length), :] for k in range(CONV)]


def conv_of(rows, taps, shift):
    out = shift
    for k in range(CONV):
        out = out + rows[k] * taps[k : k + 1, :]
    return out


def tri(lower):
    r = lax.broadcasted_iota(jnp.int32, (GROUP, GROUP), 0)
    c = lax.broadcasted_iota(jnp.int32, (GROUP, GROUP), 1)
    return ((r >= c) if lower else (r <= c)).astype(f32).astype(bf16)


def lasts(cum3_ref, blocks):
    return jnp.concatenate(
        [cum3_ref[(b + 1) * GROUP - 1 : (b + 1) * GROUP, :] for b in range(blocks)], axis=0
    )


def front_kernel(blocks, p_ref, raw_ref, taps_ref, shift_ref, sb_ref, rate_ref, *outs):
    front_body(blocks, p_ref, raw_ref, taps_ref[...], shift_ref[...], sb_ref, rate_ref, *outs)


def front_body(
    blocks, p_ref, raw_ref, taps, shift, sb_ref, rate_ref,
    x_ref, w_ref, bs_ref, dev_ref, keys_ref, queries_ref, gmat_ref, gmat_t_ref,
    step3_ref, cum3_ref, cum_t_ref,
):
    length = blocks * GROUP
    at = pl.program_id(0)
    conv = conv_of(shifted(p_ref, length), taps, shift)
    act = conv * sigmoid(conv)

    @pl.when(at == 0)
    def _():
        keys = act[:, :STATE].astype(bf16)
        queries = act[:, STATE:].astype(bf16)
        keys_ref[...] = keys
        queries_ref[...] = queries
        z = raw_ref[EDGE:, :HEADS] + sb_ref[0:1, :]
        step = jnp.maximum(z, 0.0) + jnp.log1p(jnp.exp(-jnp.abs(z)))
        decays = -step * rate_ref[0:1, :]
        step3_ref[...] = jnp.concatenate(split3(step), axis=1)
        low = tri(True)
        for b in range(blocks):
            rows = slice(b * GROUP, (b + 1) * GROUP)
            gmat_ref[b] = mm(queries[rows], keys[rows], NT)
            gmat_t_ref[b] = mm(keys[rows], queries[rows], NT)
            parts = split3(decays[rows])
            cum = mm(low, parts[0]) + mm(low, parts[1]) + mm(low, parts[2])
            cum3_ref[rows, :] = jnp.concatenate(split3(cum), axis=1)
            cum_t_ref[:, rows] = sum(
                mm(part, low, ((0,), (1,))) for part in parts
            )

    @pl.when(at > 0)
    def _():
        spread = expander(at - 1)
        step = mm(step3_ref[...], spread)
        cum = mm(cum3_ref[...], spread)
        weighted = act * step
        x_ref[...] = act.astype(bf16)
        w_ref[...] = weighted.astype(bf16)
        ends = mm(spread, lasts(cum3_ref, blocks), ((0,), (1,)))
        total = None
        for b in range(blocks):
            rows = slice(b * GROUP, (b + 1) * GROUP)
            tails = jnp.exp(cum[(b + 1) * GROUP - 1 : (b + 1) * GROUP, :] - cum[rows])
            state = mm((weighted[rows] * tails).astype(bf16), keys_ref[rows, :], TN)
            bs_ref[b] = state
            total = state if total is None else jnp.exp(ends[:, b : b + 1]) * total + state
        dev_ref[0] = total.astype(bf16)
        whole = jnp.exp(sum(ends[:, b : b + 1] for b in range(blocks)))
        dev_ref[1] = jnp.broadcast_to(whole, total.shape).astype(bf16)


def front_outs(length):
    blocks = length // GROUP
    spec = pl.BlockSpec
    xt = lambda g: (0, jnp.maximum(g - 1, 0))
    whole2 = lambda g: (0, 0)
    whole3 = lambda g: (0, 0, 0)
    specs = [
        spec((length, TILE), xt),
        spec((length, TILE), xt),
        spec((blocks, TILE, STATE), lambda g: (0, jnp.maximum(g - 1, 0), 0)),
        spec((2, TILE, STATE), lambda g: (0, jnp.maximum(g - 1, 0), 0)),
        spec((length, STATE), whole2),
        spec((length, STATE), whole2),
        spec((blocks, GROUP, GROUP), whole3),
        spec((blocks, GROUP, GROUP), whole3),
        spec((length, 3 * HEADS), whole2),
        spec((length, 3 * HEADS), whole2),
        spec((HEADS, length), whole2),
    ]
    shapes = [
        jax.ShapeDtypeStruct((length, INNER), bf16),
        jax.ShapeDtypeStruct((length, INNER), bf16),
        jax.ShapeDtypeStruct((blocks, INNER, STATE), f32),
        jax.ShapeDtypeStruct((2, INNER, STATE), bf16),
        jax.ShapeDtypeStruct((length, STATE), bf16),
        jax.ShapeDtypeStruct((length, STATE), bf16),
        jax.ShapeDtypeStruct((blocks, GROUP, GROUP), f32),
        jax.ShapeDtypeStruct((blocks, GROUP, GROUP), f32),
        jax.ShapeDtypeStruct((length, 3 * HEADS), bf16),
        jax.ShapeDtypeStruct((length, 3 * HEADS), bf16),
        jax.ShapeDtypeStruct((HEADS, length), f32),
    ]
    return specs, shapes


def front(p, raw, taps, shift, sb, rate):
    length = p.shape[0] - EDGE
    tile = lambda g: (0, lax.rem(g + TILES, TILES + 1))
    whole2 = lambda g: (0, 0)
    specs, shapes = front_outs(length)
    return pl.pallas_call(
        functools.partial(front_kernel, length // GROUP),
        grid=(TILES + 1,),
        in_specs=[
            pl.BlockSpec((length + EDGE, TILE), tile),
            pl.BlockSpec((length + EDGE, LANES), whole2),
            pl.BlockSpec((CONV, TILE), tile),
            pl.BlockSpec((1, TILE), tile),
            pl.BlockSpec((1, HEADS), whole2),
            pl.BlockSpec((1, HEADS), whole2),
        ],
        out_specs=specs,
        out_shape=shapes,
        compiler_params=params(),
        cost_estimate=pl.CostEstimate(flops=600_000_000, bytes_accessed=14_000_000, transcendentals=4_000_000),
        name="front",
    )(p, raw, taps, shift, sb, rate)


def intra_kernel(blocks, w_ref, cum3_ref, cum_t_ref, gmat_ref, y_ref):
    at = pl.program_id(0)
    cum = mm(cum3_ref[...], expander(at))
    r = lax.broadcasted_iota(jnp.int32, (GROUP, GROUP), 0)
    c = lax.broadcasted_iota(jnp.int32, (GROUP, GROUP), 1)
    causal = r >= c
    first = lax.broadcasted_iota(jnp.int32, (GROUP, LANES), 1) < HEAD_DIM
    for b in range(blocks):
        rows = slice(b * GROUP, (b + 1) * GROUP)
        gmat = gmat_ref[b]
        for pair in range(HPT // 2):
            lanes = slice(pair * LANES, (pair + 1) * LANES)
            w = w_ref[rows, lanes]
            outs = []
            for side in range(2):
                j = 2 * pair + side
                col = cum[rows, j * HEAD_DIM : j * HEAD_DIM + 1]
                row = cum_t_ref[pl.ds(HPT * at + j, 1), rows]
                kernel = jnp.exp(jnp.where(causal, col - row, -1e30)) * gmat
                outs.append(mm(kernel.astype(bf16), w))
            y_ref[rows, lanes] = jnp.where(first, outs[0], outs[1])


def intra_of(w, cum3, cum_t, gmat):
    length = w.shape[0]
    blocks = length // GROUP
    tile = lambda g: (0, g)
    whole2 = lambda g: (0, 0)
    return pl.pallas_call(
        functools.partial(intra_kernel, blocks),
        grid=(TILES,),
        in_specs=[
            pl.BlockSpec((length, TILE), tile),
            pl.BlockSpec((length, 3 * HEADS), whole2),
            pl.BlockSpec((HEADS, length), whole2),
            pl.BlockSpec((blocks, GROUP, GROUP), lambda g: (0, 0, 0)),
        ],
        out_specs=pl.BlockSpec((length, TILE), tile),
        out_shape=jax.ShapeDtypeStruct((length, INNER), f32),
        compiler_params=params(),
        cost_estimate=pl.CostEstimate(flops=2_200_000_000, bytes_accessed=7_000_000, transcendentals=4_200_000),
        name="intra",
    )(w, cum3, cum_t, gmat)


def middle_kernel(
    blocks, y_ref, x_ref, gate_ref, gno_ref, q_ref, cum3_ref, start_ref, bs_ref, skip_ref, gain_ref,
    no_ref, dgate_ref, do_ref, dgain_ref, dskip_ref, rowsum_ref, dstart_ref, gdev_ref,
    y_s, sq_s, gt_s, r_s, m_s,
):
    length = blocks * GROUP
    phase, at = pl.program_id(0), pl.program_id(1)
    spread = expander(at)
    cum = mm(cum3_ref[...], spread)
    lanes = pl.ds(pl.multiple_of(at * TILE, TILE), TILE)
    x = x_ref[...].astype(f32)
    gate = gate_ref[...]
    sig = sigmoid(gate)
    gn = gno_ref[...]
    gain = gain_ref[0:1, :]
    skip = skip_ref[0:1, :]
    ends = jnp.exp(mm(spread, lasts(cum3_ref, blocks), ((0,), (1,))))

    @pl.when(phase == 0)
    def _():
        start = start_ref[...]
        for b in range(blocks):
            rows = slice(b * GROUP, (b + 1) * GROUP)
            inter = mm(q_ref[rows, :], start.astype(bf16), NT) * jnp.exp(cum[rows])
            y_s[rows, lanes] = y_ref[rows, :] + inter
            start = ends[:, b : b + 1] * start + bs_ref[b]
        gated = (y_s[:, lanes] + skip * x) * (gate * sig)
        sq = gated * gated
        gt = gated * gn * gain
        sq = sq[:, :LANES] + sq[:, LANES:]
        gt = gt[:, :LANES] + gt[:, LANES:]

        @pl.when(at == 0)
        def _():
            sq_s[...] = sq
            gt_s[...] = gt

        @pl.when(at > 0)
        def _():
            sq_s[...] += sq
            gt_s[...] += gt

    @pl.when(phase == 1)
    def _():
        @pl.when(at == 0)
        def _():
            r = lax.rsqrt(jnp.sum(sq_s[...], axis=1, keepdims=True) / INNER + epsilon)
            m = r * r * r * (jnp.sum(gt_s[...], axis=1, keepdims=True) / INNER)
            r_s[...] = jnp.broadcast_to(r, r_s.shape)
            m_s[...] = jnp.broadcast_to(m, m_s.shape)

        r = r_s[:, 0:1]
        m = m_s[:, 0:1]
        y = y_s[:, lanes]
        ssm = y + skip * x
        silu = gate * sig
        gated = ssm * silu
        scaled = gated * r
        no_ref[...] = (scaled * gain).astype(bf16)
        dgain_ref[...] = jnp.sum(gn * scaled, axis=0, keepdims=True)
        dgated = r * gn * gain - gated * m
        dgate_ref[...] = (dgated * ssm * (sig * (1.0 + gate * (1.0 - sig)))).astype(bf16)
        dof = dgated * silu
        dob = dof.astype(bf16)
        do_ref[...] = dob
        sums = head_sums(dob.astype(f32) * y, selector(at))
        skips = jnp.broadcast_to(jnp.sum(dof * x, axis=0, keepdims=True), (8, TILE))
        skips = head_sums(skips, selector(at))[0:1]

        @pl.when(at == 0)
        def _():
            rowsum_ref[...] = sums
            dskip_ref[...] = skips

        @pl.when(at > 0)
        def _():
            rowsum_ref[...] += sums
            dskip_ref[...] += skips

        scaled_do = (dof * jnp.exp(cum)).astype(bf16)
        total = None
        for b in reversed(range(blocks)):
            rows = slice(b * GROUP, (b + 1) * GROUP)
            d = mm(scaled_do[rows], q_ref[rows, :], TN)
            dstart_ref[b] = d
            total = d if total is None else ends[:, b : b + 1] * total + d
        gdev_ref[...] = total.astype(bf16)


def middle(y, x, gate, gno, q, cum3, start, bs, skip, gain):
    length = x.shape[0]
    blocks = length // GROUP
    both = lambda p, g: (0, g)
    ph0 = lambda p, g: (0, g * (1 - p) + (TILES - 1) * p)
    ph1 = lambda p, g: (0, g * p)
    whole2 = lambda p, g: (0, 0)
    return pl.pallas_call(
        functools.partial(middle_kernel, blocks),
        grid=(2, TILES),
        in_specs=[
            pl.BlockSpec((length, TILE), ph0),
            pl.BlockSpec((length, TILE), both),
            pl.BlockSpec((length, TILE), both),
            pl.BlockSpec((length, TILE), both),
            pl.BlockSpec((length, STATE), whole2),
            pl.BlockSpec((length, 3 * HEADS), whole2),
            pl.BlockSpec((TILE, STATE), lambda p, g: (g * (1 - p) + (TILES - 1) * p, 0)),
            pl.BlockSpec((blocks, TILE, STATE), lambda p, g: (0, g * (1 - p) + (TILES - 1) * p, 0)),
            pl.BlockSpec((1, TILE), both),
            pl.BlockSpec((1, TILE), both),
        ],
        out_specs=[
            pl.BlockSpec((length, TILE), ph1),
            pl.BlockSpec((length, TILE), ph1),
            pl.BlockSpec((length, TILE), ph1),
            pl.BlockSpec((1, TILE), ph1),
            pl.BlockSpec((1, LANES), whole2),
            pl.BlockSpec((length, LANES), whole2),
            pl.BlockSpec((blocks, TILE, STATE), lambda p, g: (0, g * p, 0)),
            pl.BlockSpec((TILE, STATE), lambda p, g: (g * p, 0)),
        ],
        out_shape=[
            jax.ShapeDtypeStruct((length, INNER), bf16),
            jax.ShapeDtypeStruct((length, INNER), bf16),
            jax.ShapeDtypeStruct((length, INNER), bf16),
            jax.ShapeDtypeStruct((1, INNER), f32),
            jax.ShapeDtypeStruct((1, LANES), f32),
            jax.ShapeDtypeStruct((length, LANES), f32),
            jax.ShapeDtypeStruct((blocks, INNER, STATE), f32),
            jax.ShapeDtypeStruct((INNER, STATE), bf16),
        ],
        scratch_shapes=[
            pltpu.VMEM((length, INNER), f32),
            pltpu.VMEM((length, LANES), f32),
            pltpu.VMEM((length, LANES), f32),
            pltpu.VMEM((length, LANES), f32),
            pltpu.VMEM((length, LANES), f32),
        ],
        compiler_params=params(),
        cost_estimate=pl.CostEstimate(flops=1_200_000_000, bytes_accessed=32_000_000, transcendentals=6_000_000),
        name="middle",
    )(y, x, gate, gno, q, cum3, start, bs, skip, gain)


def intra_back_kernel(
    blocks, w_ref, do_ref, cum3_ref, cum_t_ref, gmat_t_ref, k_ref, q_ref, dw_ref, dq_ref, dk_ref, dg_s
):
    at = pl.program_id(0)
    cum = mm(cum3_ref[...], expander(at))
    r = lax.broadcasted_iota(jnp.int32, (GROUP, GROUP), 0)
    c = lax.broadcasted_iota(jnp.int32, (GROUP, GROUP), 1)
    causal = c >= r
    first = lax.broadcasted_iota(jnp.int32, (GROUP, LANES), 1) < HEAD_DIM
    for b in range(blocks):
        rows = slice(b * GROUP, (b + 1) * GROUP)
        gmat = gmat_t_ref[b]
        dg = None
        for pair in range(HPT // 2):
            lanes = slice(pair * LANES, (pair + 1) * LANES)
            w = w_ref[rows, lanes]
            do = do_ref[rows, lanes]
            outs = []
            for side in range(2):
                j = 2 * pair + side
                col = cum[rows, j * HEAD_DIM : j * HEAD_DIM + 1]
                row = cum_t_ref[pl.ds(HPT * at + j, 1), rows]
                decay = jnp.exp(jnp.where(causal, row - col, -1e30))
                outs.append(mm((decay * gmat).astype(bf16), do))
                own = jnp.where(first if side == 0 else ~first, w, jnp.zeros_like(w))
                term = mm(own, do, NT) * decay
                dg = term if dg is None else dg + term
            dw_ref[rows, lanes] = jnp.where(first, outs[0], outs[1])

        @pl.when(at == 0)
        def _():
            dg_s[b] = dg

        @pl.when(at > 0)
        def _():
            dg_s[b] += dg

    @pl.when(at == TILES - 1)
    def _():
        for b in range(blocks):
            rows = slice(b * GROUP, (b + 1) * GROUP)
            dg = dg_s[b].astype(bf16)
            dk_ref[rows, :] = mm(dg, q_ref[rows, :])
            dq_ref[rows, :] = mm(dg, k_ref[rows, :], TN)


def intra_back(w, do, cum3, cum_t, gmat_t, k, q):
    length = w.shape[0]
    blocks = length // GROUP
    tile = lambda g: (0, g)
    whole2 = lambda g: (0, 0)
    return pl.pallas_call(
        functools.partial(intra_back_kernel, blocks),
        grid=(TILES,),
        in_specs=[
            pl.BlockSpec((length, TILE), tile),
            pl.BlockSpec((length, TILE), tile),
            pl.BlockSpec((length, 3 * HEADS), whole2),
            pl.BlockSpec((HEADS, length), whole2),
            pl.BlockSpec((blocks, GROUP, GROUP), lambda g: (0, 0, 0)),
            pl.BlockSpec((length, STATE), whole2),
            pl.BlockSpec((length, STATE), whole2),
        ],
        out_specs=[
            pl.BlockSpec((length, TILE), tile),
            pl.BlockSpec((length, STATE), whole2),
            pl.BlockSpec((length, STATE), whole2),
        ],
        out_shape=[
            jax.ShapeDtypeStruct((length, INNER), f32),
            jax.ShapeDtypeStruct((length, STATE), f32),
            jax.ShapeDtypeStruct((length, STATE), f32),
        ],
        scratch_shapes=[pltpu.VMEM((blocks, GROUP, GROUP), f32)],
        compiler_params=params(),
        cost_estimate=pl.CostEstimate(flops=4_400_000_000, bytes_accessed=10_000_000, transcendentals=4_200_000),
        name="intra_back",
    )(w, do, cum3, cum_t, gmat_t, k, q)


def back_kernel(
    blocks, p_ref, taps_ref, shift_ref, x_ref, w_ref, do_ref, dwi_ref, skip_ref,
    start_ref, bs_ref, adj_ref, dstart_ref,
    k_ref, q_ref, step3_ref, cum3_ref, dqi_ref, dki_ref, rowsum_ref, raw_ref, sb_ref, rate_ref,
    gp_ref, last_ref, before_ref, dtaps_ref, dshift_ref, draw_ref, dsb_ref, drate_ref,
    dq_s, dk_s, sx_s, sw_s, sv_s, dec_s, d_s,
):
    length = blocks * GROUP
    at = pl.program_id(0)

    @pl.when(at == 0)
    def _():
        dq_s[...] = dqi_ref[...]
        dk_s[...] = dki_ref[...]
        sx_s[...] = jnp.zeros_like(sx_s)
        sw_s[...] = jnp.zeros_like(sw_s)
        sv_s[...] = jnp.zeros_like(sv_s)
        dec_s[...] = jnp.zeros_like(dec_s)
        d_s[0:EDGE, :] = jnp.zeros((EDGE, TILE), f32)
        d_s[length + EDGE :, :] = jnp.zeros((EDGE, TILE), f32)

    def conv_back(dact):
        sources = shifted(p_ref, length)
        conv = conv_of(sources, taps_ref[...], shift_ref[...])
        sig = sigmoid(conv)
        dconv = dact * (sig * (1.0 + conv * (1.0 - sig)))
        d_s[EDGE : EDGE + length, :] = dconv
        dshift_ref[...] = jnp.sum(dconv, axis=0, keepdims=True)
        dp = None
        before = None
        for k in range(CONV):
            tap = taps_ref[k : k + 1, :]
            dtaps_ref[k : k + 1, :] = jnp.sum(dconv * sources[k], axis=0, keepdims=True)
            term = tap * d_s[pl.ds(EDGE + CONV - 1 - k, length), :]
            dp = term if dp is None else dp + term
            edge = tap * d_s[pl.ds(CONV - 1 - k, EDGE), :]
            before = edge if before is None else before + edge
        gp_ref[...] = dp.astype(bf16)
        last_ref[...] = dp[length - EDGE :, :]
        before_ref[...] = before

    @pl.when(at < TILES)
    def _():
        spread = expander(at)
        sel = selector(at)
        cum = mm(cum3_ref[...], spread)
        step = mm(step3_ref[...], spread)
        ends = jnp.exp(mm(spread, lasts(cum3_ref, blocks), ((0,), (1,))))
        x = x_ref[...].astype(f32)
        w = w_ref[...].astype(f32)
        do = do_ref[...].astype(f32)
        scaled_do = (do * jnp.exp(cum)).astype(bf16)
        starts = [start_ref[...]]
        for b in range(blocks - 1):
            starts.append(ends[:, b : b + 1] * starts[b] + bs_ref[b])
        adjs = [None] * blocks
        adj = adj_ref[...]
        for b in reversed(range(blocks)):
            adjs[b] = adj
            adj = ends[:, b : b + 1] * adj + dstart_ref[b]
        dws = []
        for b in range(blocks):
            rows = slice(b * GROUP, (b + 1) * GROUP)
            tails = jnp.exp(cum[(b + 1) * GROUP - 1 : (b + 1) * GROUP, :] - cum[rows])
            ab = adjs[b].astype(bf16)
            dws.append(tails * mm(k_ref[rows, :], ab, NT))
            dk_s[rows, :] += mm((w[rows] * tails).astype(bf16), ab)
            dq_s[rows, :] += mm(scaled_do[rows], starts[b].astype(bf16))
            both = jnp.sum(dws[b] * w[rows], axis=0, keepdims=True)
            sv_s[b : b + 1, :] += head_sums(jnp.broadcast_to(both, (8, TILE)), sel)[0:1]
            hi, lo = split2(ends[:, b : b + 1] * adjs[b] * starts[b])
            dec_s[b : b + 1, :] += jnp.sum(mm(hi, sel, TN) + mm(lo, sel, TN), axis=0, keepdims=True)
        dws = jnp.concatenate(dws, axis=0)
        dw = dwi_ref[...] + dws
        sx_s[...] += head_sums(dw * x, sel)
        sw_s[...] += head_sums(dw * w, sel)
        conv_back(dw * step + do * skip_ref[0:1, :])

    @pl.when(at == TILES)
    def _():
        conv_back(jnp.concatenate([dk_s[...], dq_s[...]], axis=1))
        dcum = (rowsum_ref[...] - sw_s[...])[:, :HEADS]
        z = raw_ref[EDGE:, :HEADS] + sb_ref[0:1, :]
        step = jnp.maximum(z, 0.0) + jnp.log1p(jnp.exp(-jnp.abs(z)))
        rate = rate_ref[0:1, :]
        up = tri(False)
        decays = []
        for b in range(blocks):
            rows = slice(b * GROUP, (b + 1) * GROUP)
            parts = split3(dcum[rows])
            extra = sv_s[b : b + 1, :HEADS] + dec_s[b : b + 1, :HEADS]
            decays.append(mm(up, parts[0]) + mm(up, parts[1]) + mm(up, parts[2]) + extra)
        ddecay = jnp.concatenate(decays, axis=0)
        dstep = sx_s[...][:, :HEADS] - ddecay * rate
        dz = dstep * sigmoid(z)
        draw_ref[...] = jnp.zeros_like(draw_ref)
        draw_ref[:, :HEADS] = dz.astype(bf16)
        dsb_ref[...] = jnp.sum(dz, axis=0, keepdims=True)
        drate_ref[...] = jnp.sum(-ddecay * step * rate, axis=0, keepdims=True)


def back(p, taps, shift, x, w, do, dwi, skip, start, bs, adj, dstart, k, q, step3, cum3, dqi, dki, rowsum, raw, sb, rate):
    length = x.shape[0]
    blocks = length // GROUP
    tile = lambda g: (0, g)
    xt = lambda g: (0, jnp.minimum(g, TILES - 1))
    st = lambda g: (jnp.minimum(g, TILES - 1), 0)
    st3 = lambda g: (0, jnp.minimum(g, TILES - 1), 0)
    whole2 = lambda g: (0, 0)
    spec = pl.BlockSpec
    return pl.pallas_call(
        functools.partial(back_kernel, blocks),
        grid=(TILES + 1,),
        in_specs=[
            spec((length + EDGE, TILE), tile),
            spec((CONV, TILE), tile),
            spec((1, TILE), tile),
            spec((length, TILE), xt),
            spec((length, TILE), xt),
            spec((length, TILE), xt),
            spec((length, TILE), xt),
            spec((1, TILE), xt),
            spec((TILE, STATE), st),
            spec((blocks, TILE, STATE), st3),
            spec((TILE, STATE), st),
            spec((blocks, TILE, STATE), st3),
            spec((length, STATE), whole2),
            spec((length, STATE), whole2),
            spec((length, 3 * HEADS), whole2),
            spec((length, 3 * HEADS), whole2),
            spec((length, STATE), whole2),
            spec((length, STATE), whole2),
            spec((length, LANES), whole2),
            spec((length + EDGE, LANES), lambda g: (0, 0)),
            spec((1, HEADS), whole2),
            spec((1, HEADS), whole2),
        ],
        out_specs=[
            spec((length, TILE), tile),
            spec((EDGE, TILE), tile),
            spec((EDGE, TILE), tile),
            spec((CONV, TILE), tile),
            spec((1, TILE), tile),
            spec((length, LANES), whole2),
            spec((1, HEADS), whole2),
            spec((1, HEADS), whole2),
        ],
        out_shape=[
            jax.ShapeDtypeStruct((length, CONV_CH), bf16),
            jax.ShapeDtypeStruct((EDGE, CONV_CH), f32),
            jax.ShapeDtypeStruct((EDGE, CONV_CH), f32),
            jax.ShapeDtypeStruct((CONV, CONV_CH), f32),
            jax.ShapeDtypeStruct((1, CONV_CH), f32),
            jax.ShapeDtypeStruct((length, LANES), bf16),
            jax.ShapeDtypeStruct((1, HEADS), f32),
            jax.ShapeDtypeStruct((1, HEADS), f32),
        ],
        scratch_shapes=[
            pltpu.VMEM((length, STATE), f32),
            pltpu.VMEM((length, STATE), f32),
            pltpu.VMEM((length, LANES), f32),
            pltpu.VMEM((length, LANES), f32),
            pltpu.VMEM((8, LANES), f32),
            pltpu.VMEM((8, LANES), f32),
            pltpu.VMEM((length + 2 * EDGE, TILE), f32),
        ],
        compiler_params=params(),
        cost_estimate=pl.CostEstimate(flops=2_500_000_000, bytes_accessed=32_000_000, transcendentals=6_000_000),
        name="back",
    )(p, taps, shift, x, w, do, dwi, skip, start, bs, adj, dstart, k, q, step3, cum3, dqi, dki, rowsum, raw, sb, rate)


def ring_ok():
    return lax.axis_size("dp") == 8 and lax.axis_size("seq") == 4


def spots():
    dp, seq = lax.axis_index("dp"), lax.axis_index("seq")
    return dp // 2, dp % 2, seq // 2, seq % 2


def over_y(a):
    return lax.ppermute(a, "dp", [(i, i ^ 1) for i in range(8)])


def over_z(a, k):
    return lax.ppermute(a, "dp", [(i, (i + 2 * k) % 8) for i in range(8)])


def over_x(a):
    return lax.ppermute(a, "seq", [(i, i ^ 2) for i in range(4)])


def over_core(a):
    return lax.ppermute(a, "seq", [(i, i ^ 1) for i in range(4)])


def assemble_kernel(rows, parts, *refs):
    assemble(rows, parts, refs[:13], refs[13:-1], refs[-1])


def assemble(rows, parts, pieces, outs, sem):
    own, a3, ay, b3, by, xb3, xby, ca3, cay, cb3, cby, cxb3, cxby = pieces
    z, y, x, c = spots()
    copies = []

    def put(src, dp, row, size):
        for out, (col, width, factor, base) in zip(outs_of, parts):
            copies.append(
                pltpu.make_async_copy(
                    src.at[:, pl.ds(col, width)],
                    out.at[pl.ds(pl.multiple_of(dp * (rows * factor) + base + row, 16), size), :],
                    sem.at[len(copies)],
                )
            )

    outs_of = [outs[part[4]] for part in parts]
    parts = [part[:4] for part in parts]
    put(own, z * 2 + y, 0, rows)
    half, fourth, eighth = rows // 2, rows // 4, rows // 8
    for k in range(4):
        zz = lax.rem(z + 4 - k, 4)
        for side in range(2):
            if k == 0 and side == 0:
                continue
            yy = y if side == 0 else 1 - y
            dp = zz * 2 + yy
            for core in range(2):
                cc = c if core == 0 else 1 - c
                src = ((a3, ay), (ca3, cay))[core][side]
                put(src.at[k - 1 if side == 0 else k], dp, cc * half, fourth)
                for far in range(2):
                    xx = x if far == 0 else 1 - x
                    src = (((b3, by), (xb3, xby)), ((cb3, cby), (cxb3, cxby)))[core][far][side]
                    put(
                        src.at[k - 1 if side == 0 else k],
                        dp,
                        cc * half + fourth + xx * eighth,
                        eighth,
                    )
    for copy in copies:
        copy.start()
    for copy in copies:
        copy.wait()


def gather_plain(pieces, parts):
    full = lax.all_gather(jnp.concatenate(pieces, axis=1), "dp")
    outs = []
    for out in sorted({part[4] for part in parts}):
        chosen = [full[:, :, p[0] : p[0] + p[1]] for p in parts if p[4] == out]
        outs.append(jnp.concatenate(chosen, axis=1).reshape(-1, chosen[0].shape[2]))
    return outs


def cut(pieces, start, size):
    return jnp.concatenate([lax.dynamic_slice_in_dim(p, start, size, 0) for p in pieces], axis=1)


def along_z(pieces, fourth_part):
    rows = pieces[0].shape[0]
    z, y, x, c = spots()
    if fourth_part:
        own = cut(pieces, c * (rows // 2), rows // 4)
    else:
        own = cut(pieces, c * (rows // 2) + rows // 4 + x * (rows // 8), rows // 8)
    return own, [over_z(own, k) for k in (1, 2, 3)]


def gather_pieces(pieces, a3, ay, b3, by, xb3, xby):
    sent = [a3, ay, b3, by, xb3, xby]
    return [jnp.concatenate(pieces, axis=1), *sent, *[over_core(a) for a in sent]]


def gather_end(pieces, parts, *staged):
    rows = pieces[0].shape[0]
    arrays = gather_pieces(pieces, *staged)
    shard = arrays[0]
    widths = {part[4]: part[1:3] for part in parts}
    shapes = [
        jax.ShapeDtypeStruct((8 * rows * widths[out][1], widths[out][0]), shard.dtype)
        for out in sorted(widths)
    ]
    anywhere = pl.BlockSpec(memory_space=pl.ANY)
    return pl.pallas_call(
        functools.partial(assemble_kernel, rows, parts),
        in_specs=[anywhere] * 13,
        out_specs=[pl.BlockSpec(memory_space=pltpu.VMEM)] * len(shapes),
        out_shape=shapes,
        scratch_shapes=[pltpu.SemaphoreType.DMA((len(parts) * (1 + 7 * 6),))],
        compiler_params=params(),
        cost_estimate=pl.CostEstimate(flops=0, bytes_accessed=32 * shard.size, transcendentals=0),
        name="assemble",
    )(*arrays)


SIDE = LANES - HEADS


def side_plan():
    plan = []
    for k in range(CONV):
        plan += [("taps", k, SIDE * j, SIDE, 3 * k + j) for j in range(3)]
    plan += [("shift", 0, SIDE * j, SIDE, 12 + j) for j in range(3)]
    plan += [("pre", 0, 0, SIDE, 15), ("pre", 0, SIDE, 32, 16)]
    plan += [("norm", 0, 0, SIDE, 17), ("norm", 0, SIDE, SIDE, 18), ("norm", 0, 2 * SIDE, 64, 19)]
    plan += [(name, 0, 0, 4, 20 + j) for j, name in enumerate(("bias", "rate", "skip"))]
    return plan


SIDE_WIDTH = {"taps": 288, "shift": 288, "pre": 128, "norm": 256, "bias": 4, "rate": 4, "skip": 4}


def pack_kernel(shards_in, names, left, *refs):
    out = refs[-1]
    out[...] = jnp.zeros_like(out)
    values = {name: ref[...].astype(f32) for name, ref in zip(names, refs)}
    values = {name: v if v.ndim == 2 else v.reshape(1, -1) for name, v in values.items()}
    for i in range(shards_in):
        for name, k, col, width, row in side_plan():
            if name in values:
                start = i * SIDE_WIDTH[name] + col
                out[i * 128 + row : i * 128 + row + 1, left : left + width] = values[name][
                    k : k + 1, start : start + width
                ]


def pack(shards_in, left, named):
    names = tuple(named)
    return pl.pallas_call(
        functools.partial(pack_kernel, shards_in, names, left),
        out_shape=jax.ShapeDtypeStruct((shards_in * 128, left + SIDE), f32),
        name="pack",
    )(*named.values())


def unpack_kernel(shards_in, names, in_ref, *refs):
    unpack_side(shards_in, dict(zip(names, refs)), in_ref[...].astype(f32))


def unpack_side(shards_in, outs, block):
    for i in range(shards_in):
        for name, k, col, width, row in side_plan():
            start = i * SIDE_WIDTH[name] + col
            outs[name][k : k + 1, start : start + width] = block[
                i * 128 + row : i * 128 + row + 1, HEADS : HEADS + width
            ]
    if "lanes" in outs:
        outs["rate"][...] = jnp.exp(outs["rate"][...])
        three = jnp.concatenate(split3(jnp.broadcast_to(outs["skip"][...], (8, HEADS))), axis=1)
        for tile in range(TILES):
            outs["lanes"][:, tile * TILE : (tile + 1) * TILE] = mm(three, expander(tile))[0:1]


SIDE_NAMES = ("taps", "shift", "pre", "norm", "bias", "rate", "skip", "lanes")


def enter_kernel(blocks, *refs):
    w_ref, side_ref, edge_ref, tok_ref, normed_ref, p_ref, raw_ref = refs[:7]
    side = dict(zip(SIDE_NAMES, refs[7:15]))
    fronts = refs[15:26]
    ext_s = refs[26]
    at = pl.program_id(0)

    @pl.when(at == 0)
    def _():
        unpack_side(8, side, side_ref[...].astype(f32))
        for ref, rows_at in ((edge_ref, slice(0, EDGE)), (tok_ref, slice(EDGE, None))):
            tok = ref[...].astype(f32)
            scale = lax.rsqrt(jnp.mean(tok * tok, axis=1, keepdims=True) + epsilon)
            ext_s[rows_at, :] = (tok * scale * side["pre"][...]).astype(bf16)
        normed_ref[...] = ext_s[EDGE:, :]
        raw_ref[...] = mm(ext_s[...], side_ref[...])

    lanes = pl.ds(pl.multiple_of(lax.rem(at + TILES, TILES + 1) * TILE, TILE), TILE)
    p_ref[...] = mm(ext_s[...], w_ref[...])
    front_body(
        blocks, p_ref, raw_ref, side["taps"][:, lanes], side["shift"][:, lanes], side["bias"], side["rate"],
        *fronts,
    )


def enter(weights, edge, toks):
    length, width = toks.shape
    whole2 = lambda g: (0, 0)
    tile = lambda g: (0, lax.rem(g + TILES, TILES + 1))
    shapes = [
        jax.ShapeDtypeStruct((length, width), bf16),
        jax.ShapeDtypeStruct((length + EDGE, CONV_CH), f32),
        jax.ShapeDtypeStruct((length + EDGE, LANES), f32),
    ]
    for name in SIDE_NAMES:
        lanes = INNER if name == "lanes" else 8 * SIDE_WIDTH[name]
        shapes.append(jax.ShapeDtypeStruct((CONV if name == "taps" else 1, lanes), f32))
    specs = [pl.BlockSpec(shape.shape, whole2) for shape in shapes]
    specs[1] = pl.BlockSpec((length + EDGE, TILE), tile)
    more_specs, more_shapes = front_outs(length)
    return pl.pallas_call(
        functools.partial(enter_kernel, length // GROUP),
        grid=(TILES + 1,),
        in_specs=[
            pl.BlockSpec((width, TILE), tile),
            pl.BlockSpec((width, LANES), lambda g: (0, CONV_CH // LANES)),
            pl.BlockSpec(edge.shape, whole2),
            pl.BlockSpec(toks.shape, whole2),
        ],
        out_specs=specs + more_specs,
        out_shape=shapes + more_shapes,
        scratch_shapes=[pltpu.VMEM((length + EDGE, width), bf16)],
        compiler_params=params(36 * 1024 * 1024),
        cost_estimate=pl.CostEstimate(
            flops=3_200_000_000, bytes_accessed=36_000_000, transcendentals=4_000_000
        ),
        name="enter",
    )(weights, weights, edge, toks)


def unpack(shards_in, side, names):
    shapes = []
    for name in names:
        width = INNER if name == "lanes" else shards_in * SIDE_WIDTH[name]
        shapes.append(jax.ShapeDtypeStruct((CONV if name == "taps" else 1, width), f32))
    whole = [pl.BlockSpec(shape.shape, lambda g: (0, 0)) for shape in shapes]
    return pl.pallas_call(
        functools.partial(unpack_kernel, shards_in, names),
        grid=(1,),
        in_specs=[pl.BlockSpec((shards_in * 128, LANES), lambda g: (0, 0))],
        out_specs=whole,
        out_shape=shapes,
        name="unpack",
    )(side)


def weight_grad_kernel(rows, plan, spot_ref, *refs):
    ka_ref, kb_ref, sa_ref, sb_ref, res = refs[-5:]
    y, x, c = spot_ref[1], spot_ref[2], spot_ref[3]
    at = 0
    for lhs, rhs, add, col, folds in plan:
        width = refs[rhs].shape[1]
        product = mm(refs[lhs][...], refs[rhs][...], TN)
        if add is not None:
            product = product + refs[add][...]
        for side in range(2):
            for fold in range(folds):
                top = (side * folds + fold) * rows
                left = col + fold * width
                res[side * rows : (side + 1) * rows, left : left + width] = product[top : top + rows]
    half, fourth, eighth = rows // 2, rows // 4, rows // 8
    for core, (a_ref, b_ref) in enumerate(((ka_ref, kb_ref), (sa_ref, sb_ref))):
        cc = c if core == 0 else 1 - c
        for side in range(2):
            yy = y if side == 0 else 1 - y
            at = yy * rows + cc * half
            a_ref[side, 0] = res[pl.ds(pl.multiple_of(at, fourth), fourth), :].astype(bf16)
            for far in range(2):
                xx = x if far == 0 else 1 - x
                b_ref[far, side, 0] = res[
                    pl.ds(pl.multiple_of(at + fourth + xx * eighth, eighth), eighth), :
                ].astype(bf16)


def weight_grads(rows, cols, arrays, plan):
    z, y, x, c = spots()
    spot = jnp.stack([z, y, x, c]).astype(jnp.int32)
    fourth, eighth = rows // 4, rows // 8
    a_spec = pl.BlockSpec((2, 1, fourth, cols), lambda k, s: (0, k, 0, 0))
    b_spec = pl.BlockSpec((2, 2, 1, eighth, cols), lambda k, s: (0, 0, k, 0, 0))
    a_shape = jax.ShapeDtypeStruct((2, 4, fourth, cols), bf16)
    b_shape = jax.ShapeDtypeStruct((2, 2, 4, eighth, cols), bf16)
    specs = []
    for array, kind in arrays:
        if kind == "lhs":
            specs.append(
                pl.BlockSpec((array.shape[0], array.shape[1] // 4), lambda k, s: (0, lax.rem(s[0] + k, 4)))
            )
        elif kind == "rhs":
            specs.append(pl.BlockSpec(array.shape, lambda k, s: (0, 0)))
        else:
            specs.append(
                pl.BlockSpec((array.shape[0] // 4, array.shape[1]), lambda k, s: (lax.rem(s[0] + k, 4), 0))
            )
    length = arrays[0][0].shape[0]
    return pl.pallas_call(
        functools.partial(weight_grad_kernel, rows, plan),
        grid_spec=pltpu.PrefetchScalarGridSpec(
            num_scalar_prefetch=1,
            grid=(4,),
            in_specs=specs,
            out_specs=[a_spec, b_spec, a_spec, b_spec],
            scratch_shapes=[pltpu.VMEM((2 * rows, cols), f32)],
        ),
        out_shape=[a_shape, b_shape, a_shape, b_shape],
        compiler_params=params((20 if cols > 3000 else 16) * 1024 * 1024),
        cost_estimate=pl.CostEstimate(
            flops=2 * length * 8 * rows * cols, bytes_accessed=20 * rows * cols, transcendentals=0
        ),
        name="weight_grads",
    )(spot, *[array for array, kind in arrays])


def plus(*terms):
    return sum(term.astype(f32) for term in terms).astype(bf16)


def sum_begin(ka, kb, sa, sb):
    ra, rb = over_core(sa), over_core(sb)
    return (plus(ka[1], ra[1]), plus(kb[1], rb[1])), (ka, kb, ra, rb)


def sum_next(got, held):
    ka, kb, ra, rb = held
    got_a, got_b = got
    u = [plus(ka[0, k], ra[0, k], got_a[k]) for k in range(4)]
    b_send = plus(kb[0, 1], rb[0, 1], got_b[1])
    return (u, b_send), (kb, rb, got_b)


def sum_third(sends):
    u, b_send = sends
    return over_y(b_send), u[0], [over_z(u[k], k) for k in (1, 2, 3)]


def sum_fourth(got, held):
    b_far, own, got_u = got
    kb, rb, got_b = held
    v = [plus(kb[0, 0, k], rb[0, 0, k], got_b[0, k], b_far[k]) for k in range(4)]
    fin_a = plus(own, *got_u)
    return fin_a, over_x(fin_a), v[0], [over_z(v[k], k) for k in (1, 2, 3)]


def sum_end(got):
    fin_a, other_a, v, got_v = got
    x, c = spots()[2:]
    eighth, cols = v.shape
    fin_b = plus(v, *got_v)
    other_b = over_x(fin_b)
    b_rows = jnp.where(x == 0, jnp.stack([fin_b, other_b]), jnp.stack([other_b, fin_b]))
    mine = jnp.concatenate([plus(fin_a, other_a), b_rows.reshape(2 * eighth, cols)], axis=0)
    other = over_core(mine)
    both = jnp.where(c == 0, jnp.stack([mine, other]), jnp.stack([other, mine]))
    return both.reshape(8 * eighth, cols).astype(f32)


def turn_kernel(gate_ref, conv_ref, out_ref):
    wide = gate_ref.shape[1]
    for col in range(0, wide, LANES):
        out_ref[col : col + LANES, :] = gate_ref[:, col : col + LANES].T
    for col in range(0, CONV_CH, LANES):
        out_ref[wide + col : wide + col + LANES, :] = conv_ref[:, col : col + LANES].T
    out_ref[wide + CONV_CH :, :] = conv_ref[:, CONV_CH:].T[:HEADS]


def turned(gate, conv):
    return pl.pallas_call(
        turn_kernel,
        out_shape=jax.ShapeDtypeStruct((gate.shape[1] + CONV_CH + HEADS, gate.shape[0]), f32),
        compiler_params=params(16 * 1024 * 1024),
        name="turned",
    )(gate, conv).T


def plain_sum(lhs, rhs):
    full = lax.dot_general(lhs, rhs, (TN, ((), ())), preferred_element_type=f32)
    part = lax.psum_scatter(full.astype(bf16), "dp", scatter_dimension=0, tiled=True)
    return lax.psum(part, "seq").astype(f32)


def carried(state, decay, mate_decay, axis, reverse):
    size, here = lax.axis_size(axis), lax.axis_index(axis)
    if mate_decay is not None:
        core = here % 2
        own, other = state.astype(f32), over_core(state).astype(f32)
        ahead = (core == 0) if reverse else (core == 1)
        mate_decay = mate_decay.astype(f32)
        pair = jnp.where(ahead, decay.astype(f32) * other + own, mate_decay * own + other).astype(bf16)
        route = [(2, 0), (3, 1)] if reverse else [(0, 2), (1, 3)]
        far = lax.ppermute(pair, axis, route).astype(f32)
        return jnp.where(ahead, other + mate_decay * far, far)
    states = lax.all_gather(state, axis)
    decays = lax.all_gather(decay[:, :1], axis).astype(f32)

    def one(lap, total):
        at = size - 1 - lap if reverse else lap
        use = at > here if reverse else at < here
        new = decays[at] * total + states[at].astype(f32)
        return jnp.where(use, new, total)

    return lax.fori_loop(0, size, one, jnp.zeros(state.shape, f32))


def rms_scale(values, gains):
    return values * lax.rsqrt(jnp.mean(values * values, axis=-1, keepdims=True) + epsilon) * gains


def shards(
    tokens, cotangent, in_weight, out_weight, conv_weight, conv_bias,
    pre_gain, norm_gain, step_bias, decay_log, skip_gain,
):
    dp = lax.axis_size("dp")
    seq = lax.axis_size("seq")
    toks = tokens[0]
    length = toks.shape[0]
    edge = lax.ppermute(toks[length - EDGE :], "seq", [(i, i + 1) for i in range(seq - 1)])
    ring = ring_ok()
    high = in_weight.shape[0]
    out_rows = out_weight.shape[0] // 2
    wide = out_weight.shape[1]
    first_parts = [(0, CONV_CH + LANES, 1, 0, 0)]
    then = [in_weight[:, :INNER], out_weight[:out_rows], out_weight[out_rows:]]
    then_parts = [(0, INNER, 1, 0, 0), (INNER, wide, 2, 0, 1), (INNER + wide, wide, 2, out_rows, 1)]
    if ring:
        named = {
            "taps": conv_weight, "shift": conv_bias, "pre": pre_gain, "norm": norm_gain,
            "bias": step_bias, "rate": decay_log, "skip": skip_gain,
        }
        first = [in_weight[:, INNER:], pack(1, 0, named).astype(bf16)]
        b0, bz = along_z(first, False)
        held = lax.optimization_barrier((*first, *bz))
        a0, az = along_z(held[:2], True)
        bz = list(held[2:])
        b3 = jnp.stack(bz)
        xb3 = over_x(b3)
        by = over_y(jnp.stack([b0] + bz))
        late_b = lax.optimization_barrier((*then, *az))
        az = list(late_b[3:])
        b0_2, bz_2 = along_z(late_b[:3], False)
        a3 = jnp.stack(az)
        ay = over_y(jnp.stack([a0] + az))
        late_a = lax.optimization_barrier((*then, by))
        by = late_a[3]
        a0_2, az_2 = along_z(late_a[:3], True)
        xby = over_x(by)
        ay, xb3, xby, bz_2, az_2[0] = lax.optimization_barrier((ay, xb3, xby, bz_2, az_2[0]))
        (conv_full,) = gather_end(first, first_parts, a3, ay, b3, by, xb3, xby)
        b3_2 = jnp.stack(bz_2)
        xb3_2 = over_x(b3_2)
        by_2 = over_y(jnp.stack([b0_2] + bz_2))
        conv_full, az_2, by_2 = lax.optimization_barrier((conv_full, az_2, by_2))
        xby_2 = over_x(by_2)
        a3_2 = jnp.stack(az_2)
        a4_2 = jnp.stack([a0_2] + az_2)
        ay_2 = over_y(a4_2)
    else:
        pieces = [conv_weight, conv_bias, pre_gain, norm_gain, step_bias, decay_log, skip_gain]
        shapes = [piece.shape for piece in pieces]
        sizes = [piece.size for piece in pieces]
        used = sum(sizes)
        lanes = -(-used // high)
        flat = jnp.concatenate(
            [piece.reshape(-1) for piece in pieces] + [jnp.zeros((high * lanes - used,), bf16)]
        )
        first = [
            in_weight[:, INNER:],
            flat.reshape(high, lanes),
            jnp.zeros((high, LANES - HEADS - lanes), bf16),
        ]
        (conv_full,) = gather_plain(first, first_parts)
        gate_full, out_full = gather_plain(then, then_parts)
        small = conv_full[:, CONV_CH + HEADS : CONV_CH + HEADS + lanes].reshape(dp, high * lanes)
        got, at = [], 0
        for shape, size in zip(shapes, sizes):
            got.append(small[:, at : at + size].reshape((dp,) + shape))
            at += size
        taps = jnp.moveaxis(got[0], 0, 1).reshape(CONV, CONV_CH).astype(f32)
        shift, gains_pre, gains_norm, bias_step, log_rates, skip = [
            piece.reshape(1, -1).astype(f32) for piece in got[1:]
        ]
        rate = jnp.exp(log_rates)
        skip_lanes = jnp.repeat(skip[0], HEAD_DIM)[None]

    if ring:
        entered = enter(conv_full, edge, toks)
        entered = list(entered)
        held = lax.optimization_barrier((entered[12], entered[14], ay_2, xb3_2, xby_2))
        entered[12], entered[14], ay_2, xb3_2, xby_2 = held
        normed, p, raw, taps, shift, gains_pre, gains_norm, bias_step, rate, _, skip_lanes = entered[:11]
        fronts = entered[11:]
    else:
        toks_ext = jnp.concatenate([edge, toks], axis=0)
        normed_ext = rms_scale(toks_ext.astype(f32), gains_pre).astype(bf16)
        normed = normed_ext[EDGE:]
        p = jnp.dot(normed_ext, conv_full[:, :CONV_CH], preferred_element_type=f32)
        raw = jnp.dot(normed_ext, conv_full[:, CONV_CH:], preferred_element_type=f32)
        fronts = front(p, raw, taps, shift, bias_step, rate)
    x, w, bs, dev, k, q, gmat, gmat_t, step3, cum3, cum_t = fronts
    mate_decay = over_core(dev[1]) if ring else None
    start = carried(dev[0], dev[1], mate_decay, "seq", False)
    y = intra_of(w, cum3, cum_t, gmat)
    if ring:
        gate_full, out_full = gather_end(then, then_parts, a3_2, ay_2, b3_2, by_2, xb3_2, xby_2)
    gate = jnp.dot(normed, gate_full, preferred_element_type=f32)
    cot = cotangent[0]
    gno = lax.dot_general(cot, out_full, (((1,), (1,)), ((), ())), preferred_element_type=f32)
    no, dgate, do, dgain, dskip, rowsum, dstart, gdev = middle(
        y, x, gate, gno, q, cum3, start, bs, skip_lanes, gains_norm
    )
    adj = carried(gdev, dev[1], mate_decay, "seq", True)
    rows = toks.astype(f32)
    mixed = (rows + jnp.dot(no, out_full, preferred_element_type=f32)).astype(bf16)
    if ring:
        early = weight_grads(
            high, INNER + 2 * wide,
            [(normed, "lhs"), (dgate, "rhs"), (no, "lhs"), (cot, "rhs")],
            [(0, 1, None, 0, 1), (2, 3, None, INNER, 2)],
        )
        sends, held = sum_begin(*early)
        (cum_t, sends) = lax.optimization_barrier((cum_t, sends))
        got = over_y(sends[0]), over_x(sends[1])
    over_cols = (((1,), (1,)), ((), ()))
    dnormed_gate = lax.dot_general(dgate, gate_full, over_cols, preferred_element_type=f32)
    inside = intra_back(w, do, cum3, cum_t, gmat_t, k, q)
    if ring:
        (dqi, got, mixed, dnormed_gate) = lax.optimization_barrier((inside[1], got, mixed, dnormed_gate))
        sends, held = sum_next(got, held)
        (dqi, sends) = lax.optimization_barrier((dqi, sends))
        got = sum_third(sends)
        inside = (inside[0], dqi, inside[2])
    dwi, dqi, dki = inside
    backs = back(
        p, taps, shift, x, w, do, dwi, skip_lanes, start, bs, adj, dstart,
        k, q, step3, cum3, dqi, dki, rowsum, raw, bias_step, rate,
    )
    if ring:
        backs = list(backs)
        (backs[1], backs[2], backs[3], got) = lax.optimization_barrier((backs[1], backs[2], backs[3], got))
        got = sum_fourth(got, held)
    gp, last, before, dtaps, dshift, draw, dsb, drate = backs
    returned = lax.ppermute(before, "seq", [(i + 1, i) for i in range(seq - 1)])
    gp = gp.at[length - EDGE :].set((last + returned).astype(bf16))
    if ring:
        named = {"taps": dtaps, "shift": dshift, "norm": dgain, "bias": dsb, "rate": drate, "skip": dskip}
        addend = pack(8, HEADS, named)
        late = weight_grads(
            high, CONV_CH + LANES,
            [(normed, "lhs"), (gp, "rhs"), (draw, "rhs"), (addend, "add")],
            [(0, 1, None, 0, 1), (0, 2, 3, CONV_CH, 1)],
        )
        late = list(late)
        late[2], late[3], got_v = lax.optimization_barrier((late[2], late[3], got[3]))
        got = (*got[:3], got_v)
        sends, late_held = sum_begin(*late)
        sends, gp, draw = lax.optimization_barrier((sends, gp, draw))
        late_got = over_y(sends[0]), over_x(sends[1])
    dnormed = (
        lax.dot_general(gp, conv_full[:, :CONV_CH], over_cols, preferred_element_type=f32)
        + dnormed_gate
        + lax.dot_general(draw, conv_full[:, CONV_CH:], over_cols, preferred_element_type=f32)
    )
    r = lax.rsqrt(jnp.mean(rows * rows, axis=-1, keepdims=True) + epsilon)
    t = dnormed * gains_pre
    drows = r * t - rows * (r * r * r * jnp.mean(rows * t, axis=-1, keepdims=True))
    grad_tokens = (cot.astype(f32) + drows).astype(bf16)
    if ring:
        (late_got, grad_tokens) = lax.optimization_barrier((late_got, grad_tokens))
        sends, late_held = sum_next(late_got, late_held)
        sends, got = lax.optimization_barrier((sends, got))
        late_got = sum_third(sends)
        early = sum_end(got)
        grad_gate = early[:, :INNER]
        grad_out = jnp.concatenate([early[:, INNER : INNER + wide], early[:, INNER + wide :]], axis=0)
        grad_conv = sum_end(sum_fourth(late_got, late_held))
        own_gate, own_conv = in_weight[:, :INNER], in_weight[:, INNER:]
        dpre = jnp.sum(own_gate.astype(f32) * grad_gate, axis=1) + jnp.sum(
            own_conv.astype(f32) * grad_conv[:, : CONV_CH + HEADS], axis=1
        )
        dpre = dpre / pre_gain.astype(f32)
        names = ("taps", "shift", "pre", "norm", "bias", "rate", "skip")
        outs = unpack(1, grad_conv[:, CONV_CH:], names)
        outs = [outs[0], outs[1][0], dpre, outs[3][0], outs[4][0], outs[5][0], outs[6][0]]
    else:
        dpre = jnp.sum(dnormed * rows * r, axis=0)
        smalls = [
            jnp.moveaxis(dtaps.reshape(CONV, dp, -1), 1, 0).reshape(dp, -1),
            dshift.reshape(dp, -1),
            dpre.reshape(dp, -1),
            dgain.reshape(dp, -1),
            dsb.reshape(dp, -1),
            drate.reshape(dp, -1),
            dskip[:, :HEADS].reshape(dp, -1),
        ]
        bundle = jnp.concatenate(smalls + [jnp.zeros((dp, high * lanes - used), f32)], axis=1)
        grad_gate = plain_sum(normed, dgate)
        grad_out = plain_sum(no, cot)
        mine = lax.psum(lax.psum_scatter(bundle, "dp", scatter_dimension=0), "seq")
        grad_conv = jnp.concatenate([plain_sum(normed, gp), plain_sum(normed, draw)], axis=1)
        outs, at = [], 0
        for shape, size in zip(shapes, sizes):
            outs.append(mine[at : at + size].reshape(shape))
            at += size
    if ring:
        grad_in = turned(grad_gate, grad_conv)
    else:
        grad_in = jnp.concatenate([grad_gate, grad_conv[:, : CONV_CH + HEADS]], axis=1)
    return (
        mixed[None], grad_tokens[None], grad_in, grad_out, outs[0], outs[1],
        outs[2], outs[3], outs[4], outs[5], outs[6],
    )


def solution(mesh):
    return jax.shard_map(
        shards,
        mesh=mesh,
        in_specs=(
            P("dp", "seq", None), P("dp", "seq", None), P("dp", None), P("dp", None),
            P(None, "dp"), P("dp"), P("dp"), P("dp"), P("dp"), P("dp"), P("dp"),
        ),
        out_specs=(
            P("dp", "seq", None), P("dp", "seq", None), P("dp", None), P("dp", None),
            P(None, "dp"), P("dp"), P("dp"), P("dp"), P("dp"), P("dp"), P("dp"),
        ),
        check_vma=False,
    )
```

```python
import functools

import jax
import jax.numpy as jnp
from jax import lax
from jax.experimental import pallas as pl
from jax.experimental.pallas import tpu as pltpu
from jax.sharding import PartitionSpec as P

HEADS = 32
HEAD_DIM = 64
STATE = 128
CONV = 4
GROUP = 256
INNER = 2048
CONV_CH = 2304
EDGE = 16
TILE = 256
HPT = TILE // HEAD_DIM
TILES = INNER // TILE
LANES = 128

bf16 = jnp.bfloat16
f32 = jnp.float32
epsilon = 1e-05
VMEM_LIMIT = 24 * 1024 * 1024


def params(vmem=VMEM_LIMIT):
    return pltpu.CompilerParams(vmem_limit_bytes=vmem)


def mm(a, b, dims=((1,), (0,))):
    return lax.dot_general(a, b, (dims, ((), ())), preferred_element_type=f32)


NT = ((1,), (1,))
TN = ((0,), (0,))


def split3(v):
    hi = v.astype(bf16)
    rest = v - hi.astype(f32)
    mid = rest.astype(bf16)
    lo = (rest - mid.astype(f32)).astype(bf16)
    return hi, mid, lo


def split2(v):
    hi = v.astype(bf16)
    return hi, (v - hi.astype(f32)).astype(bf16)


def expander(tile):
    head = lax.broadcasted_iota(jnp.int32, (3 * HEADS, TILE), 0) % HEADS
    lane = lax.broadcasted_iota(jnp.int32, (3 * HEADS, TILE), 1)
    return (head == HPT * tile + lane // HEAD_DIM).astype(f32).astype(bf16)


def selector(tile):
    lane = lax.broadcasted_iota(jnp.int32, (TILE, LANES), 0)
    head = lax.broadcasted_iota(jnp.int32, (TILE, LANES), 1)
    return (head == HPT * tile + lane // HEAD_DIM).astype(f32).astype(bf16)


def head_sums(v, sel):
    hi, lo = split2(v)
    return mm(hi, sel) + mm(lo, sel)


def sigmoid(v):
    return 0.5 * jnp.tanh(0.5 * v) + 0.5


def shifted(p_ref, length):
    return [p_ref[pl.ds(EDGE - CONV + 1 + k, length), :] for k in range(CONV)]


def conv_of(rows, taps, shift):
    out = shift
    for k in range(CONV):
        out = out + rows[k] * taps[k : k + 1, :]
    return out


def tri(lower):
    r = lax.broadcasted_iota(jnp.int32, (GROUP, GROUP), 0)
    c = lax.broadcasted_iota(jnp.int32, (GROUP, GROUP), 1)
    return ((r >= c) if lower else (r <= c)).astype(f32).astype(bf16)


def lasts(cum3_ref, blocks):
    return jnp.concatenate(
        [cum3_ref[(b + 1) * GROUP - 1 : (b + 1) * GROUP, :] for b in range(blocks)], axis=0
    )


def front_kernel(blocks, p_ref, raw_ref, taps_ref, shift_ref, sb_ref, rate_ref, *outs):
    front_body(blocks, p_ref, raw_ref, taps_ref[...], shift_ref[...], sb_ref, rate_ref, *outs)


def front_body(
    blocks, p_ref, raw_ref, taps, shift, sb_ref, rate_ref,
    x_ref, w_ref, bs_ref, dev_ref, keys_ref, queries_ref, gmat_ref, gmat_t_ref,
    step3_ref, cum3_ref, cum_t_ref,
):
    length = blocks * GROUP
    at = pl.program_id(0)
    conv = conv_of(shifted(p_ref, length), taps, shift)
    act = conv * sigmoid(conv)

    @pl.when(at == 0)
    def _():
        keys = act[:, :STATE].astype(bf16)
        queries = act[:, STATE:].astype(bf16)
        keys_ref[...] = keys
        queries_ref[...] = queries
        z = raw_ref[EDGE:, :HEADS] + sb_ref[0:1, :]
        step = jnp.maximum(z, 0.0) + jnp.log1p(jnp.exp(-jnp.abs(z)))
        decays = -step * rate_ref[0:1, :]
        step3_ref[...] = jnp.concatenate(split3(step), axis=1)
        low = tri(True)
        for b in range(blocks):
            rows = slice(b * GROUP, (b + 1) * GROUP)
            gmat_ref[b] = mm(queries[rows], keys[rows], NT)
            gmat_t_ref[b] = mm(keys[rows], queries[rows], NT)
            parts = split3(decays[rows])
            cum = mm(low, parts[0]) + mm(low, parts[1]) + mm(low, parts[2])
            cum3_ref[rows, :] = jnp.concatenate(split3(cum), axis=1)
            cum_t_ref[:, rows] = sum(
                mm(part, low, ((0,), (1,))) for part in parts
            )

    @pl.when(at > 0)
    def _():
        spread = expander(at - 1)
        step = mm(step3_ref[...], spread)
        cum = mm(cum3_ref[...], spread)
        weighted = act * step
        x_ref[...] = act.astype(bf16)
        w_ref[...] = weighted.astype(bf16)
        ends = mm(spread, lasts(cum3_ref, blocks), ((0,), (1,)))
        total = None
        for b in range(blocks):
            rows = slice(b * GROUP, (b + 1) * GROUP)
            tails = jnp.exp(cum[(b + 1) * GROUP - 1 : (b + 1) * GROUP, :] - cum[rows])
            state = mm((weighted[rows] * tails).astype(bf16), keys_ref[rows, :], TN)
            bs_ref[b] = state
            total = state if total is None else jnp.exp(ends[:, b : b + 1]) * total + state
        dev_ref[0] = total.astype(bf16)
        whole = jnp.exp(sum(ends[:, b : b + 1] for b in range(blocks)))
        dev_ref[1] = jnp.broadcast_to(whole, total.shape).astype(bf16)


def front_outs(length):
    blocks = length // GROUP
    spec = pl.BlockSpec
    xt = lambda g: (0, jnp.maximum(g - 1, 0))
    whole2 = lambda g: (0, 0)
    whole3 = lambda g: (0, 0, 0)
    specs = [
        spec((length, TILE), xt),
        spec((length, TILE), xt),
        spec((blocks, TILE, STATE), lambda g: (0, jnp.maximum(g - 1, 0), 0)),
        spec((2, TILE, STATE), lambda g: (0, jnp.maximum(g - 1, 0), 0)),
        spec((length, STATE), whole2),
        spec((length, STATE), whole2),
        spec((blocks, GROUP, GROUP), whole3),
        spec((blocks, GROUP, GROUP), whole3),
        spec((length, 3 * HEADS), whole2),
        spec((length, 3 * HEADS), whole2),
        spec((HEADS, length), whole2),
    ]
    shapes = [
        jax.ShapeDtypeStruct((length, INNER), bf16),
        jax.ShapeDtypeStruct((length, INNER), bf16),
        jax.ShapeDtypeStruct((blocks, INNER, STATE), f32),
        jax.ShapeDtypeStruct((2, INNER, STATE), bf16),
        jax.ShapeDtypeStruct((length, STATE), bf16),
        jax.ShapeDtypeStruct((length, STATE), bf16),
        jax.ShapeDtypeStruct((blocks, GROUP, GROUP), f32),
        jax.ShapeDtypeStruct((blocks, GROUP, GROUP), f32),
        jax.ShapeDtypeStruct((length, 3 * HEADS), bf16),
        jax.ShapeDtypeStruct((length, 3 * HEADS), bf16),
        jax.ShapeDtypeStruct((HEADS, length), f32),
    ]
    return specs, shapes


def front(p, raw, taps, shift, sb, rate):
    length = p.shape[0] - EDGE
    tile = lambda g: (0, lax.rem(g + TILES, TILES + 1))
    whole2 = lambda g: (0, 0)
    specs, shapes = front_outs(length)
    return pl.pallas_call(
        functools.partial(front_kernel, length // GROUP),
        grid=(TILES + 1,),
        in_specs=[
            pl.BlockSpec((length + EDGE, TILE), tile),
            pl.BlockSpec((length + EDGE, LANES), whole2),
            pl.BlockSpec((CONV, TILE), tile),
            pl.BlockSpec((1, TILE), tile),
            pl.BlockSpec((1, HEADS), whole2),
            pl.BlockSpec((1, HEADS), whole2),
        ],
        out_specs=specs,
        out_shape=shapes,
        compiler_params=params(),
        cost_estimate=pl.CostEstimate(flops=600_000_000, bytes_accessed=14_000_000, transcendentals=4_000_000),
        name="front",
    )(p, raw, taps, shift, sb, rate)


def intra_kernel(blocks, w_ref, cum3_ref, cum_t_ref, gmat_ref, y_ref):
    at = pl.program_id(0)
    cum = mm(cum3_ref[...], expander(at))
    r = lax.broadcasted_iota(jnp.int32, (GROUP, GROUP), 0)
    c = lax.broadcasted_iota(jnp.int32, (GROUP, GROUP), 1)
    causal = r >= c
    first = lax.broadcasted_iota(jnp.int32, (GROUP, LANES), 1) < HEAD_DIM
    for b in range(blocks):
        rows = slice(b * GROUP, (b + 1) * GROUP)
        gmat = gmat_ref[b]
        for pair in range(HPT // 2):
            lanes = slice(pair * LANES, (pair + 1) * LANES)
            w = w_ref[rows, lanes]
            outs = []
            for side in range(2):
                j = 2 * pair + side
                col = cum[rows, j * HEAD_DIM : j * HEAD_DIM + 1]
                row = cum_t_ref[pl.ds(HPT * at + j, 1), rows]
                kernel = jnp.exp(jnp.where(causal, col - row, -1e30)) * gmat
                outs.append(mm(kernel.astype(bf16), w))
            y_ref[rows, lanes] = jnp.where(first, outs[0], outs[1])


def intra_of(w, cum3, cum_t, gmat):
    length = w.shape[0]
    blocks = length // GROUP
    tile = lambda g: (0, g)
    whole2 = lambda g: (0, 0)
    return pl.pallas_call(
        functools.partial(intra_kernel, blocks),
        grid=(TILES,),
        in_specs=[
            pl.BlockSpec((length, TILE), tile),
            pl.BlockSpec((length, 3 * HEADS), whole2),
            pl.BlockSpec((HEADS, length), whole2),
            pl.BlockSpec((blocks, GROUP, GROUP), lambda g: (0, 0, 0)),
        ],
        out_specs=pl.BlockSpec((length, TILE), tile),
        out_shape=jax.ShapeDtypeStruct((length, INNER), f32),
        compiler_params=params(),
        cost_estimate=pl.CostEstimate(flops=2_200_000_000, bytes_accessed=7_000_000, transcendentals=4_200_000),
        name="intra",
    )(w, cum3, cum_t, gmat)


def middle_kernel(
    blocks, y_ref, x_ref, gate_ref, gno_ref, q_ref, cum3_ref, start_ref, bs_ref, skip_ref, gain_ref,
    no_ref, dgate_ref, do_ref, dgain_ref, dskip_ref, rowsum_ref, dstart_ref, gdev_ref,
    y_s, sq_s, gt_s, r_s, m_s,
):
    length = blocks * GROUP
    phase, at = pl.program_id(0), pl.program_id(1)
    spread = expander(at)
    cum = mm(cum3_ref[...], spread)
    lanes = pl.ds(pl.multiple_of(at * TILE, TILE), TILE)
    x = x_ref[...].astype(f32)
    gate = gate_ref[...]
    sig = sigmoid(gate)
    gn = gno_ref[...]
    gain = gain_ref[0:1, :]
    skip = skip_ref[0:1, :]
    ends = jnp.exp(mm(spread, lasts(cum3_ref, blocks), ((0,), (1,))))

    @pl.when(phase == 0)
    def _():
        start = start_ref[...]
        for b in range(blocks):
            rows = slice(b * GROUP, (b + 1) * GROUP)
            inter = mm(q_ref[rows, :], start.astype(bf16), NT) * jnp.exp(cum[rows])
            y_s[rows, lanes] = y_ref[rows, :] + inter
            start = ends[:, b : b + 1] * start + bs_ref[b]
        gated = (y_s[:, lanes] + skip * x) * (gate * sig)
        sq = gated * gated
        gt = gated * gn * gain
        sq = sq[:, :LANES] + sq[:, LANES:]
        gt = gt[:, :LANES] + gt[:, LANES:]

        @pl.when(at == 0)
        def _():
            sq_s[...] = sq
            gt_s[...] = gt

        @pl.when(at > 0)
        def _():
            sq_s[...] += sq
            gt_s[...] += gt

    @pl.when(phase == 1)
    def _():
        @pl.when(at == 0)
        def _():
            r = lax.rsqrt(jnp.sum(sq_s[...], axis=1, keepdims=True) / INNER + epsilon)
            m = r * r * r * (jnp.sum(gt_s[...], axis=1, keepdims=True) / INNER)
            r_s[...] = jnp.broadcast_to(r, r_s.shape)
            m_s[...] = jnp.broadcast_to(m, m_s.shape)

        r = r_s[:, 0:1]
        m = m_s[:, 0:1]
        y = y_s[:, lanes]
        ssm = y + skip * x
        silu = gate * sig
        gated = ssm * silu
        scaled = gated * r
        no_ref[...] = (scaled * gain).astype(bf16)
        dgain_ref[...] = jnp.sum(gn * scaled, axis=0, keepdims=True)
        dgated = r * gn * gain - gated * m
        dgate_ref[...] = (dgated * ssm * (sig * (1.0 + gate * (1.0 - sig)))).astype(bf16)
        dof = dgated * silu
        dob = dof.astype(bf16)
        do_ref[...] = dob
        sums = head_sums(dob.astype(f32) * y, selector(at))
        skips = jnp.broadcast_to(jnp.sum(dof * x, axis=0, keepdims=True), (8, TILE))
        skips = head_sums(skips, selector(at))[0:1]

        @pl.when(at == 0)
        def _():
            rowsum_ref[...] = sums
            dskip_ref[...] = skips

        @pl.when(at > 0)
        def _():
            rowsum_ref[...] += sums
            dskip_ref[...] += skips

        scaled_do = (dof * jnp.exp(cum)).astype(bf16)
        total = None
        for b in reversed(range(blocks)):
            rows = slice(b * GROUP, (b + 1) * GROUP)
            d = mm(scaled_do[rows], q_ref[rows, :], TN)
            dstart_ref[b] = d
            total = d if total is None else ends[:, b : b + 1] * total + d
        gdev_ref[...] = total.astype(bf16)


def middle(y, x, gate, gno, q, cum3, start, bs, skip, gain):
    length = x.shape[0]
    blocks = length // GROUP
    both = lambda p, g: (0, g)
    ph0 = lambda p, g: (0, g * (1 - p) + (TILES - 1) * p)
    ph1 = lambda p, g: (0, g * p)
    whole2 = lambda p, g: (0, 0)
    return pl.pallas_call(
        functools.partial(middle_kernel, blocks),
        grid=(2, TILES),
        in_specs=[
            pl.BlockSpec((length, TILE), ph0),
            pl.BlockSpec((length, TILE), both),
            pl.BlockSpec((length, TILE), both),
            pl.BlockSpec((length, TILE), both),
            pl.BlockSpec((length, STATE), whole2),
            pl.BlockSpec((length, 3 * HEADS), whole2),
            pl.BlockSpec((TILE, STATE), lambda p, g: (g * (1 - p) + (TILES - 1) * p, 0)),
            pl.BlockSpec((blocks, TILE, STATE), lambda p, g: (0, g * (1 - p) + (TILES - 1) * p, 0)),
            pl.BlockSpec((1, TILE), both),
            pl.BlockSpec((1, TILE), both),
        ],
        out_specs=[
            pl.BlockSpec((length, TILE), ph1),
            pl.BlockSpec((length, TILE), ph1),
            pl.BlockSpec((length, TILE), ph1),
            pl.BlockSpec((1, TILE), ph1),
            pl.BlockSpec((1, LANES), whole2),
            pl.BlockSpec((length, LANES), whole2),
            pl.BlockSpec((blocks, TILE, STATE), lambda p, g: (0, g * p, 0)),
            pl.BlockSpec((TILE, STATE), lambda p, g: (g * p, 0)),
        ],
        out_shape=[
            jax.ShapeDtypeStruct((length, INNER), bf16),
            jax.ShapeDtypeStruct((length, INNER), bf16),
            jax.ShapeDtypeStruct((length, INNER), bf16),
            jax.ShapeDtypeStruct((1, INNER), f32),
            jax.ShapeDtypeStruct((1, LANES), f32),
            jax.ShapeDtypeStruct((length, LANES), f32),
            jax.ShapeDtypeStruct((blocks, INNER, STATE), f32),
            jax.ShapeDtypeStruct((INNER, STATE), bf16),
        ],
        scratch_shapes=[
            pltpu.VMEM((length, INNER), f32),
            pltpu.VMEM((length, LANES), f32),
            pltpu.VMEM((length, LANES), f32),
            pltpu.VMEM((length, LANES), f32),
            pltpu.VMEM((length, LANES), f32),
        ],
        compiler_params=params(),
        cost_estimate=pl.CostEstimate(flops=1_200_000_000, bytes_accessed=32_000_000, transcendentals=6_000_000),
        name="middle",
    )(y, x, gate, gno, q, cum3, start, bs, skip, gain)


def intra_back_kernel(
    blocks, w_ref, do_ref, cum3_ref, cum_t_ref, gmat_t_ref, k_ref, q_ref, dw_ref, dq_ref, dk_ref, dg_s
):
    at = pl.program_id(0)
    cum = mm(cum3_ref[...], expander(at))
    r = lax.broadcasted_iota(jnp.int32, (GROUP, GROUP), 0)
    c = lax.broadcasted_iota(jnp.int32, (GROUP, GROUP), 1)
    causal = c >= r
    first = lax.broadcasted_iota(jnp.int32, (GROUP, LANES), 1) < HEAD_DIM
    for b in range(blocks):
        rows = slice(b * GROUP, (b + 1) * GROUP)
        gmat = gmat_t_ref[b]
        dg = None
        for pair in range(HPT // 2):
            lanes = slice(pair * LANES, (pair + 1) * LANES)
            w = w_ref[rows, lanes]
            do = do_ref[rows, lanes]
            outs = []
            for side in range(2):
                j = 2 * pair + side
                col = cum[rows, j * HEAD_DIM : j * HEAD_DIM + 1]
                row = cum_t_ref[pl.ds(HPT * at + j, 1), rows]
                decay = jnp.exp(jnp.where(causal, row - col, -1e30))
                outs.append(mm((decay * gmat).astype(bf16), do))
                own = jnp.where(first if side == 0 else ~first, w, jnp.zeros_like(w))
                term = mm(own, do, NT) * decay
                dg = term if dg is None else dg + term
            dw_ref[rows, lanes] = jnp.where(first, outs[0], outs[1])

        @pl.when(at == 0)
        def _():
            dg_s[b] = dg

        @pl.when(at > 0)
        def _():
            dg_s[b] += dg

    @pl.when(at == TILES - 1)
    def _():
        for b in range(blocks):
            rows = slice(b * GROUP, (b + 1) * GROUP)
            dg = dg_s[b].astype(bf16)
            dk_ref[rows, :] = mm(dg, q_ref[rows, :])
            dq_ref[rows, :] = mm(dg, k_ref[rows, :], TN)


def intra_back(w, do, cum3, cum_t, gmat_t, k, q):
    length = w.shape[0]
    blocks = length // GROUP
    tile = lambda g: (0, g)
    whole2 = lambda g: (0, 0)
    return pl.pallas_call(
        functools.partial(intra_back_kernel, blocks),
        grid=(TILES,),
        in_specs=[
            pl.BlockSpec((length, TILE), tile),
            pl.BlockSpec((length, TILE), tile),
            pl.BlockSpec((length, 3 * HEADS), whole2),
            pl.BlockSpec((HEADS, length), whole2),
            pl.BlockSpec((blocks, GROUP, GROUP), lambda g: (0, 0, 0)),
            pl.BlockSpec((length, STATE), whole2),
            pl.BlockSpec((length, STATE), whole2),
        ],
        out_specs=[
            pl.BlockSpec((length, TILE), tile),
            pl.BlockSpec((length, STATE), whole2),
            pl.BlockSpec((length, STATE), whole2),
        ],
        out_shape=[
            jax.ShapeDtypeStruct((length, INNER), f32),
            jax.ShapeDtypeStruct((length, STATE), f32),
            jax.ShapeDtypeStruct((length, STATE), f32),
        ],
        scratch_shapes=[pltpu.VMEM((blocks, GROUP, GROUP), f32)],
        compiler_params=params(),
        cost_estimate=pl.CostEstimate(flops=4_400_000_000, bytes_accessed=10_000_000, transcendentals=4_200_000),
        name="intra_back",
    )(w, do, cum3, cum_t, gmat_t, k, q)


def back_kernel(
    blocks, p_ref, taps_ref, shift_ref, x_ref, w_ref, do_ref, dwi_ref, skip_ref,
    start_ref, bs_ref, adj_ref, dstart_ref,
    k_ref, q_ref, step3_ref, cum3_ref, dqi_ref, dki_ref, rowsum_ref, raw_ref, sb_ref, rate_ref,
    gp_ref, last_ref, before_ref, dtaps_ref, dshift_ref, draw_ref, dsb_ref, drate_ref,
    dq_s, dk_s, sx_s, sw_s, sv_s, dec_s, d_s,
):
    length = blocks * GROUP
    at = pl.program_id(0)

    @pl.when(at == 0)
    def _():
        dq_s[...] = dqi_ref[...]
        dk_s[...] = dki_ref[...]
        sx_s[...] = jnp.zeros_like(sx_s)
        sw_s[...] = jnp.zeros_like(sw_s)
        sv_s[...] = jnp.zeros_like(sv_s)
        dec_s[...] = jnp.zeros_like(dec_s)
        d_s[0:EDGE, :] = jnp.zeros((EDGE, TILE), f32)
        d_s[length + EDGE :, :] = jnp.zeros((EDGE, TILE), f32)

    def conv_back(dact):
        sources = shifted(p_ref, length)
        conv = conv_of(sources, taps_ref[...], shift_ref[...])
        sig = sigmoid(conv)
        dconv = dact * (sig * (1.0 + conv * (1.0 - sig)))
        d_s[EDGE : EDGE + length, :] = dconv
        dshift_ref[...] = jnp.sum(dconv, axis=0, keepdims=True)
        dp = None
        before = None
        for k in range(CONV):
            tap = taps_ref[k : k + 1, :]
            dtaps_ref[k : k + 1, :] = jnp.sum(dconv * sources[k], axis=0, keepdims=True)
            term = tap * d_s[pl.ds(EDGE + CONV - 1 - k, length), :]
            dp = term if dp is None else dp + term
            edge = tap * d_s[pl.ds(CONV - 1 - k, EDGE), :]
            before = edge if before is None else before + edge
        gp_ref[...] = dp.astype(bf16)
        last_ref[...] = dp[length - EDGE :, :]
        before_ref[...] = before

    @pl.when(at < TILES)
    def _():
        spread = expander(at)
        sel = selector(at)
        cum = mm(cum3_ref[...], spread)
        step = mm(step3_ref[...], spread)
        ends = jnp.exp(mm(spread, lasts(cum3_ref, blocks), ((0,), (1,))))
        x = x_ref[...].astype(f32)
        w = w_ref[...].astype(f32)
        do = do_ref[...].astype(f32)
        scaled_do = (do * jnp.exp(cum)).astype(bf16)
        starts = [start_ref[...]]
        for b in range(blocks - 1):
            starts.append(ends[:, b : b + 1] * starts[b] + bs_ref[b])
        adjs = [None] * blocks
        adj = adj_ref[...]
        for b in reversed(range(blocks)):
            adjs[b] = adj
            adj = ends[:, b : b + 1] * adj + dstart_ref[b]
        dws = []
        for b in range(blocks):
            rows = slice(b * GROUP, (b + 1) * GROUP)
            tails = jnp.exp(cum[(b + 1) * GROUP - 1 : (b + 1) * GROUP, :] - cum[rows])
            ab = adjs[b].astype(bf16)
            dws.append(tails * mm(k_ref[rows, :], ab, NT))
            dk_s[rows, :] += mm((w[rows] * tails).astype(bf16), ab)
            dq_s[rows, :] += mm(scaled_do[rows], starts[b].astype(bf16))
            both = jnp.sum(dws[b] * w[rows], axis=0, keepdims=True)
            sv_s[b : b + 1, :] += head_sums(jnp.broadcast_to(both, (8, TILE)), sel)[0:1]
            hi, lo = split2(ends[:, b : b + 1] * adjs[b] * starts[b])
            dec_s[b : b + 1, :] += jnp.sum(mm(hi, sel, TN) + mm(lo, sel, TN), axis=0, keepdims=True)
        dws = jnp.concatenate(dws, axis=0)
        dw = dwi_ref[...] + dws
        sx_s[...] += head_sums(dw * x, sel)
        sw_s[...] += head_sums(dw * w, sel)
        conv_back(dw * step + do * skip_ref[0:1, :])

    @pl.when(at == TILES)
    def _():
        conv_back(jnp.concatenate([dk_s[...], dq_s[...]], axis=1))
        dcum = (rowsum_ref[...] - sw_s[...])[:, :HEADS]
        z = raw_ref[EDGE:, :HEADS] + sb_ref[0:1, :]
        step = jnp.maximum(z, 0.0) + jnp.log1p(jnp.exp(-jnp.abs(z)))
        rate = rate_ref[0:1, :]
        up = tri(False)
        decays = []
        for b in range(blocks):
            rows = slice(b * GROUP, (b + 1) * GROUP)
            parts = split3(dcum[rows])
            extra = sv_s[b : b + 1, :HEADS] + dec_s[b : b + 1, :HEADS]
            decays.append(mm(up, parts[0]) + mm(up, parts[1]) + mm(up, parts[2]) + extra)
        ddecay = jnp.concatenate(decays, axis=0)
        dstep = sx_s[...][:, :HEADS] - ddecay * rate
        dz = dstep * sigmoid(z)
        draw_ref[...] = jnp.zeros_like(draw_ref)
        draw_ref[:, :HEADS] = dz.astype(bf16)
        dsb_ref[...] = jnp.sum(dz, axis=0, keepdims=True)
        drate_ref[...] = jnp.sum(-ddecay * step * rate, axis=0, keepdims=True)


def back(p, taps, shift, x, w, do, dwi, skip, start, bs, adj, dstart, k, q, step3, cum3, dqi, dki, rowsum, raw, sb, rate):
    length = x.shape[0]
    blocks = length // GROUP
    tile = lambda g: (0, g)
    xt = lambda g: (0, jnp.minimum(g, TILES - 1))
    st = lambda g: (jnp.minimum(g, TILES - 1), 0)
    st3 = lambda g: (0, jnp.minimum(g, TILES - 1), 0)
    whole2 = lambda g: (0, 0)
    spec = pl.BlockSpec
    return pl.pallas_call(
        functools.partial(back_kernel, blocks),
        grid=(TILES + 1,),
        in_specs=[
            spec((length + EDGE, TILE), tile),
            spec((CONV, TILE), tile),
            spec((1, TILE), tile),
            spec((length, TILE), xt),
            spec((length, TILE), xt),
            spec((length, TILE), xt),
            spec((length, TILE), xt),
            spec((1, TILE), xt),
            spec((TILE, STATE), st),
            spec((blocks, TILE, STATE), st3),
            spec((TILE, STATE), st),
            spec((blocks, TILE, STATE), st3),
            spec((length, STATE), whole2),
            spec((length, STATE), whole2),
            spec((length, 3 * HEADS), whole2),
            spec((length, 3 * HEADS), whole2),
            spec((length, STATE), whole2),
            spec((length, STATE), whole2),
            spec((length, LANES), whole2),
            spec((length + EDGE, LANES), lambda g: (0, 0)),
            spec((1, HEADS), whole2),
            spec((1, HEADS), whole2),
        ],
        out_specs=[
            spec((length, TILE), tile),
            spec((EDGE, TILE), tile),
            spec((EDGE, TILE), tile),
            spec((CONV, TILE), tile),
            spec((1, TILE), tile),
            spec((length, LANES), whole2),
            spec((1, HEADS), whole2),
            spec((1, HEADS), whole2),
        ],
        out_shape=[
            jax.ShapeDtypeStruct((length, CONV_CH), bf16),
            jax.ShapeDtypeStruct((EDGE, CONV_CH), f32),
            jax.ShapeDtypeStruct((EDGE, CONV_CH), f32),
            jax.ShapeDtypeStruct((CONV, CONV_CH), f32),
            jax.ShapeDtypeStruct((1, CONV_CH), f32),
            jax.ShapeDtypeStruct((length, LANES), bf16),
            jax.ShapeDtypeStruct((1, HEADS), f32),
            jax.ShapeDtypeStruct((1, HEADS), f32),
        ],
        scratch_shapes=[
            pltpu.VMEM((length, STATE), f32),
            pltpu.VMEM((length, STATE), f32),
            pltpu.VMEM((length, LANES), f32),
            pltpu.VMEM((length, LANES), f32),
            pltpu.VMEM((8, LANES), f32),
            pltpu.VMEM((8, LANES), f32),
            pltpu.VMEM((length + 2 * EDGE, TILE), f32),
        ],
        compiler_params=params(),
        cost_estimate=pl.CostEstimate(flops=2_500_000_000, bytes_accessed=32_000_000, transcendentals=6_000_000),
        name="back",
    )(p, taps, shift, x, w, do, dwi, skip, start, bs, adj, dstart, k, q, step3, cum3, dqi, dki, rowsum, raw, sb, rate)


def ring_ok():
    return lax.axis_size("dp") == 8 and lax.axis_size("seq") == 4


def spots():
    dp, seq = lax.axis_index("dp"), lax.axis_index("seq")
    return dp // 2, dp % 2, seq // 2, seq % 2


def over_y(a):
    return lax.ppermute(a, "dp", [(i, i ^ 1) for i in range(8)])


def over_z(a, k):
    return lax.ppermute(a, "dp", [(i, (i + 2 * k) % 8) for i in range(8)])


def over_x(a):
    return lax.ppermute(a, "seq", [(i, i ^ 2) for i in range(4)])


def over_core(a):
    return lax.ppermute(a, "seq", [(i, i ^ 1) for i in range(4)])


def assemble_kernel(rows, parts, *refs):
    assemble(rows, parts, refs[:13], refs[13:-1], refs[-1])


def assemble(rows, parts, pieces, outs, sem):
    own, a3, ay, b3, by, xb3, xby, ca3, cay, cb3, cby, cxb3, cxby = pieces
    z, y, x, c = spots()
    copies = []

    def put(src, dp, row, size):
        for out, (col, width, factor, base) in zip(outs_of, parts):
            copies.append(
                pltpu.make_async_copy(
                    src.at[:, pl.ds(col, width)],
                    out.at[pl.ds(pl.multiple_of(dp * (rows * factor) + base + row, 16), size), :],
                    sem.at[len(copies)],
                )
            )

    outs_of = [outs[part[4]] for part in parts]
    parts = [part[:4] for part in parts]
    put(own, z * 2 + y, 0, rows)
    half, fourth, eighth = rows // 2, rows // 4, rows // 8
    for k in range(4):
        zz = lax.rem(z + 4 - k, 4)
        for side in range(2):
            if k == 0 and side == 0:
                continue
            yy = y if side == 0 else 1 - y
            dp = zz * 2 + yy
            for core in range(2):
                cc = c if core == 0 else 1 - c
                src = ((a3, ay), (ca3, cay))[core][side]
                put(src.at[k - 1 if side == 0 else k], dp, cc * half, fourth)
                for far in range(2):
                    xx = x if far == 0 else 1 - x
                    src = (((b3, by), (xb3, xby)), ((cb3, cby), (cxb3, cxby)))[core][far][side]
                    put(
                        src.at[k - 1 if side == 0 else k],
                        dp,
                        cc * half + fourth + xx * eighth,
                        eighth,
                    )
    for copy in copies:
        copy.start()
    for copy in copies:
        copy.wait()


def gather_plain(pieces, parts):
    full = lax.all_gather(jnp.concatenate(pieces, axis=1), "dp")
    outs = []
    for out in sorted({part[4] for part in parts}):
        chosen = [full[:, :, p[0] : p[0] + p[1]] for p in parts if p[4] == out]
        outs.append(jnp.concatenate(chosen, axis=1).reshape(-1, chosen[0].shape[2]))
    return outs


def cut(pieces, start, size):
    return jnp.concatenate([lax.dynamic_slice_in_dim(p, start, size, 0) for p in pieces], axis=1)


def along_z(pieces, fourth_part):
    rows = pieces[0].shape[0]
    z, y, x, c = spots()
    if fourth_part:
        own = cut(pieces, c * (rows // 2), rows // 4)
    else:
        own = cut(pieces, c * (rows // 2) + rows // 4 + x * (rows // 8), rows // 8)
    return own, [over_z(own, k) for k in (1, 2, 3)]


def gather_pieces(pieces, a3, ay, b3, by, xb3, xby):
    sent = [a3, ay, b3, by, xb3, xby]
    return [jnp.concatenate(pieces, axis=1), *sent, *[over_core(a) for a in sent]]


def gather_end(pieces, parts, *staged):
    rows = pieces[0].shape[0]
    arrays = gather_pieces(pieces, *staged)
    shard = arrays[0]
    widths = {part[4]: part[1:3] for part in parts}
    shapes = [
        jax.ShapeDtypeStruct((8 * rows * widths[out][1], widths[out][0]), shard.dtype)
        for out in sorted(widths)
    ]
    anywhere = pl.BlockSpec(memory_space=pl.ANY)
    return pl.pallas_call(
        functools.partial(assemble_kernel, rows, parts),
        in_specs=[anywhere] * 13,
        out_specs=[pl.BlockSpec(memory_space=pltpu.VMEM)] * len(shapes),
        out_shape=shapes,
        scratch_shapes=[pltpu.SemaphoreType.DMA((len(parts) * (1 + 7 * 6),))],
        compiler_params=params(),
        cost_estimate=pl.CostEstimate(flops=0, bytes_accessed=32 * shard.size, transcendentals=0),
        name="assemble",
    )(*arrays)


SIDE = LANES - HEADS


def side_plan():
    plan = []
    for k in range(CONV):
        plan += [("taps", k, SIDE * j, SIDE, 3 * k + j) for j in range(3)]
    plan += [("shift", 0, SIDE * j, SIDE, 12 + j) for j in range(3)]
    plan += [("pre", 0, 0, SIDE, 15), ("pre", 0, SIDE, 32, 16)]
    plan += [("norm", 0, 0, SIDE, 17), ("norm", 0, SIDE, SIDE, 18), ("norm", 0, 2 * SIDE, 64, 19)]
    plan += [(name, 0, 0, 4, 20 + j) for j, name in enumerate(("bias", "rate", "skip"))]
    return plan


SIDE_WIDTH = {"taps": 288, "shift": 288, "pre": 128, "norm": 256, "bias": 4, "rate": 4, "skip": 4}


def pack_kernel(shards_in, names, left, *refs):
    out = refs[-1]
    out[...] = jnp.zeros_like(out)
    values = {name: ref[...].astype(f32) for name, ref in zip(names, refs)}
    values = {name: v if v.ndim == 2 else v.reshape(1, -1) for name, v in values.items()}
    for i in range(shards_in):
        for name, k, col, width, row in side_plan():
            if name in values:
                start = i * SIDE_WIDTH[name] + col
                out[i * 128 + row : i * 128 + row + 1, left : left + width] = values[name][
                    k : k + 1, start : start + width
                ]


def pack(shards_in, left, named):
    names = tuple(named)
    return pl.pallas_call(
        functools.partial(pack_kernel, shards_in, names, left),
        out_shape=jax.ShapeDtypeStruct((shards_in * 128, left + SIDE), f32),
        name="pack",
    )(*named.values())


def unpack_kernel(shards_in, names, in_ref, *refs):
    unpack_side(shards_in, dict(zip(names, refs)), in_ref[...].astype(f32))


def unpack_side(shards_in, outs, block):
    for i in range(shards_in):
        for name, k, col, width, row in side_plan():
            start = i * SIDE_WIDTH[name] + col
            outs[name][k : k + 1, start : start + width] = block[
                i * 128 + row : i * 128 + row + 1, HEADS : HEADS + width
            ]
    if "lanes" in outs:
        outs["rate"][...] = jnp.exp(outs["rate"][...])
        three = jnp.concatenate(split3(jnp.broadcast_to(outs["skip"][...], (8, HEADS))), axis=1)
        for tile in range(TILES):
            outs["lanes"][:, tile * TILE : (tile + 1) * TILE] = mm(three, expander(tile))[0:1]


SIDE_NAMES = ("taps", "shift", "pre", "norm", "bias", "rate", "skip", "lanes")


def enter_kernel(blocks, *refs):
    w_ref, side_ref, edge_ref, tok_ref, normed_ref, p_ref, raw_ref = refs[:7]
    side = dict(zip(SIDE_NAMES, refs[7:15]))
    fronts = refs[15:26]
    ext_s = refs[26]
    at = pl.program_id(0)

    @pl.when(at == 0)
    def _():
        unpack_side(8, side, side_ref[...].astype(f32))
        for ref, rows_at in ((edge_ref, slice(0, EDGE)), (tok_ref, slice(EDGE, None))):
            tok = ref[...].astype(f32)
            scale = lax.rsqrt(jnp.mean(tok * tok, axis=1, keepdims=True) + epsilon)
            ext_s[rows_at, :] = (tok * scale * side["pre"][...]).astype(bf16)
        normed_ref[...] = ext_s[EDGE:, :]
        raw_ref[...] = mm(ext_s[...], side_ref[...])

    lanes = pl.ds(pl.multiple_of(lax.rem(at + TILES, TILES + 1) * TILE, TILE), TILE)
    p_ref[...] = mm(ext_s[...], w_ref[...])
    front_body(
        blocks, p_ref, raw_ref, side["taps"][:, lanes], side["shift"][:, lanes], side["bias"], side["rate"],
        *fronts,
    )


def enter(weights, edge, toks):
    length, width = toks.shape
    whole2 = lambda g: (0, 0)
    tile = lambda g: (0, lax.rem(g + TILES, TILES + 1))
    shapes = [
        jax.ShapeDtypeStruct((length, width), bf16),
        jax.ShapeDtypeStruct((length + EDGE, CONV_CH), f32),
        jax.ShapeDtypeStruct((length + EDGE, LANES), f32),
    ]
    for name in SIDE_NAMES:
        lanes = INNER if name == "lanes" else 8 * SIDE_WIDTH[name]
        shapes.append(jax.ShapeDtypeStruct((CONV if name == "taps" else 1, lanes), f32))
    specs = [pl.BlockSpec(shape.shape, whole2) for shape in shapes]
    specs[1] = pl.BlockSpec((length + EDGE, TILE), tile)
    more_specs, more_shapes = front_outs(length)
    return pl.pallas_call(
        functools.partial(enter_kernel, length // GROUP),
        grid=(TILES + 1,),
        in_specs=[
            pl.BlockSpec((width, TILE), tile),
            pl.BlockSpec((width, LANES), lambda g: (0, CONV_CH // LANES)),
            pl.BlockSpec(edge.shape, whole2),
            pl.BlockSpec(toks.shape, whole2),
        ],
        out_specs=specs + more_specs,
        out_shape=shapes + more_shapes,
        scratch_shapes=[pltpu.VMEM((length + EDGE, width), bf16)],
        compiler_params=params(36 * 1024 * 1024),
        cost_estimate=pl.CostEstimate(
            flops=3_200_000_000, bytes_accessed=36_000_000, transcendentals=4_000_000
        ),
        name="enter",
    )(weights, weights, edge, toks)


def unpack(shards_in, side, names):
    shapes = []
    for name in names:
        width = INNER if name == "lanes" else shards_in * SIDE_WIDTH[name]
        shapes.append(jax.ShapeDtypeStruct((CONV if name == "taps" else 1, width), f32))
    whole = [pl.BlockSpec(shape.shape, lambda g: (0, 0)) for shape in shapes]
    return pl.pallas_call(
        functools.partial(unpack_kernel, shards_in, names),
        grid=(1,),
        in_specs=[pl.BlockSpec((shards_in * 128, LANES), lambda g: (0, 0))],
        out_specs=whole,
        out_shape=shapes,
        name="unpack",
    )(side)


def weight_grad_kernel(rows, plan, spot_ref, *refs):
    ka_ref, kb_ref, sa_ref, sb_ref, res = refs[-5:]
    y, x, c = spot_ref[1], spot_ref[2], spot_ref[3]
    at = 0
    for lhs, rhs, add, col, folds in plan:
        width = refs[rhs].shape[1]
        product = mm(refs[lhs][...], refs[rhs][...], TN)
        if add is not None:
            product = product + refs[add][...]
        for side in range(2):
            for fold in range(folds):
                top = (side * folds + fold) * rows
                left = col + fold * width
                res[side * rows : (side + 1) * rows, left : left + width] = product[top : top + rows]
    half, fourth, eighth = rows // 2, rows // 4, rows // 8
    for core, (a_ref, b_ref) in enumerate(((ka_ref, kb_ref), (sa_ref, sb_ref))):
        cc = c if core == 0 else 1 - c
        for side in range(2):
            yy = y if side == 0 else 1 - y
            at = yy * rows + cc * half
            a_ref[side, 0] = res[pl.ds(pl.multiple_of(at, fourth), fourth), :].astype(bf16)
            for far in range(2):
                xx = x if far == 0 else 1 - x
                b_ref[far, side, 0] = res[
                    pl.ds(pl.multiple_of(at + fourth + xx * eighth, eighth), eighth), :
                ].astype(bf16)


def weight_grads(rows, cols, arrays, plan):
    z, y, x, c = spots()
    spot = jnp.stack([z, y, x, c]).astype(jnp.int32)
    fourth, eighth = rows // 4, rows // 8
    a_spec = pl.BlockSpec((2, 1, fourth, cols), lambda k, s: (0, k, 0, 0))
    b_spec = pl.BlockSpec((2, 2, 1, eighth, cols), lambda k, s: (0, 0, k, 0, 0))
    a_shape = jax.ShapeDtypeStruct((2, 4, fourth, cols), bf16)
    b_shape = jax.ShapeDtypeStruct((2, 2, 4, eighth, cols), bf16)
    specs = []
    for array, kind in arrays:
        if kind == "lhs":
            specs.append(
                pl.BlockSpec((array.shape[0], array.shape[1] // 4), lambda k, s: (0, lax.rem(s[0] + k, 4)))
            )
        elif kind == "rhs":
            specs.append(pl.BlockSpec(array.shape, lambda k, s: (0, 0)))
        else:
            specs.append(
                pl.BlockSpec((array.shape[0] // 4, array.shape[1]), lambda k, s: (lax.rem(s[0] + k, 4), 0))
            )
    length = arrays[0][0].shape[0]
    return pl.pallas_call(
        functools.partial(weight_grad_kernel, rows, plan),
        grid_spec=pltpu.PrefetchScalarGridSpec(
            num_scalar_prefetch=1,
            grid=(4,),
            in_specs=specs,
            out_specs=[a_spec, b_spec, a_spec, b_spec],
            scratch_shapes=[pltpu.VMEM((2 * rows, cols), f32)],
        ),
        out_shape=[a_shape, b_shape, a_shape, b_shape],
        compiler_params=params((20 if cols > 3000 else 16) * 1024 * 1024),
        cost_estimate=pl.CostEstimate(
            flops=2 * length * 8 * rows * cols, bytes_accessed=20 * rows * cols, transcendentals=0
        ),
        name="weight_grads",
    )(spot, *[array for array, kind in arrays])


def plus(*terms):
    return sum(term.astype(f32) for term in terms).astype(bf16)


def sum_begin(ka, kb, sa, sb):
    ra, rb = over_core(sa), over_core(sb)
    return (plus(ka[1], ra[1]), plus(kb[1], rb[1])), (ka, kb, ra, rb)


def sum_next(got, held):
    ka, kb, ra, rb = held
    got_a, got_b = got
    u = [plus(ka[0, k], ra[0, k], got_a[k]) for k in range(4)]
    b_send = plus(kb[0, 1], rb[0, 1], got_b[1])
    return (u, b_send), (kb, rb, got_b)


def sum_third(sends):
    u, b_send = sends
    return over_y(b_send), u[0], [over_z(u[k], k) for k in (1, 2, 3)]


def sum_fourth(got, held):
    b_far, own, got_u = got
    kb, rb, got_b = held
    v = [plus(kb[0, 0, k], rb[0, 0, k], got_b[0, k], b_far[k]) for k in range(4)]
    fin_a = plus(own, *got_u)
    return fin_a, over_x(fin_a), v[0], [over_z(v[k], k) for k in (1, 2, 3)]


def sum_end(got):
    fin_a, other_a, v, got_v = got
    x, c = spots()[2:]
    eighth, cols = v.shape
    fin_b = plus(v, *got_v)
    other_b = over_x(fin_b)
    b_rows = jnp.where(x == 0, jnp.stack([fin_b, other_b]), jnp.stack([other_b, fin_b]))
    mine = jnp.concatenate([plus(fin_a, other_a), b_rows.reshape(2 * eighth, cols)], axis=0)
    other = over_core(mine)
    both = jnp.where(c == 0, jnp.stack([mine, other]), jnp.stack([other, mine]))
    return both.reshape(8 * eighth, cols)


def turn_kernel(gate_ref, conv_ref, out_ref):
    wide = gate_ref.shape[1]
    for col in range(0, wide, LANES):
        out_ref[col : col + LANES, :] = gate_ref[:, col : col + LANES].astype(f32).T
    for col in range(0, CONV_CH, LANES):
        out_ref[wide + col : wide + col + LANES, :] = conv_ref[:, col : col + LANES].astype(f32).T
    out_ref[wide + CONV_CH :, :] = conv_ref[:, CONV_CH:].astype(f32).T[:HEADS]


def turned(gate, conv):
    return pl.pallas_call(
        turn_kernel,
        out_shape=jax.ShapeDtypeStruct((gate.shape[1] + CONV_CH + HEADS, gate.shape[0]), f32),
        compiler_params=params(16 * 1024 * 1024),
        name="turned",
    )(gate, conv).T


def plain_sum(lhs, rhs):
    full = lax.dot_general(lhs, rhs, (TN, ((), ())), preferred_element_type=f32)
    part = lax.psum_scatter(full.astype(bf16), "dp", scatter_dimension=0, tiled=True)
    return lax.psum(part, "seq").astype(f32)


def carried(state, decay, mate_decay, axis, reverse):
    size, here = lax.axis_size(axis), lax.axis_index(axis)
    if mate_decay is not None:
        core = here % 2
        own, other = state.astype(f32), over_core(state).astype(f32)
        ahead = (core == 0) if reverse else (core == 1)
        mate_decay = mate_decay.astype(f32)
        pair = jnp.where(ahead, decay.astype(f32) * other + own, mate_decay * own + other).astype(bf16)
        route = [(2, 0), (3, 1)] if reverse else [(0, 2), (1, 3)]
        far = lax.ppermute(pair, axis, route).astype(f32)
        return jnp.where(ahead, other + mate_decay * far, far)
    states = lax.all_gather(state, axis)
    decays = lax.all_gather(decay[:, :1], axis).astype(f32)

    def one(lap, total):
        at = size - 1 - lap if reverse else lap
        use = at > here if reverse else at < here
        new = decays[at] * total + states[at].astype(f32)
        return jnp.where(use, new, total)

    return lax.fori_loop(0, size, one, jnp.zeros(state.shape, f32))


def rms_scale(values, gains):
    return values * lax.rsqrt(jnp.mean(values * values, axis=-1, keepdims=True) + epsilon) * gains


def shards(
    tokens, cotangent, in_weight, out_weight, conv_weight, conv_bias,
    pre_gain, norm_gain, step_bias, decay_log, skip_gain,
):
    dp = lax.axis_size("dp")
    seq = lax.axis_size("seq")
    toks = tokens[0]
    length = toks.shape[0]
    edge = lax.ppermute(toks[length - EDGE :], "seq", [(i, i + 1) for i in range(seq - 1)])
    ring = ring_ok()
    high = in_weight.shape[0]
    out_rows = out_weight.shape[0] // 2
    wide = out_weight.shape[1]
    first_parts = [(0, CONV_CH + LANES, 1, 0, 0)]
    then = [in_weight[:, :INNER], out_weight[:out_rows], out_weight[out_rows:]]
    then_parts = [(0, INNER, 1, 0, 0), (INNER, wide, 2, 0, 1), (INNER + wide, wide, 2, out_rows, 1)]
    if ring:
        named = {
            "taps": conv_weight, "shift": conv_bias, "pre": pre_gain, "norm": norm_gain,
            "bias": step_bias, "rate": decay_log, "skip": skip_gain,
        }
        first = [in_weight[:, INNER:], pack(1, 0, named).astype(bf16)]
        b0, bz = along_z(first, False)
        held = lax.optimization_barrier((*first, *bz))
        a0, az = along_z(held[:2], True)
        bz = list(held[2:])
        b3 = jnp.stack(bz)
        xb3 = over_x(b3)
        by = over_y(jnp.stack([b0] + bz))
        late_b = lax.optimization_barrier((*then, *az))
        az = list(late_b[3:])
        b0_2, bz_2 = along_z(late_b[:3], False)
        a3 = jnp.stack(az)
        ay = over_y(jnp.stack([a0] + az))
        late_a = lax.optimization_barrier((*then, by))
        by = late_a[3]
        a0_2, az_2 = along_z(late_a[:3], True)
        xby = over_x(by)
        ay, xb3, xby, bz_2, az_2[0] = lax.optimization_barrier((ay, xb3, xby, bz_2, az_2[0]))
        (conv_full,) = gather_end(first, first_parts, a3, ay, b3, by, xb3, xby)
        b3_2 = jnp.stack(bz_2)
        xb3_2 = over_x(b3_2)
        by_2 = over_y(jnp.stack([b0_2] + bz_2))
        conv_full, az_2, by_2 = lax.optimization_barrier((conv_full, az_2, by_2))
        xby_2 = over_x(by_2)
        a3_2 = jnp.stack(az_2)
        a4_2 = jnp.stack([a0_2] + az_2)
        ay_2 = over_y(a4_2)
    else:
        pieces = [conv_weight, conv_bias, pre_gain, norm_gain, step_bias, decay_log, skip_gain]
        shapes = [piece.shape for piece in pieces]
        sizes = [piece.size for piece in pieces]
        used = sum(sizes)
        lanes = -(-used // high)
        flat = jnp.concatenate(
            [piece.reshape(-1) for piece in pieces] + [jnp.zeros((high * lanes - used,), bf16)]
        )
        first = [
            in_weight[:, INNER:],
            flat.reshape(high, lanes),
            jnp.zeros((high, LANES - HEADS - lanes), bf16),
        ]
        (conv_full,) = gather_plain(first, first_parts)
        gate_full, out_full = gather_plain(then, then_parts)
        small = conv_full[:, CONV_CH + HEADS : CONV_CH + HEADS + lanes].reshape(dp, high * lanes)
        got, at = [], 0
        for shape, size in zip(shapes, sizes):
            got.append(small[:, at : at + size].reshape((dp,) + shape))
            at += size
        taps = jnp.moveaxis(got[0], 0, 1).reshape(CONV, CONV_CH).astype(f32)
        shift, gains_pre, gains_norm, bias_step, log_rates, skip = [
            piece.reshape(1, -1).astype(f32) for piece in got[1:]
        ]
        rate = jnp.exp(log_rates)
        skip_lanes = jnp.repeat(skip[0], HEAD_DIM)[None]

    if ring:
        entered = enter(conv_full, edge, toks)
        entered = list(entered)
        held = lax.optimization_barrier((entered[12], entered[14], ay_2, xb3_2, xby_2))
        entered[12], entered[14], ay_2, xb3_2, xby_2 = held
        normed, p, raw, taps, shift, gains_pre, gains_norm, bias_step, rate, _, skip_lanes = entered[:11]
        fronts = entered[11:]
    else:
        toks_ext = jnp.concatenate([edge, toks], axis=0)
        normed_ext = rms_scale(toks_ext.astype(f32), gains_pre).astype(bf16)
        normed = normed_ext[EDGE:]
        p = jnp.dot(normed_ext, conv_full[:, :CONV_CH], preferred_element_type=f32)
        raw = jnp.dot(normed_ext, conv_full[:, CONV_CH:], preferred_element_type=f32)
        fronts = front(p, raw, taps, shift, bias_step, rate)
    x, w, bs, dev, k, q, gmat, gmat_t, step3, cum3, cum_t = fronts
    mate_decay = over_core(dev[1]) if ring else None
    start = carried(dev[0], dev[1], mate_decay, "seq", False)
    y = intra_of(w, cum3, cum_t, gmat)
    if ring:
        gate_full, out_full = gather_end(then, then_parts, a3_2, ay_2, b3_2, by_2, xb3_2, xby_2)
    gate = jnp.dot(normed, gate_full, preferred_element_type=f32)
    cot = cotangent[0]
    gno = lax.dot_general(cot, out_full, (((1,), (1,)), ((), ())), preferred_element_type=f32)
    no, dgate, do, dgain, dskip, rowsum, dstart, gdev = middle(
        y, x, gate, gno, q, cum3, start, bs, skip_lanes, gains_norm
    )
    adj = carried(gdev, dev[1], mate_decay, "seq", True)
    rows = toks.astype(f32)
    mixed = (rows + jnp.dot(no, out_full, preferred_element_type=f32)).astype(bf16)
    if ring:
        early = weight_grads(
            high, INNER + 2 * wide,
            [(normed, "lhs"), (dgate, "rhs"), (no, "lhs"), (cot, "rhs")],
            [(0, 1, None, 0, 1), (2, 3, None, INNER, 2)],
        )
        sends, held = sum_begin(*early)
        (cum_t, sends) = lax.optimization_barrier((cum_t, sends))
        got = over_y(sends[0]), over_x(sends[1])
    over_cols = (((1,), (1,)), ((), ()))
    dnormed_gate = lax.dot_general(dgate, gate_full, over_cols, preferred_element_type=f32)
    inside = intra_back(w, do, cum3, cum_t, gmat_t, k, q)
    if ring:
        (dqi, got, mixed, dnormed_gate) = lax.optimization_barrier((inside[1], got, mixed, dnormed_gate))
        sends, held = sum_next(got, held)
        (dqi, sends) = lax.optimization_barrier((dqi, sends))
        got = sum_third(sends)
        inside = (inside[0], dqi, inside[2])
    dwi, dqi, dki = inside
    backs = back(
        p, taps, shift, x, w, do, dwi, skip_lanes, start, bs, adj, dstart,
        k, q, step3, cum3, dqi, dki, rowsum, raw, bias_step, rate,
    )
    if ring:
        backs = list(backs)
        (backs[1], backs[2], backs[3], got) = lax.optimization_barrier((backs[1], backs[2], backs[3], got))
        got = sum_fourth(got, held)
    gp, last, before, dtaps, dshift, draw, dsb, drate = backs
    returned = lax.ppermute(before, "seq", [(i + 1, i) for i in range(seq - 1)])
    gp = gp.at[length - EDGE :].set((last + returned).astype(bf16))
    if ring:
        named = {"taps": dtaps, "shift": dshift, "norm": dgain, "bias": dsb, "rate": drate, "skip": dskip}
        addend = pack(8, HEADS, named)
        late = weight_grads(
            high, CONV_CH + LANES,
            [(normed, "lhs"), (gp, "rhs"), (draw, "rhs"), (addend, "add")],
            [(0, 1, None, 0, 1), (0, 2, 3, CONV_CH, 1)],
        )
        late = list(late)
        late[2], late[3], got_v = lax.optimization_barrier((late[2], late[3], got[3]))
        got = (*got[:3], got_v)
        sends, late_held = sum_begin(*late)
        sends, gp, draw = lax.optimization_barrier((sends, gp, draw))
        late_got = over_y(sends[0]), over_x(sends[1])
    dnormed = (
        lax.dot_general(gp, conv_full[:, :CONV_CH], over_cols, preferred_element_type=f32)
        + dnormed_gate
        + lax.dot_general(draw, conv_full[:, CONV_CH:], over_cols, preferred_element_type=f32)
    )
    r = lax.rsqrt(jnp.mean(rows * rows, axis=-1, keepdims=True) + epsilon)
    t = dnormed * gains_pre
    drows = r * t - rows * (r * r * r * jnp.mean(rows * t, axis=-1, keepdims=True))
    grad_tokens = (cot.astype(f32) + drows).astype(bf16)
    if ring:
        (late_got, grad_tokens) = lax.optimization_barrier((late_got, grad_tokens))
        sends, late_held = sum_next(late_got, late_held)
        sends, got = lax.optimization_barrier((sends, got))
        late_got = sum_third(sends)
        early = sum_end(got)
        grad_gate = early[:, :INNER]
        grad_out = jnp.concatenate([early[:, INNER : INNER + wide], early[:, INNER + wide :]], axis=0).astype(f32)
        grad_conv = sum_end(sum_fourth(late_got, late_held))
        own_gate, own_conv = in_weight[:, :INNER], in_weight[:, INNER:]
        dpre = jnp.sum(own_gate.astype(f32) * grad_gate, axis=1) + jnp.sum(
            own_conv.astype(f32) * grad_conv[:, : CONV_CH + HEADS], axis=1
        )
        dpre = dpre / pre_gain.astype(f32)
        names = ("taps", "shift", "pre", "norm", "bias", "rate", "skip")
        outs = unpack(1, grad_conv[:, CONV_CH:], names)
        outs = [outs[0], outs[1][0], dpre, outs[3][0], outs[4][0], outs[5][0], outs[6][0]]
    else:
        dpre = jnp.sum(dnormed * rows * r, axis=0)
        smalls = [
            jnp.moveaxis(dtaps.reshape(CONV, dp, -1), 1, 0).reshape(dp, -1),
            dshift.reshape(dp, -1),
            dpre.reshape(dp, -1),
            dgain.reshape(dp, -1),
            dsb.reshape(dp, -1),
            drate.reshape(dp, -1),
            dskip[:, :HEADS].reshape(dp, -1),
        ]
        bundle = jnp.concatenate(smalls + [jnp.zeros((dp, high * lanes - used), f32)], axis=1)
        grad_gate = plain_sum(normed, dgate)
        grad_out = plain_sum(no, cot)
        mine = lax.psum(lax.psum_scatter(bundle, "dp", scatter_dimension=0), "seq")
        grad_conv = jnp.concatenate([plain_sum(normed, gp), plain_sum(normed, draw)], axis=1)
        outs, at = [], 0
        for shape, size in zip(shapes, sizes):
            outs.append(mine[at : at + size].reshape(shape))
            at += size
    if ring:
        grad_in = turned(grad_gate, grad_conv)
    else:
        grad_in = jnp.concatenate([grad_gate, grad_conv[:, : CONV_CH + HEADS]], axis=1)
    return (
        mixed[None], grad_tokens[None], grad_in, grad_out, outs[0], outs[1],
        outs[2], outs[3], outs[4], outs[5], outs[6],
    )


def solution(mesh):
    return jax.shard_map(
        shards,
        mesh=mesh,
        in_specs=(
            P("dp", "seq", None), P("dp", "seq", None), P("dp", None), P("dp", None),
            P(None, "dp"), P("dp"), P("dp"), P("dp"), P("dp"), P("dp"), P("dp"),
        ),
        out_specs=(
            P("dp", "seq", None), P("dp", "seq", None), P("dp", None), P("dp", None),
            P(None, "dp"), P("dp"), P("dp"), P("dp"), P("dp"), P("dp"), P("dp"),
        ),
        check_vma=False,
    )
```
